128 devices in a mesh: dp: 64 (over y, x, z_hi, core), tensor: 2 (over z_lo).
Axes of the slice: x: 4, y: 4, z: 4 (z_hi: 2, z_lo: 2; z = z_hi * 2 + z_lo), core: 2. Of those that a mesh axis runs over, the one named last changes fastest.
Arguments:
- tokens: bfloat16 [32768, 1024], P(('dp', 'tensor')), may hold values from -6 to 6
- segment: int32 [32768], P('dp'), may hold values from -1 to 255, as said below
- w_query: bfloat16 [1024, 1024], P('dp', 'tensor'), may hold values from -0.1875 to 0.1875
- w_key: bfloat16 [1024, 1024], P('dp', 'tensor'), may hold values from -0.1875 to 0.1875
- w_value: bfloat16 [1024, 1024], P('dp', 'tensor'), may hold values from -0.1875 to 0.1875
- w_out: bfloat16 [1024, 1024], P('dp', 'tensor'), may hold values from -0.75 to 0.75
- w_up: bfloat16 [1024, 4096], P('dp', 'tensor'), may hold values from -0.1875 to 0.1875
- w_down: bfloat16 [1024, 4096], P('dp', 'tensor'), may hold values from -0.09375 to 0.09375
- b_query: bfloat16 [1024], P(('tensor', 'dp')), may hold values from -3 to 3
- b_value: bfloat16 [1024], P(('tensor', 'dp')), may hold values from -3 to 3
- b_up: bfloat16 [4096], P(('tensor', 'dp')), may hold values from -3 to 3
- b_out: bfloat16 [1024], P('dp'), may hold values from -3 to 3
- b_down: bfloat16 [1024], P('dp'), may hold values from -3 to 3
- gain_one: bfloat16 [1024], P('dp'), may hold values from 0.5 to 1.5
- shift_one: bfloat16 [1024], P('dp'), may hold values from -3 to 3
- gain_two: bfloat16 [1024], P('dp'), may hold values from 0.5 to 1.5
- shift_two: bfloat16 [1024], P('dp'), may hold values from -3 to 3
- out_grad: float32 [32768, 1024], P(('dp', 'tensor')), may hold values from -6 to 6
Outputs:
- layer_out: bfloat16 [32768, 1024], P(('dp', 'tensor'))
- input_grad: float32 [32768, 1024], P(('dp', 'tensor'))
- grad_w_query: float32 [1024, 1024], P('dp', 'tensor')
- grad_w_key: float32 [1024, 1024], P('dp', 'tensor')
- grad_w_value: float32 [1024, 1024], P('dp', 'tensor')
- grad_w_out: float32 [1024, 1024], P('dp', 'tensor')
- grad_w_up: float32 [1024, 4096], P('dp', 'tensor')
- grad_w_down: float32 [1024, 4096], P('dp', 'tensor')
- grad_b_query: float32 [1024], P(('tensor', 'dp'))
- grad_b_value: float32 [1024], P(('tensor', 'dp'))
- grad_b_up: float32 [4096], P(('tensor', 'dp'))
- grad_b_out: float32 [1024], P('dp')
- grad_b_down: float32 [1024], P('dp')
- grad_gain_one: float32 [1024], P('dp')
- grad_shift_one: float32 [1024], P('dp')
- grad_gain_two: float32 [1024], P('dp')
- grad_shift_two: float32 [1024], P('dp')
The draws below stay inside these ranges and needn't reach their ends.
Inputs may be any that keep to these rules, and one draw needn't show every extreme that they name: `segment`: within each group of 512 slots the live slots come first and carry sequence numbers 0, 1, 2, ... in order, each sequence in consecutive slots; the slots after them hold -1. Sequence 0 of every group covers more than half of its slots. At least one group has no padding, and in it the last slot carries the largest sequence number.
All inputs are finite; a program needn't handle non-finite values.
Results may differ from the reference program's by a relative error of at most 0.015.
Values may be sent and summed in bfloat16 or wider, within the bound.
A program may use at most 128 MiB of HBM per device.

```python
import jax
import jax.numpy as jnp
from jax import lax

D = 1024
HEADS = 16
HEAD_DIM = 64
FF = 4096
GROUP = 512
TOKENS = 32768


def draw_segment(key, part):
    key = jax.random.fold_in(key, 7)
    first_key, live_key, full_key, bound_key = jax.random.split(key, 4)
    groups = TOKENS // GROUP
    half_group = GROUP // 2
    full_group = jax.random.randint(full_key, (), 0, groups)
    group_index = jnp.arange(groups)[:, None]
    is_full = group_index == full_group
    first_len = jax.random.randint(first_key, (groups, 1), half_group + 1, half_group + GROUP // 4 + 1)
    first_len = jnp.where(is_full, half_group + 1, first_len)
    live_count = jax.random.randint(live_key, (groups, 1), 0, GROUP + 1)
    live_count = jnp.maximum(live_count, first_len)
    live_count = jnp.where(is_full, GROUP, live_count)
    position = jnp.arange(GROUP)[None, :]
    boundary = (jax.random.randint(bound_key, (groups, GROUP), 0, GROUP) < 3).astype(jnp.int32)
    boundary = jnp.where(position > first_len, boundary, 0)
    boundary = jnp.where(is_full & (position > first_len), 1, boundary)
    boundary = jnp.where(position == first_len, 1, boundary)
    seq_ids = jnp.cumsum(boundary, axis=1)
    seq_ids = jnp.where(position < live_count, seq_ids, -1)
    return seq_ids.reshape(-1).astype(jnp.int32)


def levels(own_key, shape, shards, low, largest):
    loudness, own = 1.0, jax.random.fold_in(own_key, 6)
    for axis_at, parts in shards:
        heights = jnp.exp(jax.random.uniform(jax.random.fold_in(own, axis_at), (parts,), jnp.float32, low / len(shards), largest / len(shards)))
        loudness = loudness * jnp.repeat(heights, shape[axis_at] // parts).reshape([-1 if axis == axis_at else 1 for axis in range(len(shape))])
    return loudness


def normal_values(stream_key, shape, scale, most, cuts=(), dtype=jnp.bfloat16):
    loudness = levels(stream_key, shape, cuts, -0.22, 0.18) if cuts else 1.0
    values = jax.random.normal(stream_key, shape, jnp.float32) * scale * loudness
    return jnp.minimum(jnp.maximum(values, -most), most).astype(dtype)


def setup_inputs(seed: int = 0) -> dict:
    key_of = jax.random.split(jax.random.key(seed), 19)
    tokens = normal_values(key_of[0], (TOKENS, D), 1.0, 6.0, ((0, 128),))
    segment = draw_segment(jax.random.fold_in(key_of[18], 71), 0)
    w_query = normal_values(key_of[2], (D, D), D ** -0.5, 0.1875, ((0, 64), (1, 2)))
    w_key = normal_values(key_of[3], (D, D), D ** -0.5, 0.1875, ((0, 64), (1, 2)))
    w_value = normal_values(key_of[4], (D, D), D ** -0.5, 0.1875, ((0, 64), (1, 2)))
    w_out = normal_values(key_of[5], (D, D), HEAD_DIM ** -0.5, 0.75, ((0, 64), (1, 2)))
    w_up = normal_values(key_of[6], (D, FF), D ** -0.5, 0.1875, ((0, 64), (1, 2)))
    w_down = normal_values(key_of[7], (D, FF), FF ** -0.5, 0.09375, ((0, 64), (1, 2)))
    b_query = normal_values(key_of[8], (D,), 0.5, 3.0, ((0, 128),))
    b_value = normal_values(key_of[9], (D,), 0.5, 3.0, ((0, 128),))
    b_up = normal_values(key_of[10], (FF,), 0.5, 3.0, ((0, 128),))
    b_out = normal_values(key_of[11], (D,), 0.5, 3.0, ((0, 64),))
    b_down = normal_values(key_of[12], (D,), 0.5, 3.0, ((0, 64),))
    gain_one = jnp.clip(1.0 + 0.1 * jax.random.normal(key_of[13], (D,), jnp.float32), 0.5, 1.5).astype(jnp.bfloat16)
    shift_one = normal_values(key_of[14], (D,), 0.5, 3.0, ((0, 64),))
    gain_two = jnp.clip(1.0 + 0.1 * jax.random.normal(key_of[15], (D,), jnp.float32), 0.5, 1.5).astype(jnp.bfloat16)
    shift_two = normal_values(key_of[16], (D,), 0.5, 3.0, ((0, 64),))
    out_grad = normal_values(key_of[17], (TOKENS, D), 1.0, 6.0, ((0, 128),), jnp.float32)
    return dict(tokens=tokens, segment=segment, w_query=w_query, w_key=w_key, w_value=w_value, w_out=w_out, w_up=w_up, w_down=w_down, b_query=b_query, b_value=b_value, b_up=b_up, b_out=b_out, b_down=b_down, gain_one=gain_one, shift_one=shift_one, gain_two=gain_two, shift_two=shift_two, out_grad=out_grad)


@jax.custom_vjp
def low(v):
    return lax.optimization_barrier(v.astype(jnp.bfloat16)).astype(jnp.float32)

@jax.custom_vjp
def low_back(v):
    return v

def low_keep(v):
    return (low(v), None)

def low_pass(kept, grad):
    return (grad,)

def back_keep(v):
    return (v, None)

def back_low(kept, grad):
    return (low(grad),)
low.defvjp(low_keep, low_pass)
low_back.defvjp(back_keep, back_low)
epsilon = 1e-12
highest = lax.Precision.HIGHEST

def layer_norm(hidden, gain, shift):
    average = lax.optimization_barrier(jnp.mean(hidden, axis=-1, keepdims=True))
    centered = hidden - average
    variance = lax.optimization_barrier(jnp.mean(centered * centered, axis=-1, keepdims=True))
    return centered * lax.rsqrt(variance + epsilon) * gain + shift

def group_forward(params, rows_group, seg_group):
    w_query, w_key, w_value, w_out, w_up, w_down, b_query, b_value, b_up, b_out, b_down, gain_one, shift_one, gain_two, shift_two = params
    length = rows_group.shape[0]
    width = rows_group.shape[1]
    queries = low(low_back(jnp.dot(rows_group, w_query, precision=highest) + b_query))
    key_rows = low(low_back(jnp.dot(rows_group, w_key, precision=highest)))
    value_rows = low(low_back(jnp.dot(rows_group, w_value, precision=highest) + b_value))
    queries = queries.reshape(length, HEADS, HEAD_DIM)
    key_rows = key_rows.reshape(length, HEADS, HEAD_DIM)
    value_rows = value_rows.reshape(length, HEADS, HEAD_DIM)
    scores = jnp.einsum('qhd,khd->hqk', queries, key_rows, precision=highest) * HEAD_DIM ** (-0.5)
    scores = low_back(scores)
    allowed = seg_group[:, None] == seg_group[None, :]
    scores = jnp.where(allowed[None], scores, -1000000000.0)
    attn_probs = low(jax.nn.softmax(scores, axis=-1))
    context = jnp.einsum('hqk,khd->qhd', attn_probs, value_rows, precision=highest).reshape(length, width)
    context = low(low_back(context))
    attended = low_back(jnp.dot(context, w_out.T, precision=highest))
    normed_one = layer_norm(rows_group + attended + b_out, gain_one, shift_one)
    up_pre = low_back(jnp.dot(low(normed_one), w_up, precision=highest) + b_up)
    activated = low(jax.nn.gelu(up_pre, approximate=False))
    down_out = low_back(jnp.dot(activated, w_down.T, precision=highest))
    normed_two = layer_norm(normed_one + down_out + b_down, gain_two, shift_two)
    return normed_two * (seg_group >= 0).astype(jnp.float32)[:, None]

def reference(tokens, segment, w_query, w_key, w_value, w_out, w_up, w_down, b_query, b_value, b_up, b_out, b_down, gain_one, shift_one, gain_two, shift_two, out_grad):
    params = tuple((weight.astype(jnp.float32) for weight in (w_query, w_key, w_value, w_out, w_up, w_down, b_query, b_value, b_up, b_out, b_down, gain_one, shift_one, gain_two, shift_two)))
    rows = tokens.astype(jnp.float32)
    seg_blocks = segment.reshape(TOKENS // GROUP, GROUP)
    group_step = jax.checkpoint(group_forward)

    def forward(weights, rows_in):
        row_blocks = rows_in.reshape(TOKENS // GROUP, GROUP, D)

        def scan_body(carried, element):
            return (carried, group_step(weights, element[0], element[1]))
        unused, results = lax.scan(scan_body, jnp.zeros((), jnp.float32), (row_blocks, seg_blocks))
        return results.reshape(TOKENS, D)
    result, pullback = jax.vjp(forward, params, rows)
    param_grads, rows_grad = pullback(out_grad.astype(jnp.float32))
    return (result.astype(jnp.bfloat16), rows_grad, param_grads[0], param_grads[1], param_grads[2], param_grads[3], param_grads[4], param_grads[5], param_grads[6], param_grads[7], param_grads[8], param_grads[9], param_grads[10], param_grads[11], param_grads[12], param_grads[13], param_grads[14])
```

```python
import functools

import jax
import jax.numpy as jnp
from jax import lax
from jax.experimental import pallas as pl
from jax.experimental.pallas import tpu as pltpu
from jax.sharding import PartitionSpec as P

MESH = pl.DeviceIdType.MESH
F32 = jnp.float32
BF16 = jnp.bfloat16

SQUARES = ((1, "a"), (0, "a"), (2, "a"), (1, "b"), (0, "b"), (2, "b"))
TILES = 24
COLS = 256
ROUTES = 6
VEC_ROWS = 96


def position():
    dp, low = lax.axis_index("dp"), lax.axis_index("tensor")
    return (dp // 16, lax.rem(dp // 4, 4), lax.rem(dp // 2, 2) * 2 + low), lax.rem(dp, 2)


def device(chip, core):
    y, x, z = chip
    return (y * 16 + x * 4 + (z // 2) * 2 + core, lax.rem(z, 2))


def across(chip, square):
    axis, kind = square
    at = chip[axis]
    new = at + 1 - 2 * lax.rem(at, 2) if kind == "a" else 3 - at
    return tuple(new if k == axis else c for k, c in enumerate(chip))


def route_squares(route):
    return [SQUARES[(route + s) % 6] for s in range(6)]


def pieces(chip, done):
    per_axis = []
    for axis in range(3):
        at = chip[axis]
        kinds = {kind for a, kind in done if a == axis}
        if not kinds:
            per_axis.append([(at, 1)])
        elif kinds == {"a"}:
            per_axis.append([(at // 2 * 2, 2)])
        elif kinds == {"b"}:
            per_axis.append([(at, 1), (3 - at, 1)])
        else:
            per_axis.append([(0, 4)])
    return [
        ((ky, kx, kz), (y, x, z))
        for ky, y in enumerate(per_axis[0])
        for kx, x in enumerate(per_axis[1])
        for kz, z in enumerate(per_axis[2])
    ]


def span(done):
    sizes = []
    for axis in range(3):
        kinds = {kind for a, kind in done if a == axis}
        sizes.append(1 << len(kinds))
    return sizes


def view(ref, tiles, piece):
    return ref.at[(pl.ds(*tiles),) + tuple(pl.ds(*p) for p in piece)]


def piece_counts():
    return [[len(pieces((0, 0, 0), route_squares(r)[:s])) for s in range(6)] for r in range(ROUTES)]


COUNTS = piece_counts()
COPIES = sum(map(sum, COUNTS))


def first_sem(route, stage):
    return sum(sum(c) for c in COUNTS[:route]) + sum(COUNTS[route][:stage])


class Gather:
    def __init__(self, w, send, recv, tiles_of, base=0):
        self.w, self.send, self.recv, self.tiles_of, self.base = w, send, recv, tiles_of, base
        self.chip, self.core = position()

    def copies(self, route, stage):
        squares = route_squares(route)
        target = device(across(self.chip, squares[stage]), self.core)
        out = []
        for n, (_, piece) in enumerate(pieces(self.chip, squares[:stage])):
            part = view(self.w, self.tiles_of(route), piece)
            sem = self.base + first_sem(route, stage) + n
            out.append(
                pltpu.make_async_remote_copy(
                    src_ref=part,
                    dst_ref=part,
                    send_sem=self.send.at[sem],
                    recv_sem=self.recv.at[sem],
                    device_id=target,
                    device_id_type=MESH,
                )
            )
        return out

    def start(self, route, stage):
        for c in self.copies(route, stage):
            c.start()

    def wait_recv(self, route, stage):
        for c in self.copies(route, stage):
            c.wait_recv()

    def wait_send(self, route, stage):
        for c in self.copies(route, stage):
            c.wait_send()


def landing_shapes(tiles_of):
    shapes = []
    for route in range(ROUTES):
        for stage in range(6):
            done = route_squares(route)[: 5 - stage]
            (_, piece) = pieces((0, 0, 0), done)[0]
            shapes.append(
                (COUNTS[route][5 - stage], tiles_of(route)[1]) + tuple(n for _, n in piece) + (16, COLS)
            )
    return shapes


class Scatter:
    def __init__(self, g, landings, send, recv, tiles_of, base=0):
        self.g, self.landings, self.send, self.recv = g, landings, send, recv
        self.tiles_of, self.base = tiles_of, base
        self.chip, self.core = position()

    def copies(self, route, stage):
        squares = route_squares(route)[: 6 - stage]
        over = across(self.chip, squares[-1])
        target = device(over, self.core)
        out = []
        for n, (_, piece) in enumerate(pieces(over, squares[:-1])):
            sem = self.base + first_sem(route, 5 - stage) + n
            out.append(
                pltpu.make_async_remote_copy(
                    src_ref=view(self.g, self.tiles_of(route), piece),
                    dst_ref=self.landings[route * 6 + stage].at[n],
                    send_sem=self.send.at[sem],
                    recv_sem=self.recv.at[sem],
                    device_id=target,
                    device_id_type=MESH,
                )
            )
        return out

    def start(self, route, stage):
        for c in self.copies(route, stage):
            c.start()

    def wait_send(self, route, stage):
        for c in self.copies(route, stage):
            c.wait_send()

    def take(self, route, stage):
        for c in self.copies(route, stage):
            c.wait_recv()
        tile0, tiles = self.tiles_of(route)
        done = route_squares(route)[: 5 - stage]
        landed = self.landings[route * 6 + stage]
        for n, (_, piece) in enumerate(pieces(self.chip, done)):
            (y0, ny), (x0, nx), (z0, nz) = piece

            def add(i, carry):
                tile, y = i // ny, lax.rem(i, ny)
                at = (tile0 + tile, y0 + y, pl.ds(x0, nx), pl.ds(z0, nz))
                total = self.g[at].astype(F32) + landed[n, tile, y].astype(F32)
                self.g[at] = total.astype(BF16)
                return carry

            lax.fori_loop(0, tiles * ny, add, 0)


def greet(others):
    barrier = pltpu.get_barrier_semaphore()
    for other in others:
        pl.semaphore_signal(barrier, inc=1, device_id=other, device_id_type=MESH)
    pl.semaphore_wait(barrier, len(others))


def neighbours():
    chip, core = position()
    return [device(across(chip, square), core) for square in SQUARES]


def sibling():
    chip, core = position()
    return device(chip, 1 - core)


class VectorSum:
    def __init__(self, kept, came, send, recv, base):
        self.kept, self.came, self.send, self.recv, self.base = kept, came, send, recv, base

    def copy(self, stage):
        target = (neighbours() + [sibling()])[stage]
        return pltpu.make_async_remote_copy(
            src_ref=self.kept.at[stage],
            dst_ref=self.came.at[stage],
            send_sem=self.send.at[self.base + stage],
            recv_sem=self.recv.at[self.base + stage],
            device_id=target,
            device_id_type=MESH,
        )

    def start(self, stage):
        self.copy(stage).start()

    def take(self, stage):
        self.copy(stage).wait_recv()
        self.kept[stage + 1] = self.kept[stage] + self.came[stage]

    def wait_send(self, stage):
        self.copy(stage).wait_send()


def four_tiles(route):
    return (route * 4, 4)


def gather_kernel(own, vec, w_out, vec_out, w, kept, came, send, recv, out_sem):
    greet(neighbours() + [sibling()])
    gather = Gather(w, send, recv, four_tiles)
    vectors = VectorSum(kept, came, send, recv, COPIES)
    (y, x, z), _ = position()
    w[:, y, x, z] = own[...]
    kept[0] = vec[...]
    for stage in range(6):
        for route in range(ROUTES):
            if stage:
                gather.wait_recv(route, stage - 1)
            gather.start(route, stage)
        if stage:
            vectors.take(stage - 1)
        vectors.start(stage)
    vectors.take(5)
    vectors.start(6)
    for route in range(ROUTES):
        gather.wait_recv(route, 5)
    out = pltpu.make_async_copy(w, w_out, out_sem)
    out.start()
    vectors.take(6)
    vec_out[...] = kept[7]
    for stage in range(6):
        for route in range(ROUTES):
            gather.wait_send(route, stage)
    for stage in range(7):
        vectors.wait_send(stage)
    out.wait()


def gather_call(own, vec):
    full = (TILES, 4, 4, 4, 16, COLS)
    return pl.pallas_call(
        gather_kernel,
        out_shape=(
            jax.ShapeDtypeStruct(full, BF16),
            jax.ShapeDtypeStruct((VEC_ROWS, 128), F32),
        ),
        in_specs=[pl.BlockSpec(memory_space=pltpu.VMEM)] * 2,
        out_specs=(pl.BlockSpec(memory_space=pl.ANY), pl.BlockSpec(memory_space=pltpu.VMEM)),
        scratch_shapes=[
            pltpu.VMEM(full, BF16),
            pltpu.VMEM((8, VEC_ROWS, 128), F32),
            pltpu.VMEM((7, VEC_ROWS, 128), F32),
            pltpu.SemaphoreType.DMA((COPIES + 7,)),
            pltpu.SemaphoreType.DMA((COPIES + 7,)),
            pltpu.SemaphoreType.DMA,
        ],
        compiler_params=pltpu.CompilerParams(
            collective_id=0, has_side_effects=True, vmem_limit_bytes=60 * 2**20
        ),
    )(own, vec)


def scatter_kernel(g_in, vec, own_out, vec_out, g, kept, came, send, recv, in_sem, *landings):
    greet(neighbours() + [sibling()])
    scatter = Scatter(g, landings, send, recv, four_tiles)
    vectors = VectorSum(kept, came, send, recv, COPIES)
    kept[0] = vec[...]
    get = pltpu.make_async_copy(g_in, g, in_sem)
    get.start()
    vectors.start(0)
    get.wait()
    for stage in range(6):
        for route in range(ROUTES):
            if stage:
                scatter.take(route, stage - 1)
            scatter.start(route, stage)
        vectors.take(stage)
        vectors.start(stage + 1)
    for route in range(ROUTES):
        scatter.take(route, 5)
    (y, x, z), _ = position()
    own_out[...] = g[:, y, x, z].astype(F32)
    vectors.take(6)
    vec_out[...] = kept[7]
    for stage in range(6):
        for route in range(ROUTES):
            scatter.wait_send(route, stage)
    for stage in range(7):
        vectors.wait_send(stage)


def scatter_call(g, vec):
    full = (TILES, 4, 4, 4, 16, COLS)
    return pl.pallas_call(
        scatter_kernel,
        out_shape=(
            jax.ShapeDtypeStruct((TILES, 16, COLS), F32),
            jax.ShapeDtypeStruct((VEC_ROWS, 128), F32),
        ),
        in_specs=[pl.BlockSpec(memory_space=pl.ANY), pl.BlockSpec(memory_space=pltpu.VMEM)],
        out_specs=(pl.BlockSpec(memory_space=pltpu.VMEM),) * 2,
        scratch_shapes=[
            pltpu.VMEM(full, BF16),
            pltpu.VMEM((8, VEC_ROWS, 128), F32),
            pltpu.VMEM((7, VEC_ROWS, 128), F32),
            pltpu.SemaphoreType.DMA((COPIES + 7,)),
            pltpu.SemaphoreType.DMA((COPIES + 7,)),
            pltpu.SemaphoreType.DMA,
        ]
        + [pltpu.VMEM(shape, BF16) for shape in landing_shapes(four_tiles)],
        compiler_params=pltpu.CompilerParams(
            collective_id=1, has_side_effects=True, vmem_limit_bytes=60 * 2**20
        ),
    )(g, vec)


def swapped(array):
    pairs = []
    for dp in range(64):
        for low in range(2):
            there = (dp, low) if dp % 2 == low else (dp + 1 - 2 * (dp % 2), 1 - low)
            pairs.append((dp * 2 + low, there[0] * 2 + there[1]))
    return lax.ppermute(array, ("dp", "tensor"), pairs)


def from_sibling(array):
    return lax.ppermute(array, "dp", [(d, d + 1 - 2 * (d % 2)) for d in range(64)])


def both_halves(rows):
    other = from_sibling(rows)
    core = lax.rem(lax.axis_index("dp"), 2)
    return jnp.where(core == 0, jnp.concatenate((rows, other)), jnp.concatenate((other, rows)))


def summed_half(terms):
    core = lax.rem(lax.axis_index("dp"), 2)
    half = terms.shape[0] // 2
    theirs = from_sibling(lax.dynamic_slice_in_dim(terms, (1 - core) * half, half))
    return lax.dynamic_slice_in_dim(terms, core * half, half).astype(F32) + theirs.astype(F32)


def packed_vectors(b_query, b_value, b_up, features):
    dp, low = lax.axis_index("dp"), lax.axis_index("tensor")
    own = jnp.arange(128)[:, None] == low * 64 + dp
    parts = [jnp.where(own, v.astype(F32)[None], 0.0).reshape(-1) for v in (b_query, b_value, b_up)]
    own = (jnp.arange(64)[:, None] == dp) & (low == 0)
    parts += [jnp.where(own, v.astype(F32)[None], 0.0).reshape(-1) for v in features]
    return jnp.concatenate(parts).reshape(VEC_ROWS, 128)


def unpacked_vectors(flat):
    dp, low = lax.axis_index("dp"), lax.axis_index("tensor")
    out, at = [], 0
    for length in (8, 8, 32):
        out.append(lax.dynamic_slice(flat, (at + (low * 64 + dp) * length,), (length,)))
        at += length * 128
    for _ in range(6):
        out.append(lax.dynamic_slice(flat, (at + dp * 16,), (16,)))
        at += 1024
    return out


HEAD_DIM = 64
epsilon = 1e-12


def layer_norm(hidden, gain, shift):
    average = jnp.mean(hidden, axis=-1, keepdims=True)
    centered = hidden - average
    variance = jnp.mean(centered * centered, axis=-1, keepdims=True)
    return centered * lax.rsqrt(variance + epsilon) * gain + shift


def gelu_exact(values):
    return jax.nn.gelu(values, approximate=False)


def masked_scores(heads_query, heads_key, allowed):
    scores = jnp.einsum("qhd,khd->hqk", heads_query, heads_key, preferred_element_type=jnp.float32)
    return jnp.where(allowed[None], scores * HEAD_DIM ** (-0.5), -1000000000.0)


def on_device(
    tokens,
    segment,
    w_query,
    w_key,
    w_value,
    w_out,
    w_up,
    w_down,
    b_query,
    b_value,
    b_up,
    b_out,
    b_down,
    gain_one,
    shift_one,
    gain_two,
    shift_two,
    out_grad,
):
    own_len = tokens.shape[0]
    vec = packed_vectors(
        b_query, b_value, b_up, (b_out, b_down, gain_one, shift_one, gain_two, shift_two)
    )
    own = jnp.concatenate((w_query, w_key, w_value, w_out, w_up, w_down), axis=1)
    own, tokens, out_grad, segment = (swapped(a) for a in (own, tokens, out_grad, segment))
    own = own.reshape(16, TILES, COLS).transpose(1, 0, 2)
    w_tiles, vec = gather_call(own, vec)
    full = w_tiles.reshape(TILES, 1024, COLS).transpose(1, 0, 2).reshape(1024, TILES * COLS)
    query_full, key_full, value_full, out_full, up_full, down_full = jnp.split(
        full, (512, 1024, 1536, 2048, 4096), axis=1
    )
    core = lax.rem(lax.axis_index("dp"), 2)
    bquery_full = vec[0:8].reshape(2, 512)[core]
    bvalue_full = vec[8:16].reshape(2, 512)[core]
    bup_full = vec[16:48].reshape(2, 2048)[core]
    bout_full, bdown_full, gone_full, sone_full, gtwo_full, stwo_full = vec[48:96].reshape(6, 1024)
    rows_all = both_halves(tokens)
    group_len = rows_all.shape[0]
    local_heads = query_full.shape[1] // HEAD_DIM
    queries = (
        jnp.dot(rows_all, query_full, preferred_element_type=jnp.float32)
        + bquery_full.astype(jnp.float32)
    ).astype(jnp.bfloat16)
    key_rows = jnp.dot(rows_all, key_full, preferred_element_type=jnp.float32).astype(jnp.bfloat16)
    value_rows = (
        jnp.dot(rows_all, value_full, preferred_element_type=jnp.float32)
        + bvalue_full.astype(jnp.float32)
    ).astype(jnp.bfloat16)
    heads_query = queries.reshape(group_len, local_heads, HEAD_DIM)
    heads_key = key_rows.reshape(group_len, local_heads, HEAD_DIM)
    heads_value = value_rows.reshape(group_len, local_heads, HEAD_DIM)
    allowed = segment[:, None] == segment[None, :]
    scores = masked_scores(heads_query, heads_key, allowed)
    peak = jnp.max(scores, axis=-1, keepdims=True)
    log_total = peak + jnp.log(jnp.sum(jnp.exp(scores - peak), axis=-1, keepdims=True))
    attn_probs = jnp.exp(scores - log_total)
    context = (
        jnp.einsum(
            "hqk,khd->qhd",
            attn_probs.astype(jnp.bfloat16),
            heads_value,
            preferred_element_type=jnp.float32,
        )
        .reshape(group_len, -1)
        .astype(jnp.bfloat16)
    )
    attn_terms = jnp.einsum("gc,dc->gd", context, out_full, preferred_element_type=jnp.float32)
    attended = summed_half(attn_terms)
    mixed_sum = tokens.astype(jnp.float32) + attended + bout_full.astype(jnp.float32)
    normed_one, norm_one_back = jax.vjp(
        layer_norm, mixed_sum, gone_full.astype(jnp.float32), sone_full.astype(jnp.float32)
    )
    normed_all = both_halves(normed_one.astype(jnp.bfloat16))
    up_pre = jnp.dot(normed_all, up_full, preferred_element_type=jnp.float32) + bup_full.astype(
        jnp.float32
    )
    activated, gelu_back = jax.vjp(gelu_exact, up_pre)
    activated_low = activated.astype(jnp.bfloat16)
    mlp_terms = jnp.einsum(
        "gf,df->gd", activated_low, down_full, preferred_element_type=jnp.float32
    )
    down_out = summed_half(mlp_terms)
    normed_two, norm_two_back = jax.vjp(
        layer_norm,
        normed_one + down_out + bdown_full.astype(jnp.float32),
        gtwo_full.astype(jnp.float32),
        stwo_full.astype(jnp.float32),
    )
    own_seg = lax.dynamic_slice_in_dim(segment, core * own_len, own_len)
    live = (own_seg >= 0).astype(jnp.float32)[:, None]
    layer_out = (normed_two * live).astype(jnp.bfloat16)
    query_back, key_back, value_back, out_back, up_back, down_back = (
        query_full, key_full, value_full, out_full, up_full, down_full
    )
    d_two, grad_gain_two, grad_shift_two = norm_two_back(out_grad * live)
    grad_b_down = jnp.sum(d_two, axis=0)
    grad_down_all = both_halves(d_two.astype(jnp.bfloat16))
    grad_w_down = jnp.einsum(
        "gd,gf->df", grad_down_all, activated_low, preferred_element_type=jnp.float32
    )
    grad_act = jnp.einsum("gd,df->gf", grad_down_all, down_back, preferred_element_type=jnp.float32)
    (grad_up_pre,) = gelu_back(grad_act)
    grad_up_low = grad_up_pre.astype(jnp.bfloat16)
    grad_b_up = jnp.sum(grad_up_low, axis=0, dtype=jnp.float32)
    grad_w_up = jnp.einsum("gd,gf->df", normed_all, grad_up_low, preferred_element_type=jnp.float32)
    normed_terms = jnp.einsum("gf,df->gd", grad_up_low, up_back, preferred_element_type=jnp.float32)
    grad_normed = d_two + summed_half(normed_terms)
    d_one, grad_gain_one, grad_shift_one = norm_one_back(grad_normed)
    grad_b_out = jnp.sum(d_one, axis=0)
    grad_attn_all = both_halves(d_one.astype(jnp.bfloat16))
    grad_w_out = jnp.einsum("gd,gc->dc", grad_attn_all, context, preferred_element_type=jnp.float32)
    grad_context = jnp.einsum(
        "gd,dc->gc", grad_attn_all, out_back, preferred_element_type=jnp.float32
    )
    grad_context = grad_context.astype(jnp.bfloat16).reshape(group_len, local_heads, HEAD_DIM)
    again_probs = jnp.exp(masked_scores(heads_query, heads_key, allowed) - log_total)
    grad_probs = jnp.einsum(
        "qhd,khd->hqk", grad_context, heads_value, preferred_element_type=jnp.float32
    )
    grad_value = jnp.einsum(
        "hqk,qhd->khd",
        again_probs.astype(jnp.bfloat16),
        grad_context,
        preferred_element_type=jnp.float32,
    )
    grad_scores = again_probs * (
        grad_probs - jnp.sum(grad_probs * again_probs, axis=-1, keepdims=True)
    )
    grad_scores_low = grad_scores.astype(jnp.bfloat16)
    grad_query = jnp.einsum(
        "hqk,khd->qhd", grad_scores_low, heads_key, preferred_element_type=jnp.float32
    ) * HEAD_DIM ** (-0.5)
    grad_key = jnp.einsum(
        "hqk,qhd->khd", grad_scores_low, heads_query, preferred_element_type=jnp.float32
    ) * HEAD_DIM ** (-0.5)
    grad_query_low = grad_query.reshape(group_len, -1).astype(jnp.bfloat16)
    grad_key_low = grad_key.reshape(group_len, -1).astype(jnp.bfloat16)
    grad_value_low = grad_value.reshape(group_len, -1).astype(jnp.bfloat16)
    grad_b_query = jnp.sum(grad_query_low, axis=0, dtype=jnp.float32)
    grad_b_value = jnp.sum(grad_value_low, axis=0, dtype=jnp.float32)
    grad_w_query = jnp.einsum(
        "gd,gc->dc", rows_all, grad_query_low, preferred_element_type=jnp.float32
    )
    grad_w_key = jnp.einsum("gd,gc->dc", rows_all, grad_key_low, preferred_element_type=jnp.float32)
    grad_w_value = jnp.einsum(
        "gd,gc->dc", rows_all, grad_value_low, preferred_element_type=jnp.float32
    )
    rows_terms = (
        jnp.einsum("gc,dc->gd", grad_query_low, query_back, preferred_element_type=jnp.float32)
        + jnp.einsum("gc,dc->gd", grad_key_low, key_back, preferred_element_type=jnp.float32)
        + jnp.einsum("gc,dc->gd", grad_value_low, value_back, preferred_element_type=jnp.float32)
    )
    input_grad = d_one + summed_half(rows_terms.astype(jnp.bfloat16))
    halves = jnp.arange(2)[:, None] == core
    totals = jnp.concatenate(
        [
            jnp.where(halves, grad[None], 0.0).reshape(-1)
            for grad in (grad_b_query, grad_b_value, grad_b_up)
        ]
        + [grad_b_out, grad_b_down, grad_gain_one, grad_shift_one, grad_gain_two, grad_shift_two]
    ).reshape(VEC_ROWS, 128)
    grads = jnp.concatenate(
        (grad_w_query, grad_w_key, grad_w_value, grad_w_out, grad_w_up, grad_w_down), axis=1
    ).astype(jnp.bfloat16)
    grads = grads.reshape(4, 4, 4, 16, TILES, COLS).transpose(4, 0, 1, 2, 3, 5)
    own_grads, totals = scatter_call(grads, totals)
    own_grads = own_grads.transpose(1, 0, 2).reshape(16, TILES * COLS)
    own_grads, layer_out, input_grad = (swapped(a) for a in (own_grads, layer_out, input_grad))
    return (
        layer_out,
        input_grad,
        *jnp.split(own_grads, (512, 1024, 1536, 2048, 4096), axis=1),
        *unpacked_vectors(totals.reshape(-1)),
    )


def solution(mesh):
    placed = (
        P(("dp", "tensor"), None),
        P("dp"),
        P("dp", "tensor"),
        P("dp", "tensor"),
        P("dp", "tensor"),
        P("dp", "tensor"),
        P("dp", "tensor"),
        P("dp", "tensor"),
        P(("tensor", "dp")),
        P(("tensor", "dp")),
        P(("tensor", "dp")),
        P("dp"),
        P("dp"),
        P("dp"),
        P("dp"),
        P("dp"),
        P("dp"),
        P(("dp", "tensor"), None),
    )
    return jax.shard_map(
        on_device,
        mesh=mesh,
        in_specs=placed,
        out_specs=(
            P(("dp", "tensor"), None),
            P(("dp", "tensor"), None),
            P("dp", "tensor"),
            P("dp", "tensor"),
            P("dp", "tensor"),
            P("dp", "tensor"),
            P("dp", "tensor"),
            P("dp", "tensor"),
            P(("tensor", "dp")),
            P(("tensor", "dp")),
            P(("tensor", "dp")),
            P("dp"),
            P("dp"),
            P("dp"),
            P("dp"),
            P("dp"),
            P("dp"),
        ),
        check_vma=False,
    )
```

```python
import functools

import jax
import jax.numpy as jnp
from jax import lax
from jax.experimental import pallas as pl
from jax.experimental.pallas import tpu as pltpu
from jax.sharding import PartitionSpec as P

MESH = pl.DeviceIdType.MESH
F32 = jnp.float32
BF16 = jnp.bfloat16

SQUARES = ((1, "a"), (0, "a"), (2, "a"), (1, "b"), (0, "b"), (2, "b"))
TILES = 24
COLS = 256
ROUTES = 6
VEC_ROWS = 96


def position():
    dp, low = lax.axis_index("dp"), lax.axis_index("tensor")
    return (dp // 16, lax.rem(dp // 4, 4), lax.rem(dp // 2, 2) * 2 + low), lax.rem(dp, 2)


def device(chip, core):
    y, x, z = chip
    return (y * 16 + x * 4 + (z // 2) * 2 + core, lax.rem(z, 2))


def across(chip, square):
    axis, kind = square
    at = chip[axis]
    new = at + 1 - 2 * lax.rem(at, 2) if kind == "a" else 3 - at
    return tuple(new if k == axis else c for k, c in enumerate(chip))


def route_squares(route):
    return [SQUARES[(route + s) % 6] for s in range(6)]


def pieces(chip, done):
    per_axis = []
    for axis in range(3):
        at = chip[axis]
        kinds = {kind for a, kind in done if a == axis}
        if not kinds:
            per_axis.append([(at, 1)])
        elif kinds == {"a"}:
            per_axis.append([(at // 2 * 2, 2)])
        elif kinds == {"b"}:
            per_axis.append([(at, 1), (3 - at, 1)])
        else:
            per_axis.append([(0, 4)])
    return [
        ((ky, kx, kz), (y, x, z))
        for ky, y in enumerate(per_axis[0])
        for kx, x in enumerate(per_axis[1])
        for kz, z in enumerate(per_axis[2])
    ]


def span(done):
    sizes = []
    for axis in range(3):
        kinds = {kind for a, kind in done if a == axis}
        sizes.append(1 << len(kinds))
    return sizes


def view(ref, tiles, piece):
    return ref.at[(pl.ds(*tiles),) + tuple(pl.ds(*p) for p in piece)]


def piece_counts():
    return [[len(pieces((0, 0, 0), route_squares(r)[:s])) for s in range(6)] for r in range(ROUTES)]


COUNTS = piece_counts()
COPIES = sum(map(sum, COUNTS))


def first_sem(route, stage):
    return sum(sum(c) for c in COUNTS[:route]) + sum(COUNTS[route][:stage])


class Gather:
    def __init__(self, w, send, recv, tiles_of, base=0):
        self.w, self.send, self.recv, self.tiles_of, self.base = w, send, recv, tiles_of, base
        self.chip, self.core = position()

    def copies(self, route, stage):
        squares = route_squares(route)
        target = device(across(self.chip, squares[stage]), self.core)
        out = []
        for n, (_, piece) in enumerate(pieces(self.chip, squares[:stage])):
            part = view(self.w, self.tiles_of(route), piece)
            sem = self.base + first_sem(route, stage) + n
            out.append(
                pltpu.make_async_remote_copy(
                    src_ref=part,
                    dst_ref=part,
                    send_sem=self.send.at[sem],
                    recv_sem=self.recv.at[sem],
                    device_id=target,
                    device_id_type=MESH,
                )
            )
        return out

    def start(self, route, stage):
        for c in self.copies(route, stage):
            c.start()

    def wait_recv(self, route, stage):
        for c in self.copies(route, stage):
            c.wait_recv()

    def wait_send(self, route, stage):
        for c in self.copies(route, stage):
            c.wait_send()


def landing_shapes(tiles_of):
    shapes = []
    for route in range(ROUTES):
        for stage in range(6):
            done = route_squares(route)[: 5 - stage]
            (_, piece) = pieces((0, 0, 0), done)[0]
            shapes.append(
                (COUNTS[route][5 - stage], tiles_of(route)[1]) + tuple(n for _, n in piece) + (16, COLS)
            )
    return shapes


class Scatter:
    def __init__(self, g, landings, send, recv, tiles_of, base=0):
        self.g, self.landings, self.send, self.recv = g, landings, send, recv
        self.tiles_of, self.base = tiles_of, base
        self.chip, self.core = position()

    def copies(self, route, stage):
        squares = route_squares(route)[: 6 - stage]
        over = across(self.chip, squares[-1])
        target = device(over, self.core)
        out = []
        for n, (_, piece) in enumerate(pieces(over, squares[:-1])):
            sem = self.base + first_sem(route, 5 - stage) + n
            out.append(
                pltpu.make_async_remote_copy(
                    src_ref=view(self.g, self.tiles_of(route), piece),
                    dst_ref=self.landings[route * 6 + stage].at[n],
                    send_sem=self.send.at[sem],
                    recv_sem=self.recv.at[sem],
                    device_id=target,
                    device_id_type=MESH,
                )
            )
        return out

    def start(self, route, stage):
        for c in self.copies(route, stage):
            c.start()

    def wait_send(self, route, stage):
        for c in self.copies(route, stage):
            c.wait_send()

    def take(self, route, stage):
        for c in self.copies(route, stage):
            c.wait_recv()
        tile0, tiles = self.tiles_of(route)
        done = route_squares(route)[: 5 - stage]
        landed = self.landings[route * 6 + stage]
        for n, (_, piece) in enumerate(pieces(self.chip, done)):
            (y0, ny), (x0, nx), (z0, nz) = piece

            def add(i, carry):
                tile, y = i // ny, lax.rem(i, ny)
                at = (tile0 + tile, y0 + y, pl.ds(x0, nx), pl.ds(z0, nz))
                total = self.g[at].astype(F32) + landed[n, tile, y].astype(F32)
                self.g[at] = total.astype(BF16)
                return carry

            lax.fori_loop(0, tiles * ny, add, 0)


def greet(others):
    barrier = pltpu.get_barrier_semaphore()
    for other in others:
        pl.semaphore_signal(barrier, inc=1, device_id=other, device_id_type=MESH)
    pl.semaphore_wait(barrier, len(others))


def neighbours():
    chip, core = position()
    return [device(across(chip, square), core) for square in SQUARES]


def sibling():
    chip, core = position()
    return device(chip, 1 - core)


class VectorSum:
    def __init__(self, kept, came, send, recv, base):
        self.kept, self.came, self.send, self.recv, self.base = kept, came, send, recv, base

    def copy(self, stage):
        target = (neighbours() + [sibling()])[stage]
        return pltpu.make_async_remote_copy(
            src_ref=self.kept.at[stage],
            dst_ref=self.came.at[stage],
            send_sem=self.send.at[self.base + stage],
            recv_sem=self.recv.at[self.base + stage],
            device_id=target,
            device_id_type=MESH,
        )

    def start(self, stage):
        self.copy(stage).start()

    def take(self, stage):
        self.copy(stage).wait_recv()
        self.kept[stage + 1] = self.kept[stage] + self.came[stage]

    def wait_send(self, stage):
        self.copy(stage).wait_send()


def early_tiles(route):
    return (route, 1)


def late_tiles(route):
    return (6 + route * 3, 3)


GROUP = 512
HALF = 256
WIDTH = 1024
HEAD_DIM = 64
PAIR = 2 * HEAD_DIM
SCALE = HEAD_DIM**-0.5
EPSILON = 1e-12
NN = (((1,), (0,)), ((), ()))
NT = (((1,), (1,)), ((), ()))
TN = (((0,), (0,)), ((), ()))
Q_TILE, OUT_TILE, UP_TILE, DOWN_TILE = 0, 6, 8, 16
WEIGHT_TILES = (2, 2, 2, 2, 8, 8)


def dot(a, b, dims=NN):
    return lax.dot_general(a, b, dims, preferred_element_type=F32)


def loop(count, body):
    def step(i, carry):
        body(i)
        return carry

    lax.fori_loop(0, count, step, 0)


def layer_kernel(
    w_q, w_k, w_v, w_o, w_u, w_d, vec, seg, tokens, out_grad,
    layer_out, input_grad, g_q, g_k, g_v, g_o, g_u, g_d, vec_out,
    w, g, x, n1, gd, tr, qkv, probs, bias, ctx, gctx, ds, part, leave, come,
    hat, inv, d_two, cot, act, slope, segments, segcol, features, biases, bias_sums, sums,
    out_rows, own_grads_q, own_grads_k, own_grads_v, own_grads_o, own_grads_u, own_grads_d,
    kept, came, kept_back, came_back,
    gsend, grecv, ssend, srecv, vsend, vrecv, swap_send, swap_recv, sib_send, sib_recv,
    *landings,
):
    chip, core = position()
    y, x_at, z = chip
    low = lax.rem(z, 2)
    opposite_chip = across(chip, (2, "a"))
    diagonal = device(opposite_chip, 1 - core)
    twin = sibling()
    stays = core == low
    own_rows = pl.ds(pl.multiple_of(core * HALF, HALF), HALF)
    other_rows = pl.ds(pl.multiple_of((1 - core) * HALF, HALF), HALF)

    def swap_copies(n, src, dst_here, dst_there):
        away = pltpu.make_async_remote_copy(
            src_ref=src, dst_ref=dst_there, send_sem=swap_send.at[n], recv_sem=swap_recv.at[n],
            device_id=diagonal, device_id_type=MESH,
        )
        return away, pltpu.make_async_copy(src, dst_here, swap_recv.at[n])

    def swap_start(n, src, dst_here, dst_there):
        away, here = swap_copies(n, src, dst_here, dst_there)
        pl.when(stays)(here.start)
        pl.when(jnp.logical_not(stays))(away.start)

    def swap_wait(n, src, dst_here, dst_there):
        away, here = swap_copies(n, src, dst_here, dst_there)
        pl.when(stays)(here.wait)
        pl.when(jnp.logical_not(stays))(away.wait)

    def to_twin(n, src, dst):
        return pltpu.make_async_remote_copy(
            src_ref=src, dst_ref=dst, send_sem=sib_send.at[n], recv_sem=sib_recv.at[n],
            device_id=twin, device_id_type=MESH,
        )

    greet(neighbours() + [twin, diagonal])

    weight_moves = []
    tile = 0
    for ref, count in zip((w_q, w_k, w_v, w_o, w_u, w_d), WEIGHT_TILES):
        for k in range(count):
            weight_moves.append(
                (
                    tile,
                    ref.at[:, pl.ds(k * COLS, COLS)],
                    w.at[tile, y, x_at, z],
                    w.at[(tile,) + opposite_chip],
                )
            )
            tile += 1
    seg_move = (TILES, seg, segments, segments)
    row_move = (TILES + 1, tokens, x.at[own_rows], x.at[other_rows])
    cot_move = (TILES + 2, out_grad, cot, cot)
    for move in weight_moves:
        swap_start(*move)
    swap_start(*row_move)
    swap_start(*seg_move)
    swap_start(*cot_move)
    vectors = VectorSum(kept, came, vsend, vrecv, 0)
    kept[0] = vec[...]
    vectors.start(0)

    early = Gather(w, gsend, grecv, early_tiles)
    late = Gather(w, gsend, grecv, late_tiles, COPIES)
    for stage in range(4):
        if stage == 0:
            for move in weight_moves:
                swap_wait(*move)
        for phase in (early, late):
            for route in range(ROUTES):
                if stage:
                    phase.wait_recv(route, stage - 1)
                phase.start(route, stage)
        vectors.take(stage)
        vectors.start(stage + 1)
    for stage in (4, 5):
        for route in range(ROUTES):
            early.wait_recv(route, stage - 1)
            early.start(route, stage)
        vectors.take(stage)
        vectors.start(stage + 1)
    for route in range(ROUTES):
        late.wait_recv(route, 3)
        late.start(route, 4)

    swap_wait(*row_move)
    rows_copy = to_twin(0, x.at[own_rows], x.at[own_rows])
    rows_copy.start()
    swap_wait(*seg_move)
    across_lanes = jnp.broadcast_to(segments[0:1, :], (128, GROUP))
    segcol[...] = across_lanes.T
    for k in range(4):
        cols = slice(k * 128, k * 128 + 128)
        bias[:, cols] = jnp.where(segcol[...] == segments[0:1, cols], 0.0, -1000000000.0)
    vectors.take(6)
    for n in range(6):
        for k in range(8):
            features[n, :, k * 128 : k * 128 + 128] = kept[7, 48 + n * 8 + k : 49 + n * 8 + k, :]
    for k in range(2):
        for half in range(2):
            lanes = slice(half * 128, half * 128 + 128)
            biases[k, :, lanes] = kept[7, pl.ds(core * 4 + k * 2 + half, 1), :]
            biases[4 + k, :, lanes] = kept[7, pl.ds(8 + core * 4 + k * 2 + half, 1), :]
        biases[2 + k] = jnp.zeros((1, COLS), F32)
    for k in range(8):
        for half in range(2):
            lanes = slice(half * 128, half * 128 + 128)
            biases[6 + k, :, lanes] = kept[7, pl.ds(16 + core * 16 + k * 2 + half, 1), :]
    rows_copy.wait_recv()

    for route in range(ROUTES):
        early.wait_recv(route, 5)

    def weight(tile):
        return w[tile].reshape(WIDTH, COLS)

    def project(t):
        made = (dot(x[...], weight(t)) + biases[t]).astype(BF16)
        qkv[2 * t] = made[:, :128]
        qkv[2 * t + 1] = made[:, 128:]

    loop(6, project)
    low_lanes = lax.broadcasted_iota(jnp.int32, (1, PAIR), 1) < HEAD_DIM

    def only(head, values):
        keep = low_lanes if head == 0 else jnp.logical_not(low_lanes)
        return jnp.where(keep, values, jnp.zeros_like(values))

    def attend(pair):
        for half in range(2):
            rows = slice(half * HALF, half * HALF + HALF)
            query = qkv[pair, rows]
            outs = []
            for head in range(2):
                scores = dot(qkv[4 + pair], only(head, query), NT) * SCALE + bias[:, rows]
                scores = jnp.exp(scores - jnp.max(scores, axis=0, keepdims=True))
                weights = scores * (1.0 / jnp.sum(scores, axis=0, keepdims=True))
                weights = weights.astype(BF16)
                probs[2 * pair + head, :, rows] = weights
                outs.append(dot(weights, qkv[8 + pair], TN))
            ctx[pair, rows] = jnp.where(low_lanes, outs[0], outs[1]).astype(BF16)

    loop(2, attend)
    for route in range(ROUTES):
        late.wait_recv(route, 4)
        late.start(route, 5)
    loop(2, lambda pair: attend(pair + 2))
    for route in range(ROUTES):
        late.wait_recv(route, 5)

    terms_sent = []

    def row_terms(n, tiles, left):
        def block(rows, store):
            def one(k):
                lanes = pl.ds(pl.multiple_of(k * COLS, COLS), COLS)
                total = None
                for t, at in enumerate(tiles):
                    term = dot(left(t, rows), w[at, k].reshape(COLS, COLS), NT)
                    total = term if total is None else total + term
                store(lanes, total)

            loop(4, one)

        if n:
            terms_sent[-1].wait_send()

        def leaves(lanes, total):
            leave[:, lanes] = total.astype(BF16)

        def stays_here(lanes, total):
            part[:, lanes] = total

        block(other_rows, leaves)
        copy = to_twin(1 + n, leave, come)
        copy.start()
        block(own_rows, stays_here)
        copy.wait_recv()
        terms_sent.append(copy)

    def side_by_side(ref, first, rows=slice(None)):
        return jnp.concatenate([ref[first, rows], ref[first + 1, rows]], axis=1)

    sent = [rows_copy]
    row_terms(0, range(OUT_TILE, UP_TILE), lambda t, rows: side_by_side(ctx, 2 * t, rows))
    chunk = 64

    def by_chunks(body):
        def one(i):
            at = pl.multiple_of(i * chunk, chunk)
            body(pl.ds(at, chunk), pl.ds(pl.multiple_of(core * HALF + at, chunk), chunk))

        loop(HALF // chunk, one)

    def mean(values):
        return jnp.mean(values, axis=-1, keepdims=True)

    def normalized(hidden):
        centered = hidden - mean(hidden)
        scale = lax.rsqrt(mean(centered * centered) + EPSILON)
        return centered * scale, scale

    for n in range(6):
        sums[n] = jnp.zeros((1, WIDTH), F32)

    def add_sum(n, values):
        sums[n] += jnp.sum(values, axis=0, keepdims=True)

    b_out, b_down, gain_one, shift_one, gain_two, shift_two = range(6)

    def first_norm(here, there):
        hidden = x[there].astype(F32) + part[here] + come[here].astype(F32) + features[b_out]
        value, scale = normalized(hidden)
        hat[here] = value
        inv[here] = jnp.broadcast_to(scale, (chunk, 128))
        n1[there] = (value * features[gain_one] + features[shift_one]).astype(BF16)

    by_chunks(first_norm)

    shared = {}

    def share_rows(n, ref):
        copy = to_twin(n, ref.at[own_rows], ref.at[own_rows])
        copy.start()
        shared[n] = copy
        copy.wait_recv()

    share_rows(5, n1)

    def up(t):
        for half in range(2):
            rows = slice(half * HALF, half * HALF + HALF)
            pre = dot(n1[rows], weight(UP_TILE + t)) + biases[6 + t]
            below = 0.5 * (1.0 + lax.erf(pre * (0.5**0.5)))
            act[t, rows] = (pre * below).astype(BF16)
            bell = jnp.exp(pre * pre * -0.5) * 0.3989422804014327
            slope[t, rows] = (below + pre * bell).astype(BF16)

    loop(8, up)
    row_terms(1, range(DOWN_TILE, TILES), lambda t, rows: act[t, rows])
    swap_wait(*cot_move)

    def norm_back(values, incoming, gain, scale, gain_at, shift_at):
        add_sum(shift_at, incoming)
        add_sum(gain_at, incoming * values)
        scaled = incoming * gain
        return scale * (scaled - mean(scaled) - values * mean(scaled * values))

    def second_norm(here, there):
        first = hat[here] * features[gain_one] + features[shift_one]
        value, scale = normalized(first + part[here] + come[here].astype(F32) + features[b_down])
        live = jnp.where(segcol[there, 0:1] >= 0, 1.0, 0.0)
        out_rows[here] = ((value * features[gain_two] + features[shift_two]) * live).astype(BF16)
        back = norm_back(
            value, cot[here] * live, features[gain_two], scale, gain_two, shift_two
        )
        add_sum(b_down, back)
        d_two[here] = back
        gd[there] = back.astype(BF16)

    by_chunks(second_norm)
    out_move = (TILES + 3, out_rows, layer_out, layer_out)
    swap_start(*out_move)
    share_rows(6, gd)

    def turn(ref):
        for k in range(4):
            rows = slice(k * COLS, k * COLS + COLS)
            tr[rows, :] = ref[:, rows].T

    def store_grad(tile, right):
        for k in range(4):
            made = dot(tr[k * COLS : k * COLS + COLS, :], right)
            g[tile, k] = made.astype(BF16).reshape(4, 4, 16, COLS)

    scatter_late = Scatter(g, landings[:36], ssend, srecv, late_tiles)
    scatter_early = Scatter(g, landings[36:], ssend, srecv, early_tiles, COPIES)

    turn(gd)
    loop(8, lambda t: store_grad(DOWN_TILE + t, act[t]))
    for route in (5, 4):
        scatter_late.start(route, 0)

    def up_back(t):
        made = (dot(gd[...], weight(DOWN_TILE + t)) * slope[t].astype(F32)).astype(BF16)
        slope[t] = made
        bias_sums[6 + t] = jnp.sum(made.astype(F32), axis=0, keepdims=True)

    loop(8, up_back)
    turn(n1)
    loop(8, lambda t: store_grad(UP_TILE + t, slope[t]))
    for route in (3, 2, 1):
        scatter_late.start(route, 0)
    row_terms(2, range(UP_TILE, DOWN_TILE), lambda t, rows: slope[t, rows])

    def first_norm_back(here, there):
        incoming = d_two[here] + part[here] + come[here].astype(F32)
        back = norm_back(
            hat[here], incoming, features[gain_one], inv[here, 0:1], gain_one, shift_one
        )
        add_sum(b_out, back)
        d_two[here] = back
        n1[there] = back.astype(BF16)

    shared.pop(5).wait_send()
    d1 = n1
    by_chunks(first_norm_back)
    share_rows(7, d1)
    turn(d1)
    loop(2, lambda u: store_grad(OUT_TILE + u, side_by_side(ctx, 2 * u)))
    scatter_late.start(0, 0)

    def context_back(u):
        made = dot(d1[...], weight(OUT_TILE + u)).astype(BF16)
        gctx[2 * u] = made[:, :128]
        gctx[2 * u + 1] = made[:, 128:]

    loop(2, context_back)

    def attend_back(pair):
        for half in range(2):
            rows = slice(half * HALF, half * HALF + HALF)
            for head in range(2):
                weights = probs[2 * pair + head, :, rows].astype(F32)
                grad = dot(qkv[8 + pair], only(head, gctx[pair, rows]), NT)
                total = jnp.sum(grad * weights, axis=0, keepdims=True)
                ds[head, :, rows] = (weights * (grad - total)).astype(BF16)
        query = [dot(ds[head], qkv[4 + pair], TN) for head in range(2)]
        key = [dot(ds[head], qkv[pair]) for head in range(2)]
        value = [dot(probs[2 * pair + head], gctx[pair]) for head in range(2)]
        for at, (a, b), scale in ((0, query, SCALE), (4, key, SCALE), (8, value, 1.0)):
            made = (jnp.where(low_lanes, a, b) * scale).astype(BF16)
            qkv[at + pair] = made
            bias_sums[14 + at + pair, :, :PAIR] = jnp.sum(made.astype(F32), axis=0, keepdims=True)

    loop(4, attend_back)
    for route in range(ROUTES):
        scatter_late.take(route, 0)
        scatter_late.start(route, 1)
    turn(x)
    loop(6, lambda t: store_grad(t, side_by_side(qkv, 2 * t)))
    for route in range(ROUTES):
        scatter_early.start(route, 0)

    zero = jnp.zeros((1, 128), F32)
    kept_back[0] = jnp.zeros((VEC_ROWS, 128), F32)
    for k in range(4):
        kept_back[0, pl.ds(core * 4 + k, 1), :] = bias_sums[14 + k, :, :PAIR]
        kept_back[0, pl.ds(8 + core * 4 + k, 1), :] = bias_sums[22 + k, :, :PAIR]
    for k in range(8):
        for half in range(2):
            lanes = slice(half * 128, half * 128 + 128)
            kept_back[0, pl.ds(16 + core * 16 + k * 2 + half, 1), :] = bias_sums[6 + k, :, lanes]
    for n in range(6):
        for k in range(8):
            at = 48 + n * 8 + k
            kept_back[0, at : at + 1, :] = sums[n, :, k * 128 : k * 128 + 128]
    vectors_back = VectorSum(kept_back, came_back, vsend, vrecv, 7)
    vectors_back.start(0)
    row_terms(3, range(6), lambda t, rows: side_by_side(qkv, 2 * t, rows))

    def last_rows(here, there):
        cot[here] = d_two[here] + part[here] + come[here].astype(F32)

    by_chunks(last_rows)
    grad_move = (TILES + 4, cot, input_grad, input_grad)
    swap_start(*grad_move)

    for stage in range(1, 6):
        for route in range(ROUTES):
            scatter_late.take(route, stage)
            if stage < 5:
                scatter_late.start(route, stage + 1)
        for route in range(ROUTES):
            scatter_early.take(route, stage - 1)
            scatter_early.start(route, stage)
        vectors_back.take(stage - 1)
        vectors_back.start(stage)
    for route in range(ROUTES):
        scatter_early.take(route, 5)
    vectors_back.take(5)
    vectors_back.start(6)
    tile = 0
    grad_moves = []
    own_grads = (own_grads_q, own_grads_k, own_grads_v, own_grads_o, own_grads_u, own_grads_d)
    outs = (g_q, g_k, g_v, g_o, g_u, g_d)
    for n, (ref, out, count) in enumerate(zip(own_grads, outs, WEIGHT_TILES)):
        for k in range(count):
            ref[:, k * COLS : k * COLS + COLS] = g[tile, y, x_at, z].astype(F32)
            tile += 1
        grad_moves.append((TILES + 5 + n, ref, out, out))
        swap_start(*grad_moves[-1])
    vectors_back.take(6)
    vec_out[...] = kept_back[7]

    for move in [out_move, grad_move] + grad_moves:
        swap_wait(*move)
    for copy in sent + terms_sent[-1:] + list(shared.values()):
        copy.wait_send()
    for stage in range(6):
        for route in range(ROUTES):
            early.wait_send(route, stage)
            late.wait_send(route, stage)
            scatter_early.wait_send(route, stage)
            scatter_late.wait_send(route, stage)
    for stage in range(7):
        vectors.wait_send(stage)
        vectors_back.wait_send(stage)


def layer_call(*arrays):
    full = (TILES, 4, 4, 4, 16, COLS)
    vmem = functools.partial(pl.BlockSpec, memory_space=pltpu.VMEM)
    anywhere = functools.partial(pl.BlockSpec, memory_space=pl.ANY)
    rows = (GROUP, WIDTH)
    half = (HALF, WIDTH)
    shares = [(16, count * COLS) for count in WEIGHT_TILES]
    scratch = [
        (full, BF16), (full, BF16),
        (rows, BF16), (rows, BF16), (rows, BF16), ((WIDTH, GROUP), BF16),
        ((12, GROUP, PAIR), BF16), ((8, GROUP, GROUP), BF16), ((GROUP, GROUP), F32),
        ((4, GROUP, PAIR), BF16), ((4, GROUP, PAIR), BF16), ((2, GROUP, GROUP), BF16),
        (half, F32), (half, BF16), (half, BF16),
        (half, F32), ((HALF, 128), F32), (half, F32), (half, F32),
        ((8, GROUP, COLS), BF16), ((8, GROUP, COLS), BF16),
        ((8, GROUP), F32), ((GROUP, 128), F32),
        ((6, 1, WIDTH), F32), ((14, 1, COLS), F32), ((26, 1, COLS), F32), ((6, 1, WIDTH), F32),
        (half, BF16),
    ] + [(share, F32) for share in shares] + [
        ((8, VEC_ROWS, 128), F32), ((7, VEC_ROWS, 128), F32),
        ((8, VEC_ROWS, 128), F32), ((7, VEC_ROWS, 128), F32),
    ]
    sems = [2 * COPIES] * 4 + [14] * 2 + [TILES + 11] * 2 + [8] * 2
    return pl.pallas_call(
        layer_kernel,
        out_shape=(
            jax.ShapeDtypeStruct(half, BF16),
            jax.ShapeDtypeStruct(half, F32),
            *(jax.ShapeDtypeStruct(share, F32) for share in shares),
            jax.ShapeDtypeStruct((VEC_ROWS, 128), F32),
        ),
        in_specs=[vmem()] * 8 + [anywhere()] * 2,
        out_specs=(anywhere(),) * 2 + (vmem(),) * 7,
        scratch_shapes=[pltpu.VMEM(*s) for s in scratch]
        + [pltpu.SemaphoreType.DMA((n,)) for n in sems]
        + [pltpu.VMEM(s, BF16) for s in landing_shapes(late_tiles) + landing_shapes(early_tiles)],
        compiler_params=pltpu.CompilerParams(
            collective_id=0, has_side_effects=True, vmem_limit_bytes=64 * 2**20
        ),
    )(*arrays)


def packed_vectors(b_query, b_value, b_up, features):
    dp, low = lax.axis_index("dp"), lax.axis_index("tensor")
    own = jnp.arange(128)[:, None] == low * 64 + dp
    parts = [jnp.where(own, v.astype(F32)[None], 0.0).reshape(-1) for v in (b_query, b_value, b_up)]
    own = (jnp.arange(64)[:, None] == dp) & (low == 0)
    parts += [jnp.where(own, v.astype(F32)[None], 0.0).reshape(-1) for v in features]
    return jnp.concatenate(parts).reshape(VEC_ROWS, 128)


def unpacked_vectors(flat):
    dp, low = lax.axis_index("dp"), lax.axis_index("tensor")
    out, at = [], 0
    for length in (8, 8, 32):
        out.append(lax.dynamic_slice(flat, (at + (low * 64 + dp) * length,), (length,)))
        at += length * 128
    for _ in range(6):
        out.append(lax.dynamic_slice(flat, (at + dp * 16,), (16,)))
        at += 1024
    return out


def on_device(
    tokens, segment, w_query, w_key, w_value, w_out, w_up, w_down, b_query, b_value, b_up,
    b_out, b_down, gain_one, shift_one, gain_two, shift_two, out_grad,
):
    vec = packed_vectors(
        b_query, b_value, b_up, (b_out, b_down, gain_one, shift_one, gain_two, shift_two)
    )
    seg = jnp.broadcast_to(segment.astype(F32)[None], (8, GROUP))
    *outs, totals = layer_call(
        w_query, w_key, w_value, w_out, w_up, w_down, vec, seg, tokens, out_grad
    )
    return (*outs, *unpacked_vectors(totals.reshape(-1)))


def solution(mesh):
    placed = (
        P(("dp", "tensor"), None),
        P("dp"),
        P("dp", "tensor"),
        P("dp", "tensor"),
        P("dp", "tensor"),
        P("dp", "tensor"),
        P("dp", "tensor"),
        P("dp", "tensor"),
        P(("tensor", "dp")),
        P(("tensor", "dp")),
        P(("tensor", "dp")),
        P("dp"),
        P("dp"),
        P("dp"),
        P("dp"),
        P("dp"),
        P("dp"),
        P(("dp", "tensor"), None),
    )
    return jax.shard_map(
        on_device,
        mesh=mesh,
        in_specs=placed,
        out_specs=(
            P(("dp", "tensor"), None),
            P(("dp", "tensor"), None),
            P("dp", "tensor"),
            P("dp", "tensor"),
            P("dp", "tensor"),
            P("dp", "tensor"),
            P("dp", "tensor"),
            P("dp", "tensor"),
            P(("tensor", "dp")),
            P(("tensor", "dp")),
            P(("tensor", "dp")),
            P("dp"),
            P("dp"),
            P("dp"),
            P("dp"),
            P("dp"),
            P("dp"),
        ),
        check_vma=False,
    )
```

```python
import jax
import jax.numpy as jnp
from jax import lax
from jax.experimental import pallas as pl
from jax.experimental.pallas import tpu as pltpu
from jax.sharding import PartitionSpec as P

MESH = pl.DeviceIdType.MESH
F32 = jnp.float32
BF16 = jnp.bfloat16

TILES = 24
COLS = 256
PHASES, ROUTES, STEPS = 4, 3, 6
VEC_ROWS = 96
ORDERS = ((2, 0, 1), (1, 2, 0), (0, 1, 2))


def position():
    dp, low = lax.axis_index("dp"), lax.axis_index("tensor")
    return (dp // 16, lax.rem(dp // 4, 4), lax.rem(dp // 2, 2) * 2 + low), lax.rem(dp, 2)


def device(chip, core):
    y, x, z = chip
    return (y * 16 + x * 4 + (z // 2) * 2 + core, lax.rem(z, 2))


def moved(chip, axis, by):
    return tuple(lax.rem(c + by, 4) if k == axis else c for k, c in enumerate(chip))


def opposite_z(chip):
    y, x, z = chip
    return (y, x, z + 1 - 2 * lax.rem(z, 2))


def blocks(chip, full):
    return tuple(pl.ds(0, 4) if axis in full else pl.ds(c, 1) for axis, c in enumerate(chip))


def block_shape(full):
    return tuple(4 if axis in full else 1 for axis in range(3))


def first_tile(phase, route):
    return phase * 6 + route * 2


class Ring:
    def __init__(self, sems):
        self.send, self.recv = sems
        self.chip, self.core = position()

    def copy(self, phase, route, step, way, axis, src, dst):
        sem = ((phase * ROUTES + route) * STEPS + step) * 2 + way
        target = device(moved(self.chip, axis, 1 if way == 0 else 3), self.core)
        return pltpu.make_async_remote_copy(
            src_ref=src, dst_ref=dst, send_sem=self.send.at[sem], recv_sem=self.recv.at[sem],
            device_id=target, device_id_type=MESH,
        )

    def start(self, phase, route, step):
        for c in self.copies(phase, route, step):
            c.start()

    def wait_recv(self, phase, route, step):
        for c in self.copies(phase, route, step):
            c.wait_recv()

    def wait_send(self, phase, route, step):
        for c in self.copies(phase, route, step):
            c.wait_send()


class Gather(Ring):
    def __init__(self, w, sems):
        super().__init__(sems)
        self.w = w

    def copies(self, phase, route, step):
        order = ORDERS[route]
        axis, full = order[step // 2], order[: step // 2]
        tile = first_tile(phase, route)
        out = []
        for way in range(2):
            if step % 2 == 0:
                part = self.w.at[(pl.ds(tile, 2),) + blocks(self.chip, full)]
            else:
                behind = moved(self.chip, axis, 3 if way == 0 else 1)
                part = self.w.at[(pl.ds(tile + way, 1),) + blocks(behind, full)]
            out.append(self.copy(phase, route, step, way, axis, part, part))
        return out

    def step(self, phase, step):
        for route in range(ROUTES):
            if step:
                self.wait_recv(phase, route, step - 1)
            if step < STEPS:
                self.start(phase, route, step)


def landing_shapes():
    shapes = []
    for _ in range(PHASES):
        for order in ORDERS:
            for k in range(3):
                shapes.append((6,) + block_shape(order[: 2 - k]) + (16, COLS))
    return shapes


class Scatter(Ring):
    def __init__(self, g, landings, sems):
        super().__init__(sems)
        self.g, self.landings = g, landings

    def at(self, route, step):
        order = ORDERS[route]
        return order[2 - step // 2], order[: 2 - step // 2]

    def landing(self, phase, route, step):
        return self.landings[(phase * ROUTES + route) * 3 + step // 2]

    def copies(self, phase, route, step):
        axis, full = self.at(route, step)
        tile = first_tile(phase, route)
        landed = self.landing(phase, route, step)
        out = []
        for way in range(2):
            if step % 2 == 0:
                src = self.g.at[(pl.ds(tile + way, 1),) + blocks(moved(self.chip, axis, 2), full)]
                dst = landed.at[pl.ds(way, 1)]
            else:
                ahead = moved(self.chip, axis, 1 if way == 0 else 3)
                src = self.g.at[(pl.ds(tile, 2),) + blocks(ahead, full)]
                dst = landed.at[pl.ds(2 + 2 * way, 2)]
            out.append(self.copy(phase, route, step, way, axis, src, dst))
        return out

    def take(self, phase, route, step):
        self.wait_recv(phase, route, step)
        axis, full = self.at(route, step)
        tile = first_tile(phase, route)
        landed = self.landing(phase, route, step)
        ny, nx, nz = block_shape(full)

        def start_of(chip):
            return tuple(0 if k in full else c for k, c in enumerate(chip))

        def add(t, base, parts):
            y0, x0, z0 = base

            def one(i, carry):
                at = (tile + t, y0 + i, pl.ds(x0, nx), pl.ds(z0, nz))
                total = self.g[at].astype(F32)
                for part in parts:
                    total += landed[part, i].astype(F32)
                self.g[at] = total.astype(BF16)
                return carry

            lax.fori_loop(0, ny, one, 0)

        for t in range(2):
            if step % 2 == 0:
                add(t, start_of(moved(self.chip, axis, 1 if t == 0 else 3)), (t,))
            else:
                add(t, start_of(self.chip), (2 + t, 4 + t))

    def step(self, phase, step):
        for route in range(ROUTES):
            if step:
                self.take(phase, route, step - 1)
            if step < STEPS:
                self.start(phase, route, step)


def greet(others):
    barrier = pltpu.get_barrier_semaphore()
    for other in others:
        pl.semaphore_signal(barrier, inc=1, device_id=other, device_id_type=MESH)
    pl.semaphore_wait(barrier, len(others))


def sibling():
    chip, core = position()
    return device(chip, 1 - core)


def vector_partner(stage):
    chip, core = position()
    if stage == 0:
        return device(chip, 1 - core)
    axis = (stage - 1) // 2
    c = chip[axis]
    new = c + 1 - 2 * lax.rem(c, 2) if stage % 2 else 3 - c
    return device(tuple(new if k == axis else v for k, v in enumerate(chip)), core)


class VectorSum:
    def __init__(self, kept, came, sems, base):
        self.kept, self.came, (self.send, self.recv), self.base = kept, came, sems, base

    def copy(self, stage):
        return pltpu.make_async_remote_copy(
            src_ref=self.kept.at[stage],
            dst_ref=self.came.at[stage],
            send_sem=self.send.at[self.base + stage],
            recv_sem=self.recv.at[self.base + stage],
            device_id=vector_partner(stage),
            device_id_type=MESH,
        )

    def step(self, stage):
        if stage:
            self.copy(stage - 1).wait_recv()
            self.kept[stage] = self.kept[stage - 1] + self.came[stage - 1]
        if stage < 7:
            self.copy(stage).start()

    def wait_send(self, stage):
        self.copy(stage).wait_send()


GROUP = 512
HALF = 256
WIDTH = 1024
HEAD_DIM = 64
PAIR = 2 * HEAD_DIM
SCALE = HEAD_DIM**-0.5
EPSILON = 1e-12
NN = (((1,), (0,)), ((), ()))
NT = (((1,), (1,)), ((), ()))
TN = (((0,), (0,)), ((), ()))
Q_TILE, OUT_TILE, UP_TILE, DOWN_TILE = 0, 6, 8, 16
WEIGHT_TILES = (2, 2, 2, 2, 8, 8)


def dot(a, b, dims=NN):
    return lax.dot_general(a, b, dims, preferred_element_type=F32)


def loop(count, body):
    def step(i, carry):
        body(i)
        return carry

    lax.fori_loop(0, count, step, 0)


VECTORS = (8, 8, 32, 16, 16, 16, 16, 16, 16)
VECTOR_ROWS = (0, 8, 16, 48, 56, 64, 72, 80, 88)


def layer_kernel(
    w_q, w_k, w_v, w_o, w_u, w_d,
    v_0, v_1, v_2, v_3, v_4, v_5, v_6, v_7, v_8, segment, tokens, out_grad,
    layer_out, input_grad, shares, vec_out,
    w, g, x, n1, gd, tr, qkv, probs, bias, ctx, gctx, ds, part, leave, come,
    hat, inv, d_two, cot, act, slope, seg_here, seg_own, segments, segcol, features, biases, bias_sums, sums, out_rows,
    r_0, r_1, r_2, r_3, r_4, r_5, r_6, r_7, r_8, placed,
    kept, came, kept_front, came_front, kept_tail, came_tail,
    gsend, grecv, ssend, srecv, vsend, vrecv, swap_send, swap_recv, sib_send, sib_recv, load_sem,
    *landings,
):
    chip, core = position()
    y, x_at, z = chip
    low = lax.rem(z, 2)
    opposite_chip = opposite_z(chip)
    diagonal = device(opposite_chip, 1 - core)
    twin = sibling()
    stays = core == low
    own_rows = pl.ds(pl.multiple_of(core * HALF, HALF), HALF)
    other_rows = pl.ds(pl.multiple_of((1 - core) * HALF, HALF), HALF)

    raw = (r_0, r_1, r_2, r_3, r_4, r_5, r_6, r_7, r_8)
    loads = [
        pltpu.make_async_copy(src, dst, load_sem.at[n])
        for n, (src, dst) in enumerate(zip((v_0, v_1, v_2, v_3, v_4, v_5, v_6, v_7, v_8), raw))
    ]
    loads.append(pltpu.make_async_copy(segment, seg_here.at[0], load_sem.at[9]))
    loads.append(pltpu.make_async_copy(out_grad, d_two, load_sem.at[10]))
    for load in loads:
        load.start()

    def swap_copies(n, src, dst_here, dst_there):
        away = pltpu.make_async_remote_copy(
            src_ref=src, dst_ref=dst_there, send_sem=swap_send.at[n], recv_sem=swap_recv.at[n],
            device_id=diagonal, device_id_type=MESH,
        )
        return away, pltpu.make_async_copy(src, dst_here, swap_recv.at[n])

    def swap_start(n, src, dst_here, dst_there):
        away, here = swap_copies(n, src, dst_here, dst_there)
        pl.when(stays)(here.start)
        pl.when(jnp.logical_not(stays))(away.start)

    def swap_wait(n, src, dst_here, dst_there):
        away, here = swap_copies(n, src, dst_here, dst_there)
        pl.when(stays)(here.wait)
        pl.when(jnp.logical_not(stays))(away.wait)

    def to_twin(n, src, dst):
        return pltpu.make_async_remote_copy(
            src_ref=src, dst_ref=dst, send_sem=sib_send.at[n], recv_sem=sib_recv.at[n],
            device_id=twin, device_id_type=MESH,
        )

    greet([device(moved(chip, axis, by), core) for axis in range(3) for by in (1, 3)] + [twin, diagonal])

    weight_moves = []
    tile = 0
    for ref, count in zip((w_q, w_k, w_v, w_o, w_u, w_d), WEIGHT_TILES):
        for k in range(count):
            weight_moves.append(
                (
                    tile,
                    ref.at[:, pl.ds(k * COLS, COLS)],
                    w.at[tile, y, x_at, z],
                    w.at[(tile,) + opposite_chip],
                )
            )
            tile += 1
    for move in weight_moves[:6]:
        swap_start(*move)
    row_move = (TILES, tokens, x.at[own_rows], x.at[other_rows])
    swap_start(*row_move)
    for move in weight_moves[6:]:
        swap_start(*move)

    gather = Gather(w, (gsend, grecv))
    vectors = VectorSum(kept, came, (vsend, vrecv), 0)

    def arrived(phase):
        for move in weight_moves[6 * phase : 6 * phase + 6]:
            swap_wait(*move)

    arrived(0)
    gather.step(0, 0)

    for load in loads:
        load.wait()
    dp, tensor = lax.axis_index("dp"), lax.axis_index("tensor")
    placed[...] = jnp.zeros((VEC_ROWS, 128), F32)
    for n, (ref, length, row) in enumerate(zip(raw, VECTORS, VECTOR_ROWS)):
        at = (tensor * 64 + dp if n < 3 else dp) * length
        value = ref[...].astype(F32).reshape(1, length)
        value = jnp.concatenate([value, jnp.zeros((1, 128 - length), F32)], axis=1)
        value = pltpu.roll(jnp.broadcast_to(value, (8, 128)), lax.rem(at, 128), 1)
        if n >= 3:
            value = jnp.where(tensor == 0, value, 0.0)
        placed[pl.ds(row + at // 128, 1), :] = value[0:1]
    kept[0] = placed[...].astype(BF16)
    vectors.step(0)
    seg_own[...] = jnp.broadcast_to(seg_here[...].astype(F32), (8, GROUP))
    seg_move = (TILES + 1, seg_own, segments, segments)
    swap_start(*seg_move)

    gather.step(0, 1)
    vectors.step(1)
    arrived(1)
    gather.step(1, 0)
    swap_wait(*row_move)
    rows_copy = to_twin(0, x.at[own_rows], x.at[own_rows])
    rows_copy.start()
    gather.step(0, 2)
    vectors.step(2)
    gather.step(1, 1)
    arrived(2)
    gather.step(2, 0)
    gather.step(0, 3)
    vectors.step(3)
    gather.step(1, 2)
    gather.step(2, 1)
    arrived(3)
    gather.step(0, 4)
    vectors.step(4)
    gather.step(1, 3)
    gather.step(2, 2)
    gather.step(3, 0)
    vectors.step(5)

    swap_wait(*seg_move)
    across_lanes = jnp.broadcast_to(segments[0:1, :], (128, GROUP))
    segcol[...] = across_lanes.T
    for k in range(4):
        cols = slice(k * 128, k * 128 + 128)
        bias[:, cols] = jnp.where(segcol[...] == segments[0:1, cols], 0.0, -1000000000.0)
    vectors.step(6)
    gather.step(0, 5)
    gather.step(1, 4)
    gather.step(2, 3)
    gather.step(3, 1)
    vectors.step(7)
    placed[...] = kept[7].astype(F32)
    for n in range(6):
        for k in range(8):
            features[n, :, k * 128 : k * 128 + 128] = placed[48 + n * 8 + k : 49 + n * 8 + k, :]
    for k in range(2):
        for half in range(2):
            lanes = slice(half * 128, half * 128 + 128)
            biases[k, :, lanes] = placed[pl.ds(core * 4 + k * 2 + half, 1), :]
            biases[4 + k, :, lanes] = placed[pl.ds(8 + core * 4 + k * 2 + half, 1), :]
        biases[2 + k] = jnp.zeros((1, COLS), F32)
    for k in range(8):
        for half in range(2):
            lanes = slice(half * 128, half * 128 + 128)
            biases[6 + k, :, lanes] = placed[pl.ds(16 + core * 16 + k * 2 + half, 1), :]
    rows_copy.wait_recv()
    out_rows[...] = d_two[...].astype(BF16)
    gather.step(0, 6)

    def weight(tile):
        return w[tile].reshape(WIDTH, COLS)

    def project(t):
        made = (dot(x[...], weight(t)) + biases[t]).astype(BF16)
        qkv[2 * t] = made[:, :128]
        qkv[2 * t + 1] = made[:, 128:]

    loop(6, project)
    gather.step(2, 4)
    gather.step(3, 2)
    low_lanes = lax.broadcasted_iota(jnp.int32, (1, PAIR), 1) < HEAD_DIM

    def only(head, values):
        keep = low_lanes if head == 0 else jnp.logical_not(low_lanes)
        return jnp.where(keep, values, jnp.zeros_like(values))

    def attend(pair):
        for half in range(2):
            rows = slice(half * HALF, half * HALF + HALF)
            query = qkv[pair, rows]
            outs = []
            for head in range(2):
                scores = dot(qkv[4 + pair], only(head, query), NT) * SCALE + bias[:, rows]
                scores = jnp.exp(scores - jnp.max(scores, axis=0, keepdims=True))
                weights = scores * (1.0 / jnp.sum(scores, axis=0, keepdims=True))
                weights = weights.astype(BF16)
                probs[2 * pair + head, :, rows] = weights
                outs.append(dot(weights, qkv[8 + pair], TN))
            ctx[pair, rows] = jnp.where(low_lanes, outs[0], outs[1]).astype(BF16)

    attend(0)
    gather.step(1, 5)
    gather.step(2, 5)
    gather.step(3, 3)
    attend(1)
    gather.step(3, 4)
    attend(2)
    cot_move = (TILES + 2, out_rows, cot, cot)
    swap_start(*cot_move)
    attend(3)
    gather.step(1, 6)
    gather.step(3, 5)

    terms_sent = []

    def row_terms(n, tiles, left):
        def block(rows, store):
            def one(k):
                lanes = pl.ds(pl.multiple_of(k * COLS, COLS), COLS)
                total = None
                for t, at in enumerate(tiles):
                    term = dot(left(t, rows), w[at, k].reshape(COLS, COLS), NT)
                    total = term if total is None else total + term
                store(lanes, total)

            loop(4, one)

        if n:
            terms_sent[-1].wait_send()

        def leaves(lanes, total):
            leave[:, lanes] = total.astype(BF16)

        def stays_here(lanes, total):
            part[:, lanes] = total

        block(other_rows, leaves)
        copy = to_twin(1 + n, leave, come)
        copy.start()
        block(own_rows, stays_here)
        copy.wait_recv()
        terms_sent.append(copy)

    def side_by_side(ref, first, rows=slice(None)):
        return jnp.concatenate([ref[first, rows], ref[first + 1, rows]], axis=1)

    sent = [rows_copy]
    row_terms(0, range(OUT_TILE, UP_TILE), lambda t, rows: side_by_side(ctx, 2 * t, rows))
    chunk = 64

    def by_chunks(body):
        def one(i):
            at = pl.multiple_of(i * chunk, chunk)
            body(pl.ds(at, chunk), pl.ds(pl.multiple_of(core * HALF + at, chunk), chunk))

        loop(HALF // chunk, one)

    def mean(values):
        return jnp.mean(values, axis=-1, keepdims=True)

    def normalized(hidden):
        centered = hidden - mean(hidden)
        scale = lax.rsqrt(mean(centered * centered) + EPSILON)
        return centered * scale, scale

    for n in range(6):
        sums[n] = jnp.zeros((1, WIDTH), F32)

    def add_sum(n, values):
        sums[n] += jnp.sum(values, axis=0, keepdims=True)

    b_out, b_down, gain_one, shift_one, gain_two, shift_two = range(6)

    def first_norm(here, there):
        hidden = x[there].astype(F32) + part[here] + come[here].astype(F32) + features[b_out]
        value, scale = normalized(hidden)
        hat[here] = value
        inv[here] = jnp.broadcast_to(scale, (chunk, 128))
        n1[there] = (value * features[gain_one] + features[shift_one]).astype(BF16)

    by_chunks(first_norm)

    shared = {}

    def share_rows(n, ref):
        copy = to_twin(n, ref.at[own_rows], ref.at[own_rows])
        copy.start()
        shared[n] = copy
        copy.wait_recv()

    share_rows(5, n1)

    def up(t):
        for half in range(2):
            rows = slice(half * HALF, half * HALF + HALF)
            pre = dot(n1[rows], weight(UP_TILE + t)) + biases[6 + t]
            below = 0.5 * (1.0 + lax.erf(pre * (0.5**0.5)))
            act[t, rows] = (pre * below).astype(BF16)
            bell = jnp.exp(pre * pre * -0.5) * 0.3989422804014327
            slope[t, rows] = (below + pre * bell).astype(BF16)

    loop(4, up)
    gather.step(2, 6)
    loop(4, lambda t: up(t + 4))
    gather.step(3, 6)
    row_terms(1, range(DOWN_TILE, TILES), lambda t, rows: act[t, rows])
    swap_wait(*cot_move)

    def norm_back(values, incoming, gain, scale, gain_at, shift_at):
        add_sum(shift_at, incoming)
        add_sum(gain_at, incoming * values)
        scaled = incoming * gain
        return scale * (scaled - mean(scaled) - values * mean(scaled * values))

    def second_norm(here, there):
        first = hat[here] * features[gain_one] + features[shift_one]
        value, scale = normalized(first + part[here] + come[here].astype(F32) + features[b_down])
        live = jnp.where(segcol[there, 0:1] >= 0, 1.0, 0.0)
        out_rows[here] = ((value * features[gain_two] + features[shift_two]) * live).astype(BF16)
        back = norm_back(
            value, cot[here].astype(F32) * live, features[gain_two], scale, gain_two, shift_two
        )
        add_sum(b_down, back)
        d_two[here] = back
        gd[there] = back.astype(BF16)

    by_chunks(second_norm)
    out_move = (TILES + 3, out_rows, layer_out, layer_out)
    swap_start(*out_move)
    share_rows(6, gd)

    def turn(ref):
        for k in range(4):
            rows = slice(k * COLS, k * COLS + COLS)
            tr[rows, :] = ref[:, rows].T

    def store_grad(tile, right):
        for k in range(4):
            made = dot(tr[k * COLS : k * COLS + COLS, :], right)
            g[tile, k] = made.astype(BF16).reshape(4, 4, 16, COLS)

    scatter = Scatter(g, landings, (ssend, srecv))
    share_moves = []

    def reduced(phase):
        scatter.step(phase, 6)
        tiles = pl.ds(6 * phase, 6)
        share_moves.append(
            (TILES + 5 + phase, g.at[tiles, y, x_at, z], shares.at[tiles], shares.at[tiles])
        )
        swap_start(*share_moves[-1])

    turn(gd)
    loop(8, lambda t: store_grad(DOWN_TILE + t, act[t]))
    scatter.step(3, 0)

    def up_back(t):
        made = (dot(gd[...], weight(DOWN_TILE + t)) * slope[t].astype(F32)).astype(BF16)
        slope[t] = made
        bias_sums[6 + t] = jnp.sum(made.astype(F32), axis=0, keepdims=True)

    loop(8, up_back)
    scatter.step(3, 1)
    turn(n1)
    loop(4, lambda t: store_grad(UP_TILE + 4 + t, slope[4 + t]))
    scatter.step(2, 0)
    loop(4, lambda t: store_grad(UP_TILE + t, slope[t]))
    scatter.step(3, 2)
    row_terms(2, range(UP_TILE, DOWN_TILE), lambda t, rows: slope[t, rows])

    def first_norm_back(here, there):
        incoming = d_two[here] + part[here] + come[here].astype(F32)
        back = norm_back(
            hat[here], incoming, features[gain_one], inv[here, 0:1], gain_one, shift_one
        )
        add_sum(b_out, back)
        d_two[here] = back
        n1[there] = back.astype(BF16)

    shared.pop(5).wait_send()
    d1 = n1
    scatter.step(2, 1)
    by_chunks(first_norm_back)
    share_rows(7, d1)
    turn(d1)
    loop(2, lambda u: store_grad(OUT_TILE + u, side_by_side(ctx, 2 * u)))
    scatter.step(1, 0)
    scatter.step(2, 2)
    scatter.step(3, 3)

    kept_front[0] = jnp.zeros((VEC_ROWS - 16, 128), F32)
    for k in range(8):
        for half in range(2):
            lanes = slice(half * 128, half * 128 + 128)
            kept_front[0, pl.ds(core * 16 + k * 2 + half, 1), :] = bias_sums[6 + k, :, lanes]
    for n in range(6):
        for k in range(8):
            at = 32 + n * 8 + k
            kept_front[0, at : at + 1, :] = sums[n, :, k * 128 : k * 128 + 128]
    front = VectorSum(kept_front, came_front, (vsend, vrecv), 7)
    front.step(0)

    def context_back(u):
        made = dot(d1[...], weight(OUT_TILE + u)).astype(BF16)
        gctx[2 * u] = made[:, :128]
        gctx[2 * u + 1] = made[:, 128:]

    loop(2, context_back)
    scatter.step(1, 1)
    scatter.step(3, 4)
    front.step(1)

    def attend_back(pair):
        for half in range(2):
            rows = slice(half * HALF, half * HALF + HALF)
            for head in range(2):
                weights = probs[2 * pair + head, :, rows].astype(F32)
                grad = dot(qkv[8 + pair], only(head, gctx[pair, rows]), NT)
                total = jnp.sum(grad * weights, axis=0, keepdims=True)
                ds[head, :, rows] = (weights * (grad - total)).astype(BF16)
        query = [dot(ds[head], qkv[4 + pair], TN) for head in range(2)]
        key = [dot(ds[head], qkv[pair]) for head in range(2)]
        value = [dot(probs[2 * pair + head], gctx[pair]) for head in range(2)]
        for at, (a, b), scale in ((0, query, SCALE), (4, key, SCALE), (8, value, 1.0)):
            made = (jnp.where(low_lanes, a, b) * scale).astype(BF16)
            qkv[at + pair] = made
            bias_sums[14 + at + pair, :, :PAIR] = jnp.sum(made.astype(F32), axis=0, keepdims=True)

    attend_back(0)
    scatter.step(2, 3)
    scatter.step(1, 2)
    scatter.step(3, 5)
    front.step(2)
    attend_back(1)
    scatter.step(2, 4)
    scatter.step(1, 3)
    reduced(3)
    front.step(3)
    attend_back(2)
    scatter.step(2, 5)
    scatter.step(1, 4)
    front.step(4)
    attend_back(3)
    kept_tail[0] = jnp.zeros((16, 128), F32)
    for k in range(4):
        kept_tail[0, pl.ds(core * 4 + k, 1), :] = bias_sums[14 + k, :, :PAIR]
        kept_tail[0, pl.ds(8 + core * 4 + k, 1), :] = bias_sums[22 + k, :, :PAIR]
    tail = VectorSum(kept_tail, came_tail, (vsend, vrecv), 14)
    tail.step(0)
    turn(x)
    loop(6, lambda t: store_grad(t, side_by_side(qkv, 2 * t)))
    scatter.step(0, 0)
    scatter.step(1, 5)
    reduced(2)
    tail.step(1)
    front.step(5)
    row_terms(3, range(6), lambda t, rows: side_by_side(qkv, 2 * t, rows))
    scatter.step(0, 1)
    tail.step(2)
    front.step(6)

    def last_rows(here, there):
        cot[here] = (d_two[here] + part[here] + come[here].astype(F32)).astype(BF16)

    by_chunks(last_rows)
    grad_move = (TILES + 4, cot, input_grad, input_grad)
    swap_start(*grad_move)
    scatter.step(0, 2)
    tail.step(3)
    front.step(7)
    reduced(1)
    scatter.step(0, 3)
    tail.step(4)
    scatter.step(0, 4)
    tail.step(5)
    scatter.step(0, 5)
    tail.step(6)
    reduced(0)
    tail.step(7)
    vec_out[0:16] = kept_tail[7]
    vec_out[16:] = kept_front[7]

    for move in [out_move, grad_move] + share_moves:
        swap_wait(*move)
    for copy in sent + terms_sent[-1:] + list(shared.values()):
        copy.wait_send()
    for phase in range(PHASES):
        for route in range(ROUTES):
            for step in range(STEPS):
                gather.wait_send(phase, route, step)
                scatter.wait_send(phase, route, step)
    for stage in range(7):
        vectors.wait_send(stage)
        front.wait_send(stage)
        tail.wait_send(stage)


def layer_call(*arrays):
    full = (TILES, 4, 4, 4, 16, COLS)
    rows = (GROUP, WIDTH)
    half = (HALF, WIDTH)
    front = VEC_ROWS - 16
    scratch = [
        (full, BF16), (full, BF16),
        (rows, BF16), (rows, BF16), (rows, BF16), ((WIDTH, GROUP), BF16),
        ((12, GROUP, PAIR), BF16), ((8, GROUP, GROUP), BF16), ((GROUP, GROUP), F32),
        ((4, GROUP, PAIR), BF16), ((4, GROUP, PAIR), BF16), ((2, GROUP, GROUP), BF16),
        (half, F32), (half, BF16), (half, BF16),
        (half, F32), ((HALF, 128), F32), (half, F32), (half, BF16),
        ((8, GROUP, COLS), BF16), ((8, GROUP, COLS), BF16),
        ((1, GROUP), jnp.int32), ((8, GROUP), F32), ((8, GROUP), F32), ((GROUP, 128), F32),
        ((6, 1, WIDTH), F32), ((14, 1, COLS), F32), ((26, 1, COLS), F32), ((6, 1, WIDTH), F32),
        (half, BF16),
    ] + [((length,), BF16) for length in VECTORS] + [
        ((VEC_ROWS, 128), F32),
        ((8, VEC_ROWS, 128), BF16), ((7, VEC_ROWS, 128), BF16),
        ((8, front, 128), F32), ((7, front, 128), F32),
        ((8, 16, 128), F32), ((7, 16, 128), F32),
    ]
    sems = [PHASES * ROUTES * STEPS * 2] * 4 + [21] * 2 + [TILES + 9] * 2 + [8] * 2 + [11]
    return pl.pallas_call(
        layer_kernel,
        out_shape=(
            jax.ShapeDtypeStruct(half, BF16),
            jax.ShapeDtypeStruct(half, BF16),
            jax.ShapeDtypeStruct((TILES, 16, COLS), BF16),
            jax.ShapeDtypeStruct((VEC_ROWS, 128), F32),
        ),
        in_specs=[pl.BlockSpec(memory_space=pl.ANY)] * len(arrays),
        out_specs=(pl.BlockSpec(memory_space=pl.ANY),) * 3 + (pl.BlockSpec(memory_space=pltpu.VMEM),),
        scratch_shapes=[pltpu.VMEM(*s) for s in scratch]
        + [pltpu.SemaphoreType.DMA((n,)) for n in sems]
        + [pltpu.VMEM(s, BF16) for s in landing_shapes()],
        compiler_params=pltpu.CompilerParams(
            collective_id=0, has_side_effects=True, vmem_limit_bytes=64 * 2**20
        ),
    )(*arrays)


def unpacked_vectors(flat):
    dp, low = lax.axis_index("dp"), lax.axis_index("tensor")
    out, at = [], 0
    for length in (8, 8, 32):
        out.append(lax.dynamic_slice(flat, (at + (low * 64 + dp) * length,), (length,)))
        at += length * 128
    for _ in range(6):
        out.append(lax.dynamic_slice(flat, (at + dp * 16,), (16,)))
        at += 1024
    return out


def on_device(
    tokens, segment, w_query, w_key, w_value, w_out, w_up, w_down, b_query, b_value, b_up,
    b_out, b_down, gain_one, shift_one, gain_two, shift_two, out_grad,
):
    layer_out, input_grad, shares, totals = layer_call(
        w_query, w_key, w_value, w_out, w_up, w_down, b_query, b_value, b_up,
        b_out, b_down, gain_one, shift_one, gain_two, shift_two, segment, tokens, out_grad,
    )
    shares = shares.astype(F32).transpose(1, 0, 2).reshape(16, TILES * COLS)
    ends = [sum(WEIGHT_TILES[:k]) * COLS for k in range(1, 6)]
    return (
        layer_out,
        input_grad.astype(F32),
        *jnp.split(shares, ends, axis=1),
        *unpacked_vectors(totals.reshape(-1)),
    )


def solution(mesh):
    placed = (
        P(("dp", "tensor"), None),
        P("dp"),
        P("dp", "tensor"),
        P("dp", "tensor"),
        P("dp", "tensor"),
        P("dp", "tensor"),
        P("dp", "tensor"),
        P("dp", "tensor"),
        P(("tensor", "dp")),
        P(("tensor", "dp")),
        P(("tensor", "dp")),
        P("dp"),
        P("dp"),
        P("dp"),
        P("dp"),
        P("dp"),
        P("dp"),
        P(("dp", "tensor"), None),
    )
    return jax.shard_map(
        on_device,
        mesh=mesh,
        in_specs=placed,
        out_specs=(
            P(("dp", "tensor"), None),
            P(("dp", "tensor"), None),
            P("dp", "tensor"),
            P("dp", "tensor"),
            P("dp", "tensor"),
            P("dp", "tensor"),
            P("dp", "tensor"),
            P("dp", "tensor"),
            P(("tensor", "dp")),
            P(("tensor", "dp")),
            P(("tensor", "dp")),
            P("dp"),
            P("dp"),
            P("dp"),
            P("dp"),
            P("dp"),
            P("dp"),
        ),
        check_vma=False,
    )
```

```python
import jax
import jax.numpy as jnp
from jax import lax
from jax.experimental import pallas as pl
from jax.experimental.pallas import tpu as pltpu
from jax.sharding import PartitionSpec as P

MESH = pl.DeviceIdType.MESH
F32 = jnp.float32
BF16 = jnp.bfloat16

TILES = 24
COLS = 256
PHASES, ROUTES, STEPS = 4, 3, 4
VEC_ROWS = 96
ORDERS = ((2, 0, 1), (1, 2, 0), (0, 1, 2))
PARTNERS = (1, 3, 2)


def position():
    dp, low = lax.axis_index("dp"), lax.axis_index("tensor")
    return (dp // 16, lax.rem(dp // 4, 4), lax.rem(dp // 2, 2) * 2 + low), lax.rem(dp, 2)


def device(chip, core):
    y, x, z = chip
    return (y * 16 + x * 4 + (z // 2) * 2 + core, lax.rem(z, 2))


def moved(chip, axis, by):
    return tuple(lax.rem(c + by, 4) if k == axis else c for k, c in enumerate(chip))


def opposite_z(chip):
    y, x, z = chip
    return (y, x, z + 1 - 2 * lax.rem(z, 2))


def blocks(chip, full):
    return tuple(pl.ds(0, 4) if axis in full else pl.ds(c, 1) for axis, c in enumerate(chip))


def block_shape(full):
    return tuple(4 if axis in full else 1 for axis in range(3))


def first_tile(phase, route):
    return phase * 6 + route * 2


class Ring:
    def __init__(self, buffer, sems, sizes):
        self.buffer, (self.send, self.recv), self.sizes = buffer, sems, sizes
        self.chip, self.core = position()

    def copy(self, phase, step, target, src, dst):
        sem = phase * STEPS + step
        return pltpu.make_async_remote_copy(
            src_ref=src, dst_ref=dst, send_sem=self.send.at[sem], recv_sem=self.recv.at[sem],
            device_id=target, device_id_type=MESH,
        )

    def partner(self, axis, way):
        return device(moved(self.chip, axis, PARTNERS[way]), self.core)

    def start(self, phase, step):
        for route in range(ROUTES):
            for c in self.copies(phase, route, step):
                c.start()

    def all_of(self, phase, step):
        tiles, ny, nx, nz = self.sizes[step]
        whole = self.buffer.at[pl.ds(0, tiles), pl.ds(0, ny), pl.ds(0, nx), pl.ds(0, nz)]
        return self.copy(phase, step, self.partner(0, 0), whole, whole)

    def wait_recv(self, phase, step):
        self.all_of(phase, step).wait_recv()

    def wait_send(self, phase, step):
        self.all_of(phase, step).wait_send()


class Gather(Ring):
    def __init__(self, w, sems):
        super().__init__(w, sems, ((18, 1, 1, 1), (18, 1, 1, 4), (12, 1, 4, 4), (6, 1, 4, 4)))

    def copies(self, phase, route, step):
        order, k = ORDERS[route], min(step, 2)
        axis, full = order[k], order[:k]
        tile = first_tile(phase, route)
        out = []
        for way in range(3 if step < 2 else 2):
            if step < 3:
                part = self.buffer.at[(pl.ds(tile, 2),) + blocks(self.chip, full)]
            else:
                behind = moved(self.chip, axis, PARTNERS[1 - way])
                part = self.buffer.at[(pl.ds(tile + way, 1),) + blocks(behind, full)]
            out.append(self.copy(phase, step, self.partner(axis, way), part, part))
        return out

    def step(self, phase, step):
        if step:
            self.wait_recv(phase, step - 1)
        if step < STEPS:
            self.start(phase, step)


def landing_shapes():
    shapes = []
    for _ in range(PHASES):
        for order in ORDERS:
            for k in range(3):
                shapes.append((6,) + block_shape(order[: 2 - k]) + (16, COLS))
    return shapes


class Scatter(Ring):
    def __init__(self, g, landings, sems):
        super().__init__(g, sems, ((6, 1, 4, 4), (12, 1, 4, 4), (18, 1, 1, 4), (18, 1, 1, 1)))
        self.g, self.landings = g, landings

    def at(self, route, step):
        order, k = ORDERS[route], max(step - 1, 0)
        return order[2 - k], order[: 2 - k]

    def landing(self, phase, route, step):
        return self.landings[(phase * ROUTES + route) * 3 + max(step - 1, 0)]

    def copies(self, phase, route, step):
        axis, full = self.at(route, step)
        tile = first_tile(phase, route)
        landed = self.landing(phase, route, step)
        out = []
        for way in range(2 if step < 2 else 3):
            if step == 0:
                src = self.g.at[(pl.ds(tile + way, 1),) + blocks(moved(self.chip, axis, 2), full)]
                dst = landed.at[pl.ds(way, 1)]
            else:
                ahead = moved(self.chip, axis, PARTNERS[way])
                src = self.g.at[(pl.ds(tile, 2),) + blocks(ahead, full)]
                dst = landed.at[pl.ds(2 * way + (2 if step == 1 else 0), 2)]
            out.append(self.copy(phase, step, self.partner(axis, way), src, dst))
        return out

    def take(self, phase, route, step):
        axis, full = self.at(route, step)
        tile = first_tile(phase, route)
        landed = self.landing(phase, route, step)
        ny, nx, nz = block_shape(full)

        def start_of(chip):
            return tuple(0 if k in full else c for k, c in enumerate(chip))

        def add(t, base, parts):
            y0, x0, z0 = base

            def one(i, carry):
                at = (tile + t, y0 + i, pl.ds(x0, nx), pl.ds(z0, nz))
                total = self.g[at].astype(F32)
                for part in parts:
                    total += landed[part, i].astype(F32)
                self.g[at] = total.astype(BF16)
                return carry

            lax.fori_loop(0, ny, one, 0)

        for t in range(2):
            if step == 0:
                add(t, start_of(moved(self.chip, axis, PARTNERS[t])), (t,))
            else:
                add(t, start_of(self.chip), (2 + t, 4 + t) if step == 1 else (t, 2 + t, 4 + t))

    def step(self, phase, step):
        if step:
            self.wait_recv(phase, step - 1)
            for route in range(ROUTES):
                self.take(phase, route, step - 1)
        if step < STEPS:
            self.start(phase, step)


def greet(others):
    barrier = pltpu.get_barrier_semaphore()
    for other in others:
        pl.semaphore_signal(barrier, inc=1, device_id=other, device_id_type=MESH)
    pl.semaphore_wait(barrier, len(others))


def sibling():
    chip, core = position()
    return device(chip, 1 - core)


class VectorSum:
    def __init__(self, kept, came, sems, base):
        self.kept, self.came, (self.send, self.recv), self.base = kept, came, sems, base
        self.chip, self.core = position()

    def copy(self, stage, target, src, dst):
        return pltpu.make_async_remote_copy(
            src_ref=src,
            dst_ref=dst,
            send_sem=self.send.at[self.base + stage],
            recv_sem=self.recv.at[self.base + stage],
            device_id=target,
            device_id_type=MESH,
        )

    def targets(self, stage):
        if stage == 0:
            return [device(self.chip, 1 - self.core)]
        return [device(moved(self.chip, stage - 1, by), self.core) for by in PARTNERS]

    def all_of(self, stage):
        targets = self.targets(stage)
        whole = self.came.at[pl.ds(max(3 * stage - 2, 0), len(targets))]
        return self.copy(stage, targets[0], whole, whole)

    def step(self, stage):
        if stage:
            self.all_of(stage - 1).wait_recv()
            own = self.kept[stage - 1]
            if stage == 1:
                self.kept[1] = own + self.came[0]
            else:
                slot = 3 * stage - 5
                self.kept[stage] = (own + self.came[slot + 2]) + (self.came[slot] + self.came[slot + 1])
        if stage < 4:
            for n, target in enumerate(self.targets(stage)):
                there = self.came.at[max(3 * stage - 2, 0) + n]
                self.copy(stage, target, self.kept.at[stage], there).start()

    def wait_send(self, stage):
        self.all_of(stage).wait_send()


GROUP = 512
HALF = 256
WIDTH = 1024
HEAD_DIM = 64
PAIR = 2 * HEAD_DIM
SCALE = HEAD_DIM**-0.5
EPSILON = 1e-12
NN = (((1,), (0,)), ((), ()))
NT = (((1,), (1,)), ((), ()))
TN = (((0,), (0,)), ((), ()))
Q_TILE, OUT_TILE, UP_TILE, DOWN_TILE = 0, 6, 8, 16
WEIGHT_TILES = (2, 2, 2, 2, 8, 8)


def dot(a, b, dims=NN):
    return lax.dot_general(a, b, dims, preferred_element_type=F32)


def loop(count, body):
    def step(i, carry):
        body(i)
        return carry

    lax.fori_loop(0, count, step, 0)


VECTORS = (8, 8, 32, 16, 16, 16, 16, 16, 16)
VECTOR_ROWS = (0, 8, 16, 48, 56, 64, 72, 80, 88)


def layer_kernel(
    w_q, w_k, w_v, w_o, w_u, w_d,
    v_0, v_1, v_2, v_3, v_4, v_5, v_6, v_7, v_8, segment, tokens, out_grad,
    layer_out, input_grad, shares, vec_out,
    w, g, x, n1, gd, tr, x_tr, qkv, probs, bias, ctx, gctx, ds, part, leave, come,
    hat, inv, d_two, cot, act, slope, seg_here, seg_own, segments, segcol, features, biases, bias_sums, sums, out_rows,
    r_0, r_1, r_2, r_3, r_4, r_5, r_6, r_7, r_8, placed,
    kept, came, kept_front, came_front, kept_tail, came_tail,
    gsend, grecv, ssend, srecv, vsend, vrecv, swap_send, swap_recv, sib_send, sib_recv, load_sem,
    *landings,
):
    chip, core = position()
    y, x_at, z = chip
    low = lax.rem(z, 2)
    opposite_chip = opposite_z(chip)
    diagonal = device(opposite_chip, 1 - core)
    twin = sibling()
    stays = core == low
    own_rows = pl.ds(pl.multiple_of(core * HALF, HALF), HALF)
    other_rows = pl.ds(pl.multiple_of((1 - core) * HALF, HALF), HALF)

    raw = (r_0, r_1, r_2, r_3, r_4, r_5, r_6, r_7, r_8)
    loads = [
        pltpu.make_async_copy(src, dst, load_sem.at[n])
        for n, (src, dst) in enumerate(zip((v_0, v_1, v_2, v_3, v_4, v_5, v_6, v_7, v_8), raw))
    ]
    loads.append(pltpu.make_async_copy(segment, seg_here.at[0], load_sem.at[9]))
    loads.append(pltpu.make_async_copy(out_grad, d_two, load_sem.at[10]))
    for load in loads:
        load.start()

    def swap_copies(n, src, dst_here, dst_there):
        away = pltpu.make_async_remote_copy(
            src_ref=src, dst_ref=dst_there, send_sem=swap_send.at[n], recv_sem=swap_recv.at[n],
            device_id=diagonal, device_id_type=MESH,
        )
        return away, pltpu.make_async_copy(src, dst_here, swap_recv.at[n])

    def swap_start(n, src, dst_here, dst_there):
        away, here = swap_copies(n, src, dst_here, dst_there)
        pl.when(stays)(here.start)
        pl.when(jnp.logical_not(stays))(away.start)

    def swap_wait(n, src, dst_here, dst_there):
        away, here = swap_copies(n, src, dst_here, dst_there)
        pl.when(stays)(here.wait)
        pl.when(jnp.logical_not(stays))(away.wait)

    def to_twin(n, src, dst):
        return pltpu.make_async_remote_copy(
            src_ref=src, dst_ref=dst, send_sem=sib_send.at[n], recv_sem=sib_recv.at[n],
            device_id=twin, device_id_type=MESH,
        )

    greet([device(moved(chip, axis, by), core) for axis in range(3) for by in PARTNERS] + [twin, diagonal])

    weight_moves = []
    tile = 0
    for ref, count in zip((w_q, w_k, w_v, w_o, w_u, w_d), WEIGHT_TILES):
        for k in range(count):
            weight_moves.append(
                (
                    tile // 6,
                    ref.at[:, pl.ds(k * COLS, COLS)],
                    w.at[tile, y, x_at, z],
                    w.at[(tile,) + opposite_chip],
                )
            )
            tile += 1
    for move in weight_moves:
        swap_start(*move)

    gather = Gather(w, (gsend, grecv))
    vectors = VectorSum(kept, came, (vsend, vrecv), 0)

    def arrived(phase):
        group = w.at[pl.ds(6 * phase, 6), y, x_at, z]
        swap_wait(phase, group, group, group)

    for load in loads[:-1]:
        load.wait()
    dp, tensor = lax.axis_index("dp"), lax.axis_index("tensor")
    placed[...] = jnp.zeros((VEC_ROWS, 128), F32)
    for n, (ref, length, row) in enumerate(zip(raw, VECTORS, VECTOR_ROWS)):
        at = (tensor * 64 + dp if n < 3 else dp) * length
        value = ref[...].astype(F32).reshape(1, length)
        value = jnp.concatenate([value, jnp.zeros((1, 128 - length), F32)], axis=1)
        value = pltpu.roll(jnp.broadcast_to(value, (8, 128)), lax.rem(at, 128), 1)
        if n >= 3:
            value = jnp.where(tensor == 0, value, 0.0)
        placed[pl.ds(row + at // 128, 1), :] = value[0:1]
    kept[0] = placed[...].astype(BF16)
    vectors.step(0)
    seg_own[...] = jnp.broadcast_to(seg_here[...].astype(F32), (8, GROUP))
    seg_move = (5, seg_own, segments, segments)
    swap_start(*seg_move)
    arrived(0)
    gather.step(0, 0)
    row_move = (4, tokens, x.at[own_rows], x.at[other_rows])
    swap_start(*row_move)
    vectors.step(1)
    for phase in (1, 2, 3):
        arrived(phase)
        gather.step(phase, 0)
    gather.step(0, 1)
    vectors.step(2)
    gather.step(1, 1)

    swap_wait(*seg_move)
    across_lanes = jnp.broadcast_to(segments[0:1, :], (128, GROUP))
    segcol[...] = across_lanes.T
    for k in range(4):
        cols = slice(k * 128, k * 128 + 128)
        bias[:, cols] = jnp.where(segcol[...] == segments[0:1, cols], 0.0, -1000000000.0).astype(BF16)
    gather.step(0, 2)
    vectors.step(3)
    gather.step(2, 1)
    swap_wait(*row_move)
    rows_copy = to_twin(0, x.at[own_rows], x.at[own_rows])
    rows_copy.start()
    loads[-1].wait()
    out_rows[...] = d_two[...].astype(BF16)
    gather.step(0, 3)
    gather.step(1, 2)
    gather.step(3, 1)
    vectors.step(4)
    placed[...] = kept[4].astype(F32)
    for n in range(6):
        for k in range(8):
            features[n, :, k * 128 : k * 128 + 128] = placed[48 + n * 8 + k : 49 + n * 8 + k, :]
    for k in range(2):
        for half in range(2):
            lanes = slice(half * 128, half * 128 + 128)
            biases[k, :, lanes] = placed[pl.ds(core * 4 + k * 2 + half, 1), :]
            biases[4 + k, :, lanes] = placed[pl.ds(8 + core * 4 + k * 2 + half, 1), :]
        biases[2 + k] = jnp.zeros((1, COLS), F32)
    for k in range(8):
        for half in range(2):
            lanes = slice(half * 128, half * 128 + 128)
            biases[6 + k, :, lanes] = placed[pl.ds(16 + core * 16 + k * 2 + half, 1), :]
    rows_copy.wait_recv()

    def turn(ref, out=tr):
        for k in range(4):
            rows = slice(k * COLS, k * COLS + COLS)
            out[rows, :] = ref[:, rows].T

    turn(x, x_tr)
    gather.step(0, 4)

    def weight(tile):
        return w[tile].reshape(WIDTH, COLS)

    def project(t):
        made = (dot(x[...], weight(t)) + biases[t]).astype(BF16)
        qkv[2 * t] = made[:, :128]
        qkv[2 * t + 1] = made[:, 128:]

    loop(6, project)
    gather.step(1, 3)
    gather.step(2, 2)
    low_lanes = lax.broadcasted_iota(jnp.int32, (1, PAIR), 1) < HEAD_DIM

    def only(head, values):
        keep = low_lanes if head == 0 else jnp.logical_not(low_lanes)
        return jnp.where(keep, values, jnp.zeros_like(values))

    def attend(pair):
        for half in range(2):
            rows = slice(half * HALF, half * HALF + HALF)
            query = qkv[pair, rows]
            outs = []
            for head in range(2):
                scores = dot(qkv[4 + pair], only(head, query), NT) * SCALE + bias[:, rows].astype(F32)
                scores = jnp.exp(scores - jnp.max(scores, axis=0, keepdims=True))
                weights = scores * (1.0 / jnp.sum(scores, axis=0, keepdims=True))
                weights = weights.astype(BF16)
                probs[2 * pair + head, :, rows] = weights
                outs.append(dot(weights, qkv[8 + pair], TN))
            ctx[pair, rows] = jnp.where(low_lanes, outs[0], outs[1]).astype(BF16)

    attend(0)
    gather.step(3, 2)
    attend(1)
    gather.step(2, 3)
    attend(2)
    gather.step(3, 3)
    cot_move = (6, out_rows, cot, cot)
    swap_start(*cot_move)
    attend(3)
    gather.step(1, 4)

    terms_sent = []

    def row_terms(n, tiles, left):
        def block(rows, store):
            def one(k):
                lanes = pl.ds(pl.multiple_of(k * COLS, COLS), COLS)
                total = None
                for t, at in enumerate(tiles):
                    term = dot(left(t, rows), w[at, k].reshape(COLS, COLS), NT)
                    total = term if total is None else total + term
                store(lanes, total)

            loop(4, one)

        if n:
            terms_sent[-1].wait_send()

        def leaves(lanes, total):
            leave[:, lanes] = total.astype(BF16)

        def stays_here(lanes, total):
            part[:, lanes] = total

        block(other_rows, leaves)
        copy = to_twin(1 + n, leave, come)
        copy.start()
        block(own_rows, stays_here)
        copy.wait_recv()
        terms_sent.append(copy)

    def side_by_side(ref, first, rows=slice(None)):
        return jnp.concatenate([ref[first, rows], ref[first + 1, rows]], axis=1)

    sent = [rows_copy]
    row_terms(0, range(OUT_TILE, UP_TILE), lambda t, rows: side_by_side(ctx, 2 * t, rows))
    chunk = 64

    def by_chunks(body):
        def one(i):
            at = pl.multiple_of(i * chunk, chunk)
            body(pl.ds(at, chunk), pl.ds(pl.multiple_of(core * HALF + at, chunk), chunk))

        loop(HALF // chunk, one)

    def mean(values):
        return jnp.mean(values, axis=-1, keepdims=True)

    def normalized(hidden):
        centered = hidden - mean(hidden)
        scale = lax.rsqrt(mean(centered * centered) + EPSILON)
        return centered * scale, scale

    for n in range(6):
        sums[n] = jnp.zeros((1, WIDTH), F32)

    def add_sum(n, values):
        sums[n] += jnp.sum(values, axis=0, keepdims=True)

    b_out, b_down, gain_one, shift_one, gain_two, shift_two = range(6)

    def first_norm(here, there):
        hidden = x[there].astype(F32) + part[here] + come[here].astype(F32) + features[b_out]
        value, scale = normalized(hidden)
        hat[here] = value
        inv[here] = jnp.broadcast_to(scale, (chunk, 128))
        n1[there] = (value * features[gain_one] + features[shift_one]).astype(BF16)

    by_chunks(first_norm)

    shared = {}

    def share_rows(n, ref):
        copy = to_twin(n, ref.at[own_rows], ref.at[own_rows])
        copy.start()
        shared[n] = copy
        copy.wait_recv()

    share_rows(5, n1)

    def up(t):
        for half in range(2):
            rows = slice(half * HALF, half * HALF + HALF)
            pre = dot(n1[rows], weight(UP_TILE + t)) + biases[6 + t]
            below = 0.5 * (1.0 + lax.erf(pre * (0.5**0.5)))
            act[t, rows] = (pre * below).astype(BF16)
            bell = jnp.exp(pre * pre * -0.5) * 0.3989422804014327
            slope[t, rows] = (below + pre * bell).astype(BF16)

    loop(4, up)
    gather.step(2, 4)
    loop(4, lambda t: up(t + 4))
    gather.step(3, 4)
    row_terms(1, range(DOWN_TILE, TILES), lambda t, rows: act[t, rows])
    swap_wait(*cot_move)

    def norm_back(values, incoming, gain, scale, gain_at, shift_at):
        add_sum(shift_at, incoming)
        add_sum(gain_at, incoming * values)
        scaled = incoming * gain
        return scale * (scaled - mean(scaled) - values * mean(scaled * values))

    def second_norm(here, there):
        first = hat[here] * features[gain_one] + features[shift_one]
        value, scale = normalized(first + part[here] + come[here].astype(F32) + features[b_down])
        live = jnp.where(segcol[there, 0:1] >= 0, 1.0, 0.0)
        out_rows[here] = ((value * features[gain_two] + features[shift_two]) * live).astype(BF16)
        back = norm_back(
            value, cot[here].astype(F32) * live, features[gain_two], scale, gain_two, shift_two
        )
        add_sum(b_down, back)
        d_two[here] = back
        gd[there] = back.astype(BF16)

    by_chunks(second_norm)
    out_move = (7, out_rows, layer_out, layer_out)
    swap_start(*out_move)
    share_rows(6, gd)

    def store_grad(tile, right, left=tr):
        for k in range(4):
            made = dot(left[k * COLS : k * COLS + COLS, :], right)
            g[tile, k] = made.astype(BF16).reshape(4, 4, 16, COLS)

    scatter = Scatter(g, landings, (ssend, srecv))
    share_moves = []

    def reduced(phase):
        scatter.step(phase, 4)
        tiles = pl.ds(6 * phase, 6)
        share_moves.append(
            (9 + phase, g.at[tiles, y, x_at, z], shares.at[tiles], shares.at[tiles])
        )
        swap_start(*share_moves[-1])

    turn(gd)
    loop(8, lambda t: store_grad(DOWN_TILE + t, act[t]))
    scatter.step(3, 0)

    def up_back(t):
        made = (dot(gd[...], weight(DOWN_TILE + t)) * slope[t].astype(F32)).astype(BF16)
        slope[t] = made
        bias_sums[6 + t] = jnp.sum(made.astype(F32), axis=0, keepdims=True)

    loop(8, up_back)
    scatter.step(3, 1)
    turn(n1)
    loop(4, lambda t: store_grad(UP_TILE + 4 + t, slope[4 + t]))
    scatter.step(2, 0)
    loop(4, lambda t: store_grad(UP_TILE + t, slope[t]))
    row_terms(2, range(UP_TILE, DOWN_TILE), lambda t, rows: slope[t, rows])

    def first_norm_back(here, there):
        incoming = d_two[here] + part[here] + come[here].astype(F32)
        back = norm_back(
            hat[here], incoming, features[gain_one], inv[here, 0:1], gain_one, shift_one
        )
        add_sum(b_out, back)
        d_two[here] = back
        n1[there] = back.astype(BF16)

    shared.pop(5).wait_send()
    d1 = n1
    scatter.step(3, 2)
    scatter.step(2, 1)
    by_chunks(first_norm_back)
    share_rows(7, d1)
    turn(d1)
    loop(2, lambda u: store_grad(OUT_TILE + u, side_by_side(ctx, 2 * u)))
    scatter.step(1, 0)
    scatter.step(3, 3)

    kept_front[0] = jnp.zeros((VEC_ROWS - 16, 128), F32)
    for k in range(8):
        for half in range(2):
            lanes = slice(half * 128, half * 128 + 128)
            kept_front[0, pl.ds(core * 16 + k * 2 + half, 1), :] = bias_sums[6 + k, :, lanes]
    for n in range(6):
        for k in range(8):
            at = 32 + n * 8 + k
            kept_front[0, at : at + 1, :] = sums[n, :, k * 128 : k * 128 + 128]
    front = VectorSum(kept_front, came_front, (vsend, vrecv), 4)
    front.step(0)

    def context_back(u):
        made = dot(d1[...], weight(OUT_TILE + u)).astype(BF16)
        gctx[2 * u] = made[:, :128]
        gctx[2 * u + 1] = made[:, 128:]

    loop(2, context_back)
    scatter.step(2, 2)
    front.step(1)

    def attend_back(pair):
        for half in range(2):
            rows = slice(half * HALF, half * HALF + HALF)
            for head in range(2):
                weights = probs[2 * pair + head, :, rows].astype(F32)
                grad = dot(qkv[8 + pair], only(head, gctx[pair, rows]), NT)
                total = jnp.sum(grad * weights, axis=0, keepdims=True)
                ds[head, :, rows] = (weights * (grad - total)).astype(BF16)
        query = [dot(ds[head], qkv[4 + pair], TN) for head in range(2)]
        key = [dot(ds[head], qkv[pair]) for head in range(2)]
        value = [dot(probs[2 * pair + head], gctx[pair]) for head in range(2)]
        for at, (a, b), scale in ((0, query, SCALE), (4, key, SCALE), (8, value, 1.0)):
            made = (jnp.where(low_lanes, a, b) * scale).astype(BF16)
            qkv[at + pair] = made
            bias_sums[14 + at + pair, :, :PAIR] = jnp.sum(made.astype(F32), axis=0, keepdims=True)

    attend_back(0)
    scatter.step(1, 1)
    reduced(3)
    front.step(2)
    attend_back(1)
    scatter.step(2, 3)
    front.step(3)
    attend_back(2)
    scatter.step(1, 2)
    front.step(4)
    reduced(2)
    attend_back(3)
    scatter.step(1, 3)
    kept_tail[0] = jnp.zeros((16, 128), F32)
    for k in range(4):
        kept_tail[0, pl.ds(core * 4 + k, 1), :] = bias_sums[14 + k, :, :PAIR]
        kept_tail[0, pl.ds(8 + core * 4 + k, 1), :] = bias_sums[22 + k, :, :PAIR]
    tail = VectorSum(kept_tail, came_tail, (vsend, vrecv), 8)
    tail.step(0)
    loop(6, lambda t: store_grad(t, side_by_side(qkv, 2 * t), x_tr))
    scatter.step(0, 0)
    tail.step(1)
    reduced(1)
    row_terms(3, range(6), lambda t, rows: side_by_side(qkv, 2 * t, rows))
    scatter.step(0, 1)
    tail.step(2)

    def last_rows(here, there):
        cot[here] = (d_two[here] + part[here] + come[here].astype(F32)).astype(BF16)

    by_chunks(last_rows)
    grad_move = (8, cot, input_grad, input_grad)
    swap_start(*grad_move)
    scatter.step(0, 2)
    tail.step(3)
    scatter.step(0, 3)
    tail.step(4)
    reduced(0)
    vec_out[0:16] = kept_tail[4]
    vec_out[16:] = kept_front[4]

    for move in [out_move, grad_move] + share_moves:
        swap_wait(*move)
    for copy in sent + terms_sent[-1:] + list(shared.values()):
        copy.wait_send()
    for phase in range(PHASES):
        for step in range(STEPS):
            gather.wait_send(phase, step)
            scatter.wait_send(phase, step)
    for stage in range(4):
        vectors.wait_send(stage)
        front.wait_send(stage)
        tail.wait_send(stage)


def layer_call(*arrays):
    full = (TILES, 4, 4, 4, 16, COLS)
    rows = (GROUP, WIDTH)
    half = (HALF, WIDTH)
    front = VEC_ROWS - 16
    scratch = [
        (full, BF16), (full, BF16),
        (rows, BF16), (rows, BF16), (rows, BF16), ((WIDTH, GROUP), BF16), ((WIDTH, GROUP), BF16),
        ((12, GROUP, PAIR), BF16), ((8, GROUP, GROUP), BF16), ((GROUP, GROUP), BF16),
        ((4, GROUP, PAIR), BF16), ((4, GROUP, PAIR), BF16), ((2, GROUP, GROUP), BF16),
        (half, F32), (half, BF16), (half, BF16),
        (half, F32), ((HALF, 128), F32), (half, F32), (half, BF16),
        ((8, GROUP, COLS), BF16), ((8, GROUP, COLS), BF16),
        ((1, GROUP), jnp.int32), ((8, GROUP), F32), ((8, GROUP), F32), ((GROUP, 128), F32),
        ((6, 1, WIDTH), F32), ((14, 1, COLS), F32), ((26, 1, COLS), F32), ((6, 1, WIDTH), F32),
        (half, BF16),
    ] + [((length,), BF16) for length in VECTORS] + [
        ((VEC_ROWS, 128), F32),
        ((5, VEC_ROWS, 128), BF16), ((10, VEC_ROWS, 128), BF16),
        ((5, front, 128), F32), ((10, front, 128), F32),
        ((5, 16, 128), F32), ((10, 16, 128), F32),
    ]
    sems = [PHASES * STEPS] * 4 + [12] * 2 + [13] * 2 + [8] * 2 + [11]
    return pl.pallas_call(
        layer_kernel,
        out_shape=(
            jax.ShapeDtypeStruct(half, BF16),
            jax.ShapeDtypeStruct(half, BF16),
            jax.ShapeDtypeStruct((TILES, 16, COLS), BF16),
            jax.ShapeDtypeStruct((VEC_ROWS, 128), F32),
        ),
        in_specs=[pl.BlockSpec(memory_space=pl.ANY)] * len(arrays),
        out_specs=(pl.BlockSpec(memory_space=pl.ANY),) * 3 + (pl.BlockSpec(memory_space=pltpu.VMEM),),
        scratch_shapes=[pltpu.VMEM(*s) for s in scratch]
        + [pltpu.SemaphoreType.DMA((n,)) for n in sems]
        + [pltpu.VMEM(s, BF16) for s in landing_shapes()],
        compiler_params=pltpu.CompilerParams(
            collective_id=0, has_side_effects=True, vmem_limit_bytes=64 * 2**20
        ),
    )(*arrays)


def finish_kernel(
    layer_in, grad_in, shares_in, totals_in,
    layer_out, input_grad, g_q, g_k, g_v, g_o, g_u, g_d, o_0, o_1, o_2, o_3, o_4, o_5, o_6, o_7, o_8,
    layer, grad_low, shares, totals, grad, f_q, f_k, f_v, f_o, f_u, f_d, s_0, s_1, s_2, s_3, s_4, s_5, s_6, s_7, s_8,
    in_sem, out_sem,
):
    pairs = ((totals_in, totals), (shares_in, shares), (grad_in, grad_low), (layer_in, layer))
    loads = [pltpu.make_async_copy(src, dst, in_sem.at[n]) for n, (src, dst) in enumerate(pairs)]
    for load in loads:
        load.start()
    dp, tensor = lax.axis_index("dp"), lax.axis_index("tensor")
    stores = []

    def store(src, dst):
        stores.append(pltpu.make_async_copy(src, dst, out_sem.at[len(stores)]))
        stores[-1].start()

    loads[0].wait()
    rows = (s_0, s_1, s_2, s_3, s_4, s_5, s_6, s_7, s_8)
    outs = (o_0, o_1, o_2, o_3, o_4, o_5, o_6, o_7, o_8)
    for n, (kept, out, length, row) in enumerate(zip(rows, outs, VECTORS, VECTOR_ROWS)):
        at = (tensor * 64 + dp if n < 3 else dp) * length
        value = jnp.broadcast_to(totals[pl.ds(row + at // 128, 1), :], (8, 128))
        value = pltpu.roll(value, lax.rem(128 - lax.rem(at, 128), 128), 1)
        kept[...] = value[0:1, :length].reshape(length)
        store(kept, out)
    loads[1].wait()
    tile = 0
    for kept, out, count in zip((f_q, f_k, f_v, f_o, f_u, f_d), (g_q, g_k, g_v, g_o, g_u, g_d), WEIGHT_TILES):
        for k in range(count):
            kept[:, k * COLS : k * COLS + COLS] = shares[tile].astype(F32)
            tile += 1
        store(kept, out)
    loads[2].wait()
    for k in range(4):
        part = slice(k * 64, k * 64 + 64)
        grad[part] = grad_low[part].astype(F32)
        store(grad.at[part], input_grad.at[part])
    loads[3].wait()
    store(layer, layer_out)
    for copy in stores:
        copy.wait()


def finish_call(*arrays):
    half = (HALF, WIDTH)
    shares = [(16, count * COLS) for count in WEIGHT_TILES]
    vectors = [(length,) for length in VECTORS]
    outs = [(half, BF16)] + [(shape, F32) for shape in [half] + shares + vectors]
    scratch = [(half, BF16), (half, BF16), ((TILES, 16, COLS), BF16), ((VEC_ROWS, 128), F32)] + outs[1:]
    return pl.pallas_call(
        finish_kernel,
        out_shape=tuple(jax.ShapeDtypeStruct(*o) for o in outs),
        in_specs=[pl.BlockSpec(memory_space=pl.ANY)] * len(arrays),
        out_specs=(pl.BlockSpec(memory_space=pl.ANY),) * len(outs),
        scratch_shapes=[pltpu.VMEM(*o) for o in scratch]
        + [pltpu.SemaphoreType.DMA((4,)), pltpu.SemaphoreType.DMA((20,))],
    )(*arrays)


def on_device(
    tokens, segment, w_query, w_key, w_value, w_out, w_up, w_down, b_query, b_value, b_up,
    b_out, b_down, gain_one, shift_one, gain_two, shift_two, out_grad,
):
    made = layer_call(
        w_query, w_key, w_value, w_out, w_up, w_down, b_query, b_value, b_up,
        b_out, b_down, gain_one, shift_one, gain_two, shift_two, segment, tokens, out_grad,
    )
    return tuple(finish_call(*made))


def solution(mesh):
    placed = (
        P(("dp", "tensor"), None),
        P("dp"),
        P("dp", "tensor"),
        P("dp", "tensor"),
        P("dp", "tensor"),
        P("dp", "tensor"),
        P("dp", "tensor"),
        P("dp", "tensor"),
        P(("tensor", "dp")),
        P(("tensor", "dp")),
        P(("tensor", "dp")),
        P("dp"),
        P("dp"),
        P("dp"),
        P("dp"),
        P("dp"),
        P("dp"),
        P(("dp", "tensor"), None),
    )
    return jax.shard_map(
        on_device,
        mesh=mesh,
        in_specs=placed,
        out_specs=(
            P(("dp", "tensor"), None),
            P(("dp", "tensor"), None),
            P("dp", "tensor"),
            P("dp", "tensor"),
            P("dp", "tensor"),
            P("dp", "tensor"),
            P("dp", "tensor"),
            P("dp", "tensor"),
            P(("tensor", "dp")),
            P(("tensor", "dp")),
            P(("tensor", "dp")),
            P("dp"),
            P("dp"),
            P("dp"),
            P("dp"),
            P("dp"),
            P("dp"),
        ),
        check_vma=False,
    )
```

```python
import jax
import jax.numpy as jnp
from jax import lax
from jax.experimental import pallas as pl
from jax.experimental.pallas import tpu as pltpu
from jax.sharding import PartitionSpec as P

MESH = pl.DeviceIdType.MESH
F32 = jnp.float32
BF16 = jnp.bfloat16

TILES = 24
COLS = 256
PHASES, ROUTES, STEPS = 4, 3, 4
VEC_ROWS = 96
ORDERS = ((2, 0, 1), (1, 2, 0), (0, 1, 2))
PARTNERS = (1, 3, 2)


def position():
    dp, low = lax.axis_index("dp"), lax.axis_index("tensor")
    return (dp // 16, lax.rem(dp // 4, 4), lax.rem(dp // 2, 2) * 2 + low), lax.rem(dp, 2)


def device(chip, core):
    y, x, z = chip
    return (y * 16 + x * 4 + (z // 2) * 2 + core, lax.rem(z, 2))


def moved(chip, axis, by):
    return tuple(lax.rem(c + by, 4) if k == axis else c for k, c in enumerate(chip))


def opposite_z(chip):
    y, x, z = chip
    return (y, x, z + 1 - 2 * lax.rem(z, 2))


def blocks(chip, full):
    return tuple(pl.ds(0, 4) if axis in full else pl.ds(c, 1) for axis, c in enumerate(chip))


def block_shape(full):
    return tuple(4 if axis in full else 1 for axis in range(3))


def first_tile(phase, route):
    return phase * 6 + route * 2


class Ring:
    def __init__(self, buffer, sems):
        self.buffer, (self.send, self.recv) = buffer, sems
        self.chip, self.core = position()

    def copy(self, phase, step, target, src, dst):
        sem = phase * STEPS + step
        return pltpu.make_async_remote_copy(
            src_ref=src, dst_ref=dst, send_sem=self.send.at[sem], recv_sem=self.recv.at[sem],
            device_id=target, device_id_type=MESH,
        )

    def partner(self, axis, way):
        return device(moved(self.chip, axis, PARTNERS[way]), self.core)

    def start_route(self, phase, route, step):
        for c in self.copies(phase, route, step):
            c.start()

    def start(self, phase, step):
        for route in range(ROUTES):
            self.start_route(phase, route, step)

    def all_of(self, phase, step):
        tiles, ny, nx, nz = self.size(phase, step)
        whole = self.buffer.at[pl.ds(0, tiles), pl.ds(0, ny), pl.ds(0, nx), pl.ds(0, nz)]
        return self.copy(phase, step, self.partner(0, 0), whole, whole)

    def wait_recv(self, phase, step):
        self.all_of(phase, step).wait_recv()

    def wait_send(self, phase, step):
        self.all_of(phase, step).wait_send()


class Gather(Ring):
    def size(self, phase, step):
        return ((18, 1, 1, 1), (18, 1, 1, 4), (12, 1, 4, 4), (6, 1, 4, 4))[step]

    def copies(self, phase, route, step):
        order, k = ORDERS[route], min(step, 2)
        axis, full = order[k], order[:k]
        tile = first_tile(phase, route)
        out = []
        for way in range(3 if step < 2 else 2):
            if step < 3:
                part = self.buffer.at[(pl.ds(tile, 2),) + blocks(self.chip, full)]
            else:
                behind = moved(self.chip, axis, PARTNERS[1 - way])
                part = self.buffer.at[(pl.ds(tile + way, 1),) + blocks(behind, full)]
            out.append(self.copy(phase, step, self.partner(axis, way), part, part))
        return out

    def step(self, phase, step):
        if step:
            self.wait_recv(phase, step - 1)
        if step < STEPS:
            self.start(phase, step)


HALVES = (0, 4)


def scatter_tiles(phase, route):
    if phase in HALVES:
        return 2 * route + HALVES.index(phase), 1
    return first_tile(phase, route), 2


def scatter_steps(phase):
    return 3 if phase in HALVES else STEPS


def landing_shapes():
    shapes = []
    for phase in range(PHASES + 1):
        for order in ORDERS:
            for k in range(3):
                tiles = 3 if phase in HALVES else 6
                shapes.append((tiles,) + block_shape(order[: 2 - k]) + (16, COLS))
    return shapes


class Scatter(Ring):
    def __init__(self, g, landings, sems):
        super().__init__(g, sems)
        self.g, self.landings = g, landings

    def size(self, phase, step):
        if phase in HALVES:
            return ((9, 1, 4, 4), (9, 1, 1, 4), (9, 1, 1, 1))[step]
        return ((6, 1, 4, 4), (12, 1, 4, 4), (18, 1, 1, 4), (18, 1, 1, 1))[step]

    def at(self, phase, route, step):
        order, k = ORDERS[route], step if phase in HALVES else max(step - 1, 0)
        return order[2 - k], order[: 2 - k], self.landings[(phase * ROUTES + route) * 3 + k]

    def copies(self, phase, route, step):
        axis, full, landed = self.at(phase, route, step)
        tile, count = scatter_tiles(phase, route)
        out = []
        for way in range(2 if count == 2 and step < 2 else 3):
            if count == 2 and step == 0:
                src = self.g.at[(pl.ds(tile + way, 1),) + blocks(moved(self.chip, axis, 2), full)]
                dst = landed.at[pl.ds(way, 1)]
            else:
                ahead = moved(self.chip, axis, PARTNERS[way])
                src = self.g.at[(pl.ds(tile, count),) + blocks(ahead, full)]
                dst = landed.at[pl.ds(count * way + (2 if count == 2 and step == 1 else 0), count)]
            out.append(self.copy(phase, step, self.partner(axis, way), src, dst))
        return out

    def take(self, phase, route, step):
        axis, full, landed = self.at(phase, route, step)
        tile, count = scatter_tiles(phase, route)
        ny, nx, nz = block_shape(full)

        def start_of(chip):
            return tuple(0 if k in full else c for k, c in enumerate(chip))

        def add(t, base, parts):
            y0, x0, z0 = base

            def one(i, carry):
                at = (tile + t, y0 + i, pl.ds(x0, nx), pl.ds(z0, nz))
                total = self.g[at].astype(F32)
                for part in parts:
                    total += landed[part, i].astype(F32)
                self.g[at] = total.astype(BF16)
                return carry

            lax.fori_loop(0, ny, one, 0)

        for t in range(count):
            if count == 2 and step == 0:
                add(t, start_of(moved(self.chip, axis, PARTNERS[t])), (t,))
            elif count == 2 and step == 1:
                add(t, start_of(self.chip), (2 + t, 4 + t))
            else:
                add(t, start_of(self.chip), (t, count + t, 2 * count + t))

    def step(self, phase, step):
        if step:
            self.wait_recv(phase, step - 1)
            for route in range(ROUTES):
                self.take(phase, route, step - 1)
        if step < scatter_steps(phase):
            self.start(phase, step)


def greet(others):
    barrier = pltpu.get_barrier_semaphore()
    for other in others:
        pl.semaphore_signal(barrier, inc=1, device_id=other, device_id_type=MESH)
    pl.semaphore_wait(barrier, len(others))


def sibling():
    chip, core = position()
    return device(chip, 1 - core)


class VectorSum:
    def __init__(self, kept, came, sems, base):
        self.kept, self.came, (self.send, self.recv), self.base = kept, came, sems, base
        self.chip, self.core = position()

    def copy(self, stage, target, src, dst):
        return pltpu.make_async_remote_copy(
            src_ref=src,
            dst_ref=dst,
            send_sem=self.send.at[self.base + stage],
            recv_sem=self.recv.at[self.base + stage],
            device_id=target,
            device_id_type=MESH,
        )

    def targets(self, stage):
        if stage == 0:
            return [device(self.chip, 1 - self.core)]
        return [device(moved(self.chip, stage - 1, by), self.core) for by in PARTNERS]

    def all_of(self, stage):
        targets = self.targets(stage)
        whole = self.came.at[pl.ds(max(3 * stage - 2, 0), len(targets))]
        return self.copy(stage, targets[0], whole, whole)

    def step(self, stage):
        if stage:
            self.all_of(stage - 1).wait_recv()
            own = self.kept[stage - 1]
            if stage == 1:
                self.kept[1] = own + self.came[0]
            else:
                slot = 3 * stage - 5
                self.kept[stage] = (own + self.came[slot + 2]) + (self.came[slot] + self.came[slot + 1])
        if stage < 4:
            for n, target in enumerate(self.targets(stage)):
                there = self.came.at[max(3 * stage - 2, 0) + n]
                self.copy(stage, target, self.kept.at[stage], there).start()

    def wait_send(self, stage):
        self.all_of(stage).wait_send()


GROUP = 512
HALF = 256
WIDTH = 1024
HEAD_DIM = 64
PAIR = 2 * HEAD_DIM
SCALE = HEAD_DIM**-0.5
EPSILON = 1e-12
NN = (((1,), (0,)), ((), ()))
NT = (((1,), (1,)), ((), ()))
TN = (((0,), (0,)), ((), ()))
Q_TILE, OUT_TILE, UP_TILE, DOWN_TILE = 0, 6, 8, 16
WEIGHT_TILES = (2, 2, 2, 2, 8, 8)


def dot(a, b, dims=NN):
    return lax.dot_general(a, b, dims, preferred_element_type=F32)


def loop(count, body, together=2):
    def step(i, carry):
        for k in range(together):
            body(i * together + k)
        return carry

    lax.fori_loop(0, count // together, step, 0)


VECTORS = (8, 8, 32, 16, 16, 16, 16, 16, 16)
VECTOR_ROWS = (0, 8, 16, 48, 56, 64, 72, 80, 88)


def layer_kernel(
    w_q, w_k, w_v, w_o, w_u, w_d,
    v_0, v_1, v_2, v_3, v_4, v_5, v_6, v_7, v_8, segment, tokens, out_grad,
    layer_out, input_grad, shares, vec_out,
    w, g, x, n1, gd, tr, x_tr, qkv, probs, bias, ctx, gctx, ds, part, leave, come,
    hat, inv, d_two, cot, act, slope, seg_here, seg_own, segments, segcol, features, biases, bias_sums, sums, out_rows,
    r_0, r_1, r_2, r_3, r_4, r_5, r_6, r_7, r_8, placed,
    kept, came, kept_front, came_front, kept_tail, came_tail,
    gsend, grecv, ssend, srecv, vsend, vrecv, swap_send, swap_recv, sib_send, sib_recv, load_sem,
    *landings,
):
    chip, core = position()
    y, x_at, z = chip
    low = lax.rem(z, 2)
    opposite_chip = opposite_z(chip)
    diagonal = device(opposite_chip, 1 - core)
    twin = sibling()
    stays = core == low
    own_rows = pl.ds(pl.multiple_of(core * HALF, HALF), HALF)
    other_rows = pl.ds(pl.multiple_of((1 - core) * HALF, HALF), HALF)

    raw = (r_0, r_1, r_2, r_3, r_4, r_5, r_6, r_7, r_8)
    loads = [
        pltpu.make_async_copy(src, dst, load_sem.at[n])
        for n, (src, dst) in enumerate(zip((v_0, v_1, v_2, v_3, v_4, v_5, v_6, v_7, v_8), raw))
    ]
    loads.append(pltpu.make_async_copy(segment, seg_here.at[0], load_sem.at[9]))
    loads.append(pltpu.make_async_copy(out_grad, d_two, load_sem.at[10]))
    for load in loads:
        load.start()

    def swap_copies(n, src, dst_here, dst_there):
        away = pltpu.make_async_remote_copy(
            src_ref=src, dst_ref=dst_there, send_sem=swap_send.at[n], recv_sem=swap_recv.at[n],
            device_id=diagonal, device_id_type=MESH,
        )
        return away, pltpu.make_async_copy(src, dst_here, swap_recv.at[n])

    def swap_start(n, src, dst_here, dst_there):
        away, here = swap_copies(n, src, dst_here, dst_there)
        pl.when(stays)(here.start)
        pl.when(jnp.logical_not(stays))(away.start)

    def swap_wait(n, src, dst_here, dst_there):
        away, here = swap_copies(n, src, dst_here, dst_there)
        pl.when(stays)(here.wait)
        pl.when(jnp.logical_not(stays))(away.wait)

    def to_twin(n, src, dst):
        return pltpu.make_async_remote_copy(
            src_ref=src, dst_ref=dst, send_sem=sib_send.at[n], recv_sem=sib_recv.at[n],
            device_id=twin, device_id_type=MESH,
        )

    greet([device(moved(chip, axis, by), core) for axis in range(3) for by in PARTNERS] + [twin, diagonal])

    weight_moves = []
    tile = 0
    for ref, count in zip((w_q, w_k, w_v, w_o, w_u, w_d), WEIGHT_TILES):
        for k in range(count):
            weight_moves.append(
                (
                    tile // 6,
                    ref.at[:, pl.ds(k * COLS, COLS)],
                    w.at[tile, y, x_at, z],
                    w.at[(tile,) + opposite_chip],
                )
            )
            tile += 1
    for move in weight_moves:
        swap_start(*move)

    gather = Gather(w, (gsend, grecv))
    vectors = VectorSum(kept, came, (vsend, vrecv), 0)

    def arrived(phase):
        group = w.at[pl.ds(6 * phase, 6), y, x_at, z]
        swap_wait(phase, group, group, group)

    for load in loads[:-1]:
        load.wait()
    dp, tensor = lax.axis_index("dp"), lax.axis_index("tensor")
    placed[...] = jnp.zeros((VEC_ROWS, 128), F32)
    for n, (ref, length, row) in enumerate(zip(raw, VECTORS, VECTOR_ROWS)):
        at = (tensor * 64 + dp if n < 3 else dp) * length
        value = ref[...].astype(F32).reshape(1, length)
        value = jnp.concatenate([value, jnp.zeros((1, 128 - length), F32)], axis=1)
        value = pltpu.roll(jnp.broadcast_to(value, (8, 128)), lax.rem(at, 128), 1)
        if n >= 3:
            value = jnp.where(tensor == 0, value, 0.0)
        placed[pl.ds(row + at // 128, 1), :] = value[0:1]
    kept[0] = placed[...].astype(BF16)
    vectors.step(0)
    seg_own[...] = jnp.broadcast_to(seg_here[...].astype(F32), (8, GROUP))
    seg_move = (5, seg_own, segments, segments)
    swap_start(*seg_move)
    arrived(0)
    gather.step(0, 0)
    row_move = (4, tokens, x.at[own_rows], x.at[other_rows])
    swap_start(*row_move)
    vectors.step(1)
    for phase in (1, 2, 3):
        arrived(phase)
        gather.step(phase, 0)
    gather.step(0, 1)
    vectors.step(2)
    gather.step(1, 1)
    gather.step(0, 2)
    vectors.step(3)
    gather.step(2, 1)

    swap_wait(*seg_move)
    across_lanes = jnp.broadcast_to(segments[0:1, :], (128, GROUP))
    segcol[...] = across_lanes.T
    for k in range(4):
        cols = slice(k * 128, k * 128 + 128)
        bias[:, cols] = jnp.where(segcol[...] == segments[0:1, cols], 0.0, -1000000000.0).astype(BF16)
    swap_wait(*row_move)
    rows_copy = to_twin(0, x.at[own_rows], x.at[own_rows])
    rows_copy.start()
    gather.step(0, 3)
    gather.step(3, 1)
    gather.step(1, 2)
    vectors.step(4)
    gather.step(2, 2)
    loads[-1].wait()
    out_rows[...] = d_two[...].astype(BF16)
    placed[...] = kept[4].astype(F32)
    for n in range(6):
        for k in range(8):
            features[n, :, k * 128 : k * 128 + 128] = placed[48 + n * 8 + k : 49 + n * 8 + k, :]
    for k in range(2):
        for half in range(2):
            lanes = slice(half * 128, half * 128 + 128)
            biases[k, :, lanes] = placed[pl.ds(core * 4 + k * 2 + half, 1), :]
            biases[4 + k, :, lanes] = placed[pl.ds(8 + core * 4 + k * 2 + half, 1), :]
        biases[2 + k] = jnp.zeros((1, COLS), F32)
    for k in range(8):
        for half in range(2):
            lanes = slice(half * 128, half * 128 + 128)
            biases[6 + k, :, lanes] = placed[pl.ds(16 + core * 16 + k * 2 + half, 1), :]
    rows_copy.wait_recv()

    def turn(ref, out=tr):
        for k in range(4):
            rows = slice(k * COLS, k * COLS + COLS)
            out[rows, :] = ref[:, rows].T

    def turn_half(ref, half):
        lanes = pl.ds(pl.multiple_of(half * HALF, HALF), HALF)
        for k in range(4):
            rows = slice(k * COLS, k * COLS + COLS)
            tr[rows, lanes] = ref[lanes, rows].T

    turn(x, x_tr)
    gather.step(0, 4)

    def weight(tile):
        return w[tile].reshape(WIDTH, COLS)

    def project(t):
        made = (dot(x[...], weight(t)) + biases[t]).astype(BF16)
        qkv[2 * t] = made[:, :128]
        qkv[2 * t + 1] = made[:, 128:]

    loop(6, project)
    low_lanes = lax.broadcasted_iota(jnp.int32, (1, PAIR), 1) < HEAD_DIM

    def only(head, values):
        keep = low_lanes if head == 0 else jnp.logical_not(low_lanes)
        return jnp.where(keep, values, jnp.zeros_like(values))

    def attend(pair):
        for half in range(2):
            rows = slice(half * HALF, half * HALF + HALF)
            query = qkv[pair, rows]
            outs = []
            for head in range(2):
                scores = dot(qkv[4 + pair], only(head, query), NT) * SCALE + bias[:, rows].astype(F32)
                scores = jnp.exp(scores - jnp.max(scores, axis=0, keepdims=True))
                weights = scores * (1.0 / jnp.sum(scores, axis=0, keepdims=True))
                weights = weights.astype(BF16)
                probs[2 * pair + head, :, rows] = weights
                outs.append(dot(weights, qkv[8 + pair], TN))
            ctx[pair, rows] = jnp.where(low_lanes, outs[0], outs[1]).astype(BF16)

    attend(0)
    attend(1)
    gather.step(1, 3)
    gather.step(3, 2)
    attend(2)
    attend(3)
    gather.step(2, 3)
    gather.step(1, 4)

    terms_sent = []

    def row_terms(n, tiles, left):
        def block(rows, store):
            def one(k):
                lanes = pl.ds(pl.multiple_of(k * COLS, COLS), COLS)
                total = None
                for t, at in enumerate(tiles):
                    term = dot(left(t, rows), w[at, k].reshape(COLS, COLS), NT)
                    total = term if total is None else total + term
                store(lanes, total)

            loop(4, one)

        if n:
            terms_sent[-1].wait_send()

        def leaves(lanes, total):
            leave[:, lanes] = total.astype(BF16)

        def stays_here(lanes, total):
            part[:, lanes] = total

        block(other_rows, leaves)
        copy = to_twin(1 + n, leave, come)
        copy.start()
        block(own_rows, stays_here)
        copy.wait_recv()
        terms_sent.append(copy)

    def side_by_side(ref, first, rows=slice(None)):
        return jnp.concatenate([ref[first, rows], ref[first + 1, rows]], axis=1)

    sent = [rows_copy]
    row_terms(0, range(OUT_TILE, UP_TILE), lambda t, rows: side_by_side(ctx, 2 * t, rows))
    chunk = 64

    def by_chunks(body):
        def one(i):
            at = pl.multiple_of(i * chunk, chunk)
            body(pl.ds(at, chunk), pl.ds(pl.multiple_of(core * HALF + at, chunk), chunk))

        loop(HALF // chunk, one, 1)

    def mean(values):
        return jnp.mean(values, axis=-1, keepdims=True)

    def normalized(hidden):
        centered = hidden - mean(hidden)
        scale = lax.rsqrt(mean(centered * centered) + EPSILON)
        return centered * scale, scale

    for n in range(6):
        sums[n] = jnp.zeros((1, WIDTH), F32)

    def add_sum(n, values):
        sums[n] += jnp.sum(values, axis=0, keepdims=True)

    b_out, b_down, gain_one, shift_one, gain_two, shift_two = range(6)

    def first_norm(here, there):
        hidden = x[there].astype(F32) + part[here] + come[here].astype(F32) + features[b_out]
        value, scale = normalized(hidden)
        hat[here] = value
        inv[here] = jnp.broadcast_to(scale, (chunk, 128))
        n1[there] = (value * features[gain_one] + features[shift_one]).astype(BF16)

    by_chunks(first_norm)
    gather.step(3, 3)
    cot_move = (6, out_rows, cot, cot)
    swap_start(*cot_move)

    shared = {}

    def share_rows(n, ref, meanwhile=None):
        copy = to_twin(n, ref.at[own_rows], ref.at[own_rows])
        copy.start()
        shared[n] = copy
        if meanwhile:
            meanwhile()
        copy.wait_recv()

    share_rows(5, n1)

    def up(t):
        for half in range(2):
            rows = slice(half * HALF, half * HALF + HALF)
            pre = dot(n1[rows], weight(UP_TILE + t)) + biases[6 + t]
            below = 0.5 * (1.0 + lax.erf(pre * (0.5**0.5)))
            act[t, rows] = (pre * below).astype(BF16)
            bell = jnp.exp(pre * pre * -0.5) * 0.3989422804014327
            slope[t, rows] = (below + pre * bell).astype(BF16)

    loop(4, up)
    gather.step(2, 4)
    loop(4, lambda t: up(t + 4))
    gather.step(3, 4)
    row_terms(1, range(DOWN_TILE, TILES), lambda t, rows: act[t, rows])
    swap_wait(*cot_move)

    def norm_back(values, incoming, gain, scale, gain_at, shift_at):
        add_sum(shift_at, incoming)
        add_sum(gain_at, incoming * values)
        scaled = incoming * gain
        return scale * (scaled - mean(scaled) - values * mean(scaled * values))

    def second_norm(here, there):
        first = hat[here] * features[gain_one] + features[shift_one]
        value, scale = normalized(first + part[here] + come[here].astype(F32) + features[b_down])
        live = jnp.where(segcol[there, 0:1] >= 0, 1.0, 0.0)
        out_rows[here] = ((value * features[gain_two] + features[shift_two]) * live).astype(BF16)
        back = norm_back(
            value, cot[here].astype(F32) * live, features[gain_two], scale, gain_two, shift_two
        )
        add_sum(b_down, back)
        d_two[here] = back
        gd[there] = back.astype(BF16)

    by_chunks(second_norm)
    out_move = (7, out_rows, layer_out, layer_out)
    swap_start(*out_move)
    share_rows(6, gd, lambda: turn_half(gd, core))
    turn_half(gd, 1 - core)

    def store_grad(tile, right, left=tr):
        for k in range(4):
            made = dot(left[k * COLS : k * COLS + COLS, :], right)
            g[tile, k] = made.astype(BF16).reshape(4, 4, 16, COLS)

    scatter = Scatter(g, landings, (ssend, srecv))
    share_moves = []

    def reduced(phase):
        scatter.step(phase, scatter_steps(phase))
        n = 9 + phase
        if phase in HALVES:
            moves = [scatter_tiles(phase, route)[0] for route in range(ROUTES)]
            whole = pl.ds(0, ROUTES)
        else:
            moves = [pl.ds(6 * phase, 6)]
            whole = moves[0]
        for tiles in moves:
            swap_start(n, g.at[tiles, y, x_at, z], shares.at[tiles], shares.at[tiles])
        share_moves.append((n, g.at[whole, y, x_at, z], shares.at[whole], shares.at[whole]))

    for route in range(ROUTES):
        for t in (2 + 2 * route, 3 + 2 * route):
            store_grad(DOWN_TILE + t, act[t])
        scatter.start_route(3, route, 0)
    for t in range(2):
        store_grad(DOWN_TILE + t, act[t])

    def up_back(t):
        made = (dot(gd[...], weight(DOWN_TILE + t)) * slope[t].astype(F32)).astype(BF16)
        slope[t] = made
        bias_sums[6 + t] = jnp.sum(made.astype(F32), axis=0, keepdims=True)

    loop(8, up_back)
    scatter.step(3, 1)
    turn(n1)
    loop(4, lambda t: store_grad(UP_TILE + 4 + t, slope[4 + t]))
    scatter.step(2, 0)
    loop(4, lambda t: store_grad(UP_TILE + t, slope[t]))
    row_terms(2, range(UP_TILE, DOWN_TILE), lambda t, rows: slope[t, rows])

    def first_norm_back(here, there):
        incoming = d_two[here] + part[here] + come[here].astype(F32)
        back = norm_back(
            hat[here], incoming, features[gain_one], inv[here, 0:1], gain_one, shift_one
        )
        add_sum(b_out, back)
        d_two[here] = back
        n1[there] = back.astype(BF16)

    shared.pop(5).wait_send()
    d1 = n1
    scatter.step(3, 2)
    by_chunks(first_norm_back)
    def meanwhile():
        turn_half(d1, core)
        scatter.step(2, 1)

    share_rows(7, d1, meanwhile)
    turn_half(d1, 1 - core)
    loop(2, lambda u: store_grad(OUT_TILE + u, side_by_side(ctx, 2 * u)))
    scatter.step(1, 0)
    scatter.step(3, 3)

    kept_front[0] = jnp.zeros((VEC_ROWS - 16, 128), F32)
    for k in range(8):
        for half in range(2):
            lanes = slice(half * 128, half * 128 + 128)
            kept_front[0, pl.ds(core * 16 + k * 2 + half, 1), :] = bias_sums[6 + k, :, lanes]
    for n in range(6):
        for k in range(8):
            at = 32 + n * 8 + k
            kept_front[0, at : at + 1, :] = sums[n, :, k * 128 : k * 128 + 128]
    front = VectorSum(kept_front, came_front, (vsend, vrecv), 4)
    front.step(0)

    def context_back(u):
        made = dot(d1[...], weight(OUT_TILE + u)).astype(BF16)
        gctx[2 * u] = made[:, :128]
        gctx[2 * u + 1] = made[:, 128:]

    loop(2, context_back)

    def attend_back(pair):
        for half in range(2):
            rows = slice(half * HALF, half * HALF + HALF)
            for head in range(2):
                weights = probs[2 * pair + head, :, rows].astype(F32)
                grad = dot(qkv[8 + pair], only(head, gctx[pair, rows]), NT)
                total = jnp.sum(grad * weights, axis=0, keepdims=True)
                ds[head, :, rows] = (weights * (grad - total)).astype(BF16)
        query = [dot(ds[head], qkv[4 + pair], TN) for head in range(2)]
        key = [dot(ds[head], qkv[pair]) for head in range(2)]
        value = [dot(probs[2 * pair + head], gctx[pair]) for head in range(2)]
        for at, (a, b), scale in ((0, query, SCALE), (4, key, SCALE), (8, value, 1.0)):
            made = (jnp.where(low_lanes, a, b) * scale).astype(BF16)
            qkv[at + pair] = made
            bias_sums[14 + at + pair, :, :PAIR] = jnp.sum(made.astype(F32), axis=0, keepdims=True)

    def store_qkv_grads(half):
        loop(3, lambda t: store_grad(2 * t + half, side_by_side(qkv, 4 * t + 2 * half), x_tr), 1)

    attend_back(0)
    scatter.step(2, 2)
    front.step(1)
    attend_back(1)
    scatter.step(1, 1)
    store_qkv_grads(0)
    scatter.step(0, 0)
    reduced(3)
    front.step(2)
    attend_back(2)
    scatter.step(2, 3)
    front.step(3)
    attend_back(3)
    scatter.step(1, 2)
    front.step(4)
    reduced(2)
    kept_tail[0] = jnp.zeros((16, 128), F32)
    for k in range(4):
        kept_tail[0, pl.ds(core * 4 + k, 1), :] = bias_sums[14 + k, :, :PAIR]
        kept_tail[0, pl.ds(8 + core * 4 + k, 1), :] = bias_sums[22 + k, :, :PAIR]
    tail = VectorSum(kept_tail, came_tail, (vsend, vrecv), 8)
    tail.step(0)
    store_qkv_grads(1)
    scatter.step(4, 0)
    scatter.step(0, 1)
    tail.step(1)
    scatter.step(1, 3)
    row_terms(3, range(6), lambda t, rows: side_by_side(qkv, 2 * t, rows))
    scatter.step(0, 2)
    tail.step(2)
    scatter.step(4, 1)

    def last_rows(here, there):
        cot[here] = (d_two[here] + part[here] + come[here].astype(F32)).astype(BF16)

    by_chunks(last_rows)
    grad_move = (8, cot, input_grad, input_grad)
    swap_start(*grad_move)
    reduced(1)
    reduced(0)
    tail.step(3)
    scatter.step(4, 2)
    tail.step(4)
    reduced(4)
    vec_out[0:16] = kept_tail[4]
    vec_out[16:] = kept_front[4]

    for move in [out_move, grad_move] + share_moves:
        swap_wait(*move)
    for copy in sent + terms_sent[-1:] + list(shared.values()):
        copy.wait_send()
    for phase in range(PHASES):
        for step in range(STEPS):
            gather.wait_send(phase, step)
    for phase in range(PHASES + 1):
        for step in range(scatter_steps(phase)):
            scatter.wait_send(phase, step)
    for stage in range(4):
        vectors.wait_send(stage)
        front.wait_send(stage)
        tail.wait_send(stage)


def layer_call(*arrays):
    full = (TILES, 4, 4, 4, 16, COLS)
    rows = (GROUP, WIDTH)
    half = (HALF, WIDTH)
    front = VEC_ROWS - 16
    scratch = [
        (full, BF16), (full, BF16),
        (rows, BF16), (rows, BF16), (rows, BF16), ((WIDTH, GROUP), BF16), ((WIDTH, GROUP), BF16),
        ((12, GROUP, PAIR), BF16), ((8, GROUP, GROUP), BF16), ((GROUP, GROUP), BF16),
        ((4, GROUP, PAIR), BF16), ((4, GROUP, PAIR), BF16), ((2, GROUP, GROUP), BF16),
        (half, F32), (half, BF16), (half, BF16),
        (half, F32), ((HALF, 128), F32), (half, F32), (half, BF16),
        ((8, GROUP, COLS), BF16), ((8, GROUP, COLS), BF16),
        ((1, GROUP), jnp.int32), ((8, GROUP), F32), ((8, GROUP), F32), ((GROUP, 128), F32),
        ((6, 1, WIDTH), F32), ((14, 1, COLS), F32), ((26, 1, COLS), F32), ((6, 1, WIDTH), F32),
        (half, BF16),
    ] + [((length,), BF16) for length in VECTORS] + [
        ((VEC_ROWS, 128), F32),
        ((5, VEC_ROWS, 128), BF16), ((10, VEC_ROWS, 128), BF16),
        ((5, front, 128), F32), ((10, front, 128), F32),
        ((5, 16, 128), F32), ((10, 16, 128), F32),
    ]
    sems = [PHASES * STEPS] * 2 + [(PHASES + 1) * STEPS] * 2 + [12] * 2 + [14] * 2 + [8] * 2 + [11]
    return pl.pallas_call(
        layer_kernel,
        out_shape=(
            jax.ShapeDtypeStruct(half, BF16),
            jax.ShapeDtypeStruct(half, BF16),
            jax.ShapeDtypeStruct((TILES, 16, COLS), BF16),
            jax.ShapeDtypeStruct((VEC_ROWS, 128), F32),
        ),
        in_specs=[pl.BlockSpec(memory_space=pl.ANY)] * len(arrays),
        out_specs=(pl.BlockSpec(memory_space=pl.ANY),) * 3 + (pl.BlockSpec(memory_space=pltpu.VMEM),),
        scratch_shapes=[pltpu.VMEM(*s) for s in scratch]
        + [pltpu.SemaphoreType.DMA((n,)) for n in sems]
        + [pltpu.VMEM(s, BF16) for s in landing_shapes()],
        compiler_params=pltpu.CompilerParams(
            collective_id=0, has_side_effects=True, vmem_limit_bytes=64 * 2**20
        ),
    )(*arrays)


def finish_kernel(
    layer_in, grad_in, shares_in, totals_in,
    layer_out, input_grad, g_q, g_k, g_v, g_o, g_u, g_d, o_0, o_1, o_2, o_3, o_4, o_5, o_6, o_7, o_8,
    layer, grad_low, shares, totals, grad, f_q, f_k, f_v, f_o, f_u, f_d, s_0, s_1, s_2, s_3, s_4, s_5, s_6, s_7, s_8,
    in_sem, out_sem,
):
    pairs = ((totals_in, totals), (shares_in, shares), (grad_in, grad_low), (layer_in, layer))
    loads = [pltpu.make_async_copy(src, dst, in_sem.at[n]) for n, (src, dst) in enumerate(pairs)]
    for load in loads:
        load.start()
    dp, tensor = lax.axis_index("dp"), lax.axis_index("tensor")
    stores = []

    def store(src, dst):
        stores.append(pltpu.make_async_copy(src, dst, out_sem.at[len(stores)]))
        stores[-1].start()

    loads[0].wait()
    rows = (s_0, s_1, s_2, s_3, s_4, s_5, s_6, s_7, s_8)
    outs = (o_0, o_1, o_2, o_3, o_4, o_5, o_6, o_7, o_8)
    for n, (kept, out, length, row) in enumerate(zip(rows, outs, VECTORS, VECTOR_ROWS)):
        at = (tensor * 64 + dp if n < 3 else dp) * length
        value = jnp.broadcast_to(totals[pl.ds(row + at // 128, 1), :], (8, 128))
        value = pltpu.roll(value, lax.rem(128 - lax.rem(at, 128), 128), 1)
        kept[...] = value[0:1, :length].reshape(length)
        store(kept, out)
    loads[1].wait()
    tile = 0
    for kept, out, count in zip((f_q, f_k, f_v, f_o, f_u, f_d), (g_q, g_k, g_v, g_o, g_u, g_d), WEIGHT_TILES):
        for k in range(count):
            kept[:, k * COLS : k * COLS + COLS] = shares[tile].astype(F32)
            tile += 1
        store(kept, out)
    loads[2].wait()
    for k in range(4):
        part = slice(k * 64, k * 64 + 64)
        grad[part] = grad_low[part].astype(F32)
        store(grad.at[part], input_grad.at[part])
    loads[3].wait()
    store(layer, layer_out)
    for copy in stores:
        copy.wait()


def finish_call(*arrays):
    half = (HALF, WIDTH)
    shares = [(16, count * COLS) for count in WEIGHT_TILES]
    vectors = [(length,) for length in VECTORS]
    outs = [(half, BF16)] + [(shape, F32) for shape in [half] + shares + vectors]
    scratch = [(half, BF16), (half, BF16), ((TILES, 16, COLS), BF16), ((VEC_ROWS, 128), F32)] + outs[1:]
    return pl.pallas_call(
        finish_kernel,
        out_shape=tuple(jax.ShapeDtypeStruct(*o) for o in outs),
        in_specs=[pl.BlockSpec(memory_space=pl.ANY)] * len(arrays),
        out_specs=(pl.BlockSpec(memory_space=pl.ANY),) * len(outs),
        scratch_shapes=[pltpu.VMEM(*o) for o in scratch]
        + [pltpu.SemaphoreType.DMA((4,)), pltpu.SemaphoreType.DMA((20,))],
    )(*arrays)


def on_device(
    tokens, segment, w_query, w_key, w_value, w_out, w_up, w_down, b_query, b_value, b_up,
    b_out, b_down, gain_one, shift_one, gain_two, shift_two, out_grad,
):
    made = layer_call(
        w_query, w_key, w_value, w_out, w_up, w_down, b_query, b_value, b_up,
        b_out, b_down, gain_one, shift_one, gain_two, shift_two, segment, tokens, out_grad,
    )
    return tuple(finish_call(*made))


def solution(mesh):
    placed = (
        P(("dp", "tensor"), None),
        P("dp"),
        P("dp", "tensor"),
        P("dp", "tensor"),
        P("dp", "tensor"),
        P("dp", "tensor"),
        P("dp", "tensor"),
        P("dp", "tensor"),
        P(("tensor", "dp")),
        P(("tensor", "dp")),
        P(("tensor", "dp")),
        P("dp"),
        P("dp"),
        P("dp"),
        P("dp"),
        P("dp"),
        P("dp"),
        P(("dp", "tensor"), None),
    )
    return jax.shard_map(
        on_device,
        mesh=mesh,
        in_specs=placed,
        out_specs=(
            P(("dp", "tensor"), None),
            P(("dp", "tensor"), None),
            P("dp", "tensor"),
            P("dp", "tensor"),
            P("dp", "tensor"),
            P("dp", "tensor"),
            P("dp", "tensor"),
            P("dp", "tensor"),
            P(("tensor", "dp")),
            P(("tensor", "dp")),
            P(("tensor", "dp")),
            P("dp"),
            P("dp"),
            P("dp"),
            P("dp"),
            P("dp"),
            P("dp"),
        ),
        check_vma=False,
    )
```

```python
import jax
import jax.numpy as jnp
from jax import lax
from jax.experimental import pallas as pl
from jax.experimental.pallas import tpu as pltpu
from jax.sharding import PartitionSpec as P

MESH = pl.DeviceIdType.MESH
F32 = jnp.float32
BF16 = jnp.bfloat16

TILES = 24
COLS = 256
PHASES, ROUTES, STEPS = 4, 3, 4
VEC_ROWS = 96
ORDERS = ((2, 0, 1), (1, 2, 0), (0, 1, 2))
PARTNERS = (1, 3, 2)


def position():
    dp, low = lax.axis_index("dp"), lax.axis_index("tensor")
    return (dp // 16, lax.rem(dp // 4, 4), lax.rem(dp // 2, 2) * 2 + low), lax.rem(dp, 2)


def device(chip, core):
    y, x, z = chip
    return (y * 16 + x * 4 + (z // 2) * 2 + core, lax.rem(z, 2))


def moved(chip, axis, by):
    return tuple(lax.rem(c + by, 4) if k == axis else c for k, c in enumerate(chip))


def opposite_z(chip):
    y, x, z = chip
    return (y, x, z + 1 - 2 * lax.rem(z, 2))


def blocks(chip, full):
    return tuple(pl.ds(0, 4) if axis in full else pl.ds(c, 1) for axis, c in enumerate(chip))


def block_shape(full):
    return tuple(4 if axis in full else 1 for axis in range(3))


def first_tile(phase, route):
    return phase * 6 + route * 2


class Ring:
    def __init__(self, buffer, sems):
        self.buffer, (self.send, self.recv) = buffer, sems
        self.chip, self.core = position()

    def copy(self, phase, step, target, src, dst):
        sem = phase * STEPS + step
        return pltpu.make_async_remote_copy(
            src_ref=src, dst_ref=dst, send_sem=self.send.at[sem], recv_sem=self.recv.at[sem],
            device_id=target, device_id_type=MESH,
        )

    def partner(self, axis, way):
        return device(moved(self.chip, axis, PARTNERS[way]), self.core)

    def start_route(self, phase, route, step):
        for c in self.copies(phase, route, step):
            c.start()

    def start(self, phase, step):
        for route in range(ROUTES):
            self.start_route(phase, route, step)

    def all_of(self, phase, step):
        tiles, ny, nx, nz = self.size(phase, step)
        whole = self.buffer.at[pl.ds(0, tiles), pl.ds(0, ny), pl.ds(0, nx), pl.ds(0, nz)]
        return self.copy(phase, step, self.partner(0, 0), whole, whole)

    def wait_recv(self, phase, step):
        self.all_of(phase, step).wait_recv()

    def wait_send(self, phase, step):
        self.all_of(phase, step).wait_send()


class Gather(Ring):
    def size(self, phase, step):
        return ((18, 1, 1, 1), (18, 1, 1, 4), (12, 1, 4, 4), (6, 1, 4, 4))[step]

    def copies(self, phase, route, step):
        order, k = ORDERS[route], min(step, 2)
        axis, full = order[k], order[:k]
        tile = first_tile(phase, route)
        out = []
        for way in range(3 if step < 2 else 2):
            if step < 3:
                part = self.buffer.at[(pl.ds(tile, 2),) + blocks(self.chip, full)]
            else:
                behind = moved(self.chip, axis, PARTNERS[1 - way])
                part = self.buffer.at[(pl.ds(tile + way, 1),) + blocks(behind, full)]
            out.append(self.copy(phase, step, self.partner(axis, way), part, part))
        return out

    def step(self, phase, step):
        if step:
            self.wait_recv(phase, step - 1)
        if step < STEPS:
            self.start(phase, step)


HALVES = (0, 4)


def scatter_tiles(phase, route):
    if phase in HALVES:
        return 2 * route + HALVES.index(phase), 1
    return first_tile(phase, route), 2


def scatter_steps(phase):
    return 3 if phase in HALVES else STEPS


def landing_shapes():
    shapes = []
    for phase in range(PHASES + 1):
        for order in ORDERS:
            for k in range(3):
                tiles = 3 if phase in HALVES else 6
                shapes.append((tiles,) + block_shape(order[: 2 - k]) + (16, COLS))
    return shapes


class Scatter(Ring):
    def __init__(self, g, landings, sems):
        super().__init__(g, sems)
        self.g, self.landings = g, landings

    def size(self, phase, step):
        if phase in HALVES:
            return ((9, 1, 4, 4), (9, 1, 1, 4), (9, 1, 1, 1))[step]
        return ((6, 1, 4, 4), (12, 1, 4, 4), (18, 1, 1, 4), (18, 1, 1, 1))[step]

    def at(self, phase, route, step):
        order, k = ORDERS[route], step if phase in HALVES else max(step - 1, 0)
        return order[2 - k], order[: 2 - k], self.landings[(phase * ROUTES + route) * 3 + k]

    def copies(self, phase, route, step):
        axis, full, landed = self.at(phase, route, step)
        tile, count = scatter_tiles(phase, route)
        out = []
        for way in range(2 if count == 2 and step < 2 else 3):
            if count == 2 and step == 0:
                src = self.g.at[(pl.ds(tile + way, 1),) + blocks(moved(self.chip, axis, 2), full)]
                dst = landed.at[pl.ds(way, 1)]
            else:
                ahead = moved(self.chip, axis, PARTNERS[way])
                src = self.g.at[(pl.ds(tile, count),) + blocks(ahead, full)]
                dst = landed.at[pl.ds(count * way + (2 if count == 2 and step == 1 else 0), count)]
            out.append(self.copy(phase, step, self.partner(axis, way), src, dst))
        return out

    def take(self, phase, route, step):
        axis, full, landed = self.at(phase, route, step)
        tile, count = scatter_tiles(phase, route)
        ny, nx, nz = block_shape(full)

        def start_of(chip):
            return tuple(0 if k in full else c for k, c in enumerate(chip))

        def add(t, base, parts):
            y0, x0, z0 = base

            def one(i, carry):
                at = (tile + t, y0 + i, pl.ds(x0, nx), pl.ds(z0, nz))
                total = self.g[at].astype(F32)
                for part in parts:
                    total += landed[part, i].astype(F32)
                self.g[at] = total.astype(BF16)
                return carry

            lax.fori_loop(0, ny, one, 0)

        for t in range(count):
            if count == 2 and step == 0:
                add(t, start_of(moved(self.chip, axis, PARTNERS[t])), (t,))
            elif count == 2 and step == 1:
                add(t, start_of(self.chip), (2 + t, 4 + t))
            else:
                add(t, start_of(self.chip), (t, count + t, 2 * count + t))

    def step(self, phase, step):
        if step:
            self.wait_recv(phase, step - 1)
            for route in range(ROUTES):
                self.take(phase, route, step - 1)
        if step < scatter_steps(phase):
            self.start(phase, step)


def greet(others):
    barrier = pltpu.get_barrier_semaphore()
    for other in others:
        pl.semaphore_signal(barrier, inc=1, device_id=other, device_id_type=MESH)
    pl.semaphore_wait(barrier, len(others))


def sibling():
    chip, core = position()
    return device(chip, 1 - core)


class VectorSum:
    def __init__(self, kept, came, sems, base):
        self.kept, self.came, (self.send, self.recv), self.base = kept, came, sems, base
        self.chip, self.core = position()

    def copy(self, stage, target, src, dst):
        return pltpu.make_async_remote_copy(
            src_ref=src,
            dst_ref=dst,
            send_sem=self.send.at[self.base + stage],
            recv_sem=self.recv.at[self.base + stage],
            device_id=target,
            device_id_type=MESH,
        )

    def targets(self, stage):
        if stage == 0:
            return [device(self.chip, 1 - self.core)]
        return [device(moved(self.chip, stage - 1, by), self.core) for by in PARTNERS]

    def all_of(self, stage):
        targets = self.targets(stage)
        whole = self.came.at[pl.ds(max(3 * stage - 2, 0), len(targets))]
        return self.copy(stage, targets[0], whole, whole)

    def step(self, stage):
        if stage:
            self.all_of(stage - 1).wait_recv()
            own = self.kept[stage - 1]
            if stage == 1:
                self.kept[1] = own + self.came[0]
            else:
                slot = 3 * stage - 5
                self.kept[stage] = (own + self.came[slot + 2]) + (self.came[slot] + self.came[slot + 1])
        if stage < 4:
            for n, target in enumerate(self.targets(stage)):
                there = self.came.at[max(3 * stage - 2, 0) + n]
                self.copy(stage, target, self.kept.at[stage], there).start()

    def wait_send(self, stage):
        self.all_of(stage).wait_send()


GROUP = 512
HALF = 256
WIDTH = 1024
HEAD_DIM = 64
PAIR = 2 * HEAD_DIM
SCALE = HEAD_DIM**-0.5
EPSILON = 1e-12
NN = (((1,), (0,)), ((), ()))
NT = (((1,), (1,)), ((), ()))
TN = (((0,), (0,)), ((), ()))
Q_TILE, OUT_TILE, UP_TILE, DOWN_TILE = 0, 6, 8, 16
WEIGHT_TILES = (2, 2, 2, 2, 8, 8)


def dot(a, b, dims=NN):
    return lax.dot_general(a, b, dims, preferred_element_type=F32)


def loop(count, body, together=2):
    def step(i, carry):
        for k in range(together):
            body(i * together + k)
        return carry

    lax.fori_loop(0, count // together, step, 0)


VECTORS = (8, 8, 32, 16, 16, 16, 16, 16, 16)
VECTOR_ROWS = (0, 8, 16, 48, 56, 64, 72, 80, 88)


def layer_kernel(
    w_q, w_k, w_v, w_o, w_u, w_d,
    v_0, v_1, v_2, v_3, v_4, v_5, v_6, v_7, v_8, segment, tokens, out_grad,
    layer_out, input_grad, shares, vec_out,
    w, g, x, n1, gd, tr, x_tr, qkv, probs, bias, ctx, gctx, ds, part, leave, come,
    hat, inv, d_two, cot, act, slope, seg_here, seg_own, segments, segcol, features, biases, bias_sums, sums, out_rows,
    r_0, r_1, r_2, r_3, r_4, r_5, r_6, r_7, r_8, placed,
    kept, came, kept_front, came_front, kept_tail, came_tail,
    gsend, grecv, ssend, srecv, vsend, vrecv, swap_send, swap_recv, sib_send, sib_recv, load_sem,
    *landings,
):
    chip, core = position()
    y, x_at, z = chip
    low = lax.rem(z, 2)
    opposite_chip = opposite_z(chip)
    diagonal = device(opposite_chip, 1 - core)
    twin = sibling()
    stays = core == low
    own_rows = pl.ds(pl.multiple_of(core * HALF, HALF), HALF)
    other_rows = pl.ds(pl.multiple_of((1 - core) * HALF, HALF), HALF)

    raw = (r_0, r_1, r_2, r_3, r_4, r_5, r_6, r_7, r_8)
    loads = [
        pltpu.make_async_copy(src, dst, load_sem.at[n])
        for n, (src, dst) in enumerate(zip((v_0, v_1, v_2, v_3, v_4, v_5, v_6, v_7, v_8), raw))
    ]
    loads.append(pltpu.make_async_copy(segment, seg_here.at[0], load_sem.at[9]))
    loads.append(pltpu.make_async_copy(out_grad, d_two, load_sem.at[10]))
    for load in loads:
        load.start()

    def swap_copies(n, src, dst_here, dst_there):
        away = pltpu.make_async_remote_copy(
            src_ref=src, dst_ref=dst_there, send_sem=swap_send.at[n], recv_sem=swap_recv.at[n],
            device_id=diagonal, device_id_type=MESH,
        )
        return away, pltpu.make_async_copy(src, dst_here, swap_recv.at[n])

    def swap_start(n, src, dst_here, dst_there):
        away, here = swap_copies(n, src, dst_here, dst_there)
        pl.when(stays)(here.start)
        pl.when(jnp.logical_not(stays))(away.start)

    def swap_wait(n, src, dst_here, dst_there):
        away, here = swap_copies(n, src, dst_here, dst_there)
        pl.when(stays)(here.wait)
        pl.when(jnp.logical_not(stays))(away.wait)

    def to_twin(n, src, dst):
        return pltpu.make_async_remote_copy(
            src_ref=src, dst_ref=dst, send_sem=sib_send.at[n], recv_sem=sib_recv.at[n],
            device_id=twin, device_id_type=MESH,
        )

    greet([device(moved(chip, axis, by), core) for axis in range(3) for by in PARTNERS] + [twin, diagonal])

    weight_moves = []
    tile = 0
    for ref, count in zip((w_q, w_k, w_v, w_o, w_u, w_d), WEIGHT_TILES):
        for k in range(count):
            weight_moves.append(
                (
                    tile // 6,
                    ref.at[:, pl.ds(k * COLS, COLS)],
                    w.at[tile, y, x_at, z],
                    w.at[(tile,) + opposite_chip],
                )
            )
            tile += 1
    for move in weight_moves:
        swap_start(*move)

    gather = Gather(w, (gsend, grecv))
    vectors = VectorSum(kept, came, (vsend, vrecv), 0)

    def arrived(phase):
        group = w.at[pl.ds(6 * phase, 6), y, x_at, z]
        swap_wait(phase, group, group, group)

    for load in loads[:-1]:
        load.wait()
    dp, tensor = lax.axis_index("dp"), lax.axis_index("tensor")
    placed[...] = jnp.zeros((VEC_ROWS, 128), F32)
    for n, (ref, length, row) in enumerate(zip(raw, VECTORS, VECTOR_ROWS)):
        at = (tensor * 64 + dp if n < 3 else dp) * length
        value = ref[...].astype(F32).reshape(1, length)
        value = jnp.concatenate([value, jnp.zeros((1, 128 - length), F32)], axis=1)
        value = pltpu.roll(jnp.broadcast_to(value, (8, 128)), lax.rem(at, 128), 1)
        if n >= 3:
            value = jnp.where(tensor == 0, value, 0.0)
        placed[pl.ds(row + at // 128, 1), :] = value[0:1]
    kept[0] = placed[...].astype(BF16)
    vectors.step(0)
    seg_own[...] = jnp.broadcast_to(seg_here[...].astype(F32), (8, GROUP))
    seg_move = (5, seg_own, segments, segments)
    swap_start(*seg_move)
    arrived(0)
    gather.step(0, 0)
    row_move = (4, tokens, x.at[own_rows], x.at[other_rows])
    swap_start(*row_move)
    vectors.step(1)
    for phase in (1, 2, 3):
        arrived(phase)
        gather.step(phase, 0)
    gather.step(0, 1)
    vectors.step(2)
    gather.step(1, 1)
    gather.step(0, 2)
    vectors.step(3)
    gather.step(2, 1)

    swap_wait(*seg_move)
    across_lanes = jnp.broadcast_to(segments[0:1, :], (128, GROUP))
    segcol[...] = across_lanes.T
    for k in range(4):
        cols = slice(k * 128, k * 128 + 128)
        bias[:, cols] = jnp.where(segcol[...] == segments[0:1, cols], 0.0, -1000000000.0).astype(BF16)
    swap_wait(*row_move)
    rows_copy = to_twin(0, x.at[own_rows], x.at[own_rows])
    rows_copy.start()
    gather.step(0, 3)
    gather.step(3, 1)
    gather.step(1, 2)
    vectors.step(4)
    gather.step(2, 2)
    loads[-1].wait()
    out_rows[...] = d_two[...].astype(BF16)
    placed[...] = kept[4].astype(F32)
    for n in range(6):
        for k in range(8):
            features[n, :, k * 128 : k * 128 + 128] = placed[48 + n * 8 + k : 49 + n * 8 + k, :]
    for k in range(2):
        for half in range(2):
            lanes = slice(half * 128, half * 128 + 128)
            biases[k, :, lanes] = placed[pl.ds(core * 4 + k * 2 + half, 1), :]
            biases[4 + k, :, lanes] = placed[pl.ds(8 + core * 4 + k * 2 + half, 1), :]
        biases[2 + k] = jnp.zeros((1, COLS), F32)
    for k in range(8):
        for half in range(2):
            lanes = slice(half * 128, half * 128 + 128)
            biases[6 + k, :, lanes] = placed[pl.ds(16 + core * 16 + k * 2 + half, 1), :]
    rows_copy.wait_recv()

    def turn(ref, out=tr):
        for k in range(4):
            rows = slice(k * COLS, k * COLS + COLS)
            out[rows, :] = ref[:, rows].T

    def turn_half(ref, half):
        lanes = pl.ds(pl.multiple_of(half * HALF, HALF), HALF)
        for k in range(4):
            rows = slice(k * COLS, k * COLS + COLS)
            tr[rows, lanes] = ref[lanes, rows].T

    turn(x, x_tr)
    gather.step(0, 4)

    def weight(tile):
        return w[tile].reshape(WIDTH, COLS)

    def project(t):
        made = (dot(x[...], weight(t)) + biases[t]).astype(BF16)
        qkv[2 * t] = made[:, :128]
        qkv[2 * t + 1] = made[:, 128:]

    loop(6, project)
    low_lanes = lax.broadcasted_iota(jnp.int32, (1, PAIR), 1) < HEAD_DIM

    def only(head, values):
        keep = low_lanes if head == 0 else jnp.logical_not(low_lanes)
        return jnp.where(keep, values, jnp.zeros_like(values))

    def attend(pair):
        for half in range(2):
            rows = slice(half * HALF, half * HALF + HALF)
            query = qkv[pair, rows]
            outs = []
            for head in range(2):
                scores = dot(qkv[4 + pair], only(head, query), NT) * SCALE + bias[:, rows].astype(F32)
                scores = jnp.exp(scores - jnp.max(scores, axis=0, keepdims=True))
                weights = scores * (1.0 / jnp.sum(scores, axis=0, keepdims=True))
                weights = weights.astype(BF16)
                probs[2 * pair + head, :, rows] = weights
                outs.append(dot(weights, qkv[8 + pair], TN))
            ctx[pair, rows] = jnp.where(low_lanes, outs[0], outs[1]).astype(BF16)

    attend(0)
    attend(1)
    gather.step(1, 3)
    gather.step(3, 2)
    attend(2)
    attend(3)
    gather.step(2, 3)
    gather.step(1, 4)

    terms_sent = []

    def row_terms(n, tiles, left):
        def block(rows, store):
            def one(k):
                lanes = pl.ds(pl.multiple_of(k * COLS, COLS), COLS)
                total = None
                for t, at in enumerate(tiles):
                    term = dot(left(t, rows), w[at, k].reshape(COLS, COLS), NT)
                    total = term if total is None else total + term
                store(lanes, total)

            loop(4, one)

        if n:
            terms_sent[-1].wait_send()

        def leaves(lanes, total):
            leave[:, lanes] = total.astype(BF16)

        def stays_here(lanes, total):
            part[:, lanes] = total

        block(other_rows, leaves)
        copy = to_twin(1 + n, leave, come)
        copy.start()
        block(own_rows, stays_here)
        copy.wait_recv()
        terms_sent.append(copy)

    def side_by_side(ref, first, rows=slice(None)):
        return jnp.concatenate([ref[first, rows], ref[first + 1, rows]], axis=1)

    sent = [rows_copy]
    row_terms(0, range(OUT_TILE, UP_TILE), lambda t, rows: side_by_side(ctx, 2 * t, rows))
    chunk = 128

    def by_chunks(body):
        def one(i):
            at = pl.multiple_of(i * chunk, chunk)
            body(pl.ds(at, chunk), pl.ds(pl.multiple_of(core * HALF + at, chunk), chunk))

        loop(HALF // chunk, one, 1)

    def mean(values):
        return jnp.mean(values, axis=-1, keepdims=True)

    def normalized(hidden):
        centered = hidden - mean(hidden)
        scale = lax.rsqrt(mean(centered * centered) + EPSILON)
        return centered * scale, scale

    for n in range(6):
        sums[n] = jnp.zeros((1, WIDTH), F32)

    def add_sum(n, values):
        sums[n] += jnp.sum(values, axis=0, keepdims=True)

    b_out, b_down, gain_one, shift_one, gain_two, shift_two = range(6)

    def first_norm(here, there):
        hidden = x[there].astype(F32) + part[here] + come[here].astype(F32) + features[b_out]
        value, scale = normalized(hidden)
        hat[here] = value
        inv[here] = jnp.broadcast_to(scale, (chunk, 128))
        n1[there] = (value * features[gain_one] + features[shift_one]).astype(BF16)

    by_chunks(first_norm)
    gather.step(3, 3)
    cot_move = (6, out_rows, cot, cot)
    swap_start(*cot_move)

    shared = {}

    def share_rows(n, ref, meanwhile=None):
        copy = to_twin(n, ref.at[own_rows], ref.at[own_rows])
        copy.start()
        shared[n] = copy
        if meanwhile:
            meanwhile()
        copy.wait_recv()

    share_rows(5, n1)

    def up(t):
        for half in range(2):
            rows = slice(half * HALF, half * HALF + HALF)
            pre = dot(n1[rows], weight(UP_TILE + t)) + biases[6 + t]
            below = 0.5 * (1.0 + lax.erf(pre * (0.5**0.5)))
            act[t, rows] = (pre * below).astype(BF16)
            bell = jnp.exp(pre * pre * -0.5) * 0.3989422804014327
            slope[t, rows] = (below + pre * bell).astype(BF16)

    loop(4, up)
    gather.step(2, 4)
    loop(4, lambda t: up(t + 4))
    gather.step(3, 4)
    row_terms(1, range(DOWN_TILE, TILES), lambda t, rows: act[t, rows])
    swap_wait(*cot_move)

    def norm_back(values, incoming, gain, scale, gain_at, shift_at):
        add_sum(shift_at, incoming)
        add_sum(gain_at, incoming * values)
        scaled = incoming * gain
        return scale * (scaled - mean(scaled) - values * mean(scaled * values))

    def second_norm(here, there):
        first = hat[here] * features[gain_one] + features[shift_one]
        value, scale = normalized(first + part[here] + come[here].astype(F32) + features[b_down])
        live = jnp.where(segcol[there, 0:1] >= 0, 1.0, 0.0)
        out_rows[here] = ((value * features[gain_two] + features[shift_two]) * live).astype(BF16)
        back = norm_back(
            value, cot[here].astype(F32) * live, features[gain_two], scale, gain_two, shift_two
        )
        add_sum(b_down, back)
        d_two[here] = back
        gd[there] = back.astype(BF16)

    by_chunks(second_norm)
    out_move = (7, out_rows, layer_out, layer_out)
    swap_start(*out_move)
    share_rows(6, gd, lambda: turn_half(gd, core))
    turn_half(gd, 1 - core)

    def store_grad(tile, right, left=tr):
        for k in range(4):
            made = dot(left[k * COLS : k * COLS + COLS, :], right)
            g[tile, k] = made.astype(BF16).reshape(4, 4, 16, COLS)

    scatter = Scatter(g, landings, (ssend, srecv))
    share_moves = []

    def reduced(phase):
        scatter.step(phase, scatter_steps(phase))
        n = 9 + phase
        if phase in HALVES:
            moves = [scatter_tiles(phase, route)[0] for route in range(ROUTES)]
            whole = pl.ds(0, ROUTES)
        else:
            moves = [pl.ds(6 * phase, 6)]
            whole = moves[0]
        for tiles in moves:
            swap_start(n, g.at[tiles, y, x_at, z], shares.at[tiles], shares.at[tiles])
        share_moves.append((n, g.at[whole, y, x_at, z], shares.at[whole], shares.at[whole]))

    for route in range(ROUTES):
        for t in (2 + 2 * route, 3 + 2 * route):
            store_grad(DOWN_TILE + t, act[t])
        scatter.start_route(3, route, 0)
    for t in range(2):
        store_grad(DOWN_TILE + t, act[t])

    def up_back(t):
        made = (dot(gd[...], weight(DOWN_TILE + t)) * slope[t].astype(F32)).astype(BF16)
        slope[t] = made
        bias_sums[6 + t] = jnp.sum(made.astype(F32), axis=0, keepdims=True)

    loop(8, up_back)
    scatter.step(3, 1)
    turn(n1)
    loop(4, lambda t: store_grad(UP_TILE + 4 + t, slope[4 + t]))
    scatter.step(2, 0)
    loop(4, lambda t: store_grad(UP_TILE + t, slope[t]))
    row_terms(2, range(UP_TILE, DOWN_TILE), lambda t, rows: slope[t, rows])

    def first_norm_back(here, there):
        incoming = d_two[here] + part[here] + come[here].astype(F32)
        back = norm_back(
            hat[here], incoming, features[gain_one], inv[here, 0:1], gain_one, shift_one
        )
        add_sum(b_out, back)
        d_two[here] = back
        n1[there] = back.astype(BF16)

    shared.pop(5).wait_send()
    d1 = n1
    scatter.step(3, 2)
    by_chunks(first_norm_back)
    def meanwhile():
        turn_half(d1, core)
        scatter.step(2, 1)

    share_rows(7, d1, meanwhile)
    turn_half(d1, 1 - core)
    loop(2, lambda u: store_grad(OUT_TILE + u, side_by_side(ctx, 2 * u)))
    scatter.step(1, 0)
    scatter.step(3, 3)

    kept_front[0] = jnp.zeros((VEC_ROWS - 16, 128), F32)
    for k in range(8):
        for half in range(2):
            lanes = slice(half * 128, half * 128 + 128)
            kept_front[0, pl.ds(core * 16 + k * 2 + half, 1), :] = bias_sums[6 + k, :, lanes]
    for n in range(6):
        for k in range(8):
            at = 32 + n * 8 + k
            kept_front[0, at : at + 1, :] = sums[n, :, k * 128 : k * 128 + 128]
    front = VectorSum(kept_front, came_front, (vsend, vrecv), 4)
    front.step(0)

    def context_back(u):
        made = dot(d1[...], weight(OUT_TILE + u)).astype(BF16)
        gctx[2 * u] = made[:, :128]
        gctx[2 * u + 1] = made[:, 128:]

    loop(2, context_back)

    def attend_back(pair):
        for half in range(2):
            rows = slice(half * HALF, half * HALF + HALF)
            for head in range(2):
                weights = probs[2 * pair + head, :, rows].astype(F32)
                grad = dot(qkv[8 + pair], only(head, gctx[pair, rows]), NT)
                total = jnp.sum(grad * weights, axis=0, keepdims=True)
                ds[head, :, rows] = (weights * (grad - total)).astype(BF16)
        query = [dot(ds[head], qkv[4 + pair], TN) for head in range(2)]
        key = [dot(ds[head], qkv[pair]) for head in range(2)]
        value = [dot(probs[2 * pair + head], gctx[pair]) for head in range(2)]
        for at, (a, b), scale in ((0, query, SCALE), (4, key, SCALE), (8, value, 1.0)):
            made = (jnp.where(low_lanes, a, b) * scale).astype(BF16)
            qkv[at + pair] = made
            bias_sums[14 + at + pair, :, :PAIR] = jnp.sum(made.astype(F32), axis=0, keepdims=True)

    def store_qkv_grads(half):
        loop(3, lambda t: store_grad(2 * t + half, side_by_side(qkv, 4 * t + 2 * half), x_tr), 1)

    attend_back(0)
    scatter.step(2, 2)
    front.step(1)
    attend_back(1)
    scatter.step(1, 1)
    store_qkv_grads(0)
    scatter.step(0, 0)
    reduced(3)
    front.step(2)
    attend_back(2)
    scatter.step(2, 3)
    front.step(3)
    attend_back(3)
    scatter.step(1, 2)
    front.step(4)
    reduced(2)
    kept_tail[0] = jnp.zeros((16, 128), F32)
    for k in range(4):
        kept_tail[0, pl.ds(core * 4 + k, 1), :] = bias_sums[14 + k, :, :PAIR]
        kept_tail[0, pl.ds(8 + core * 4 + k, 1), :] = bias_sums[22 + k, :, :PAIR]
    tail = VectorSum(kept_tail, came_tail, (vsend, vrecv), 8)
    tail.step(0)
    store_qkv_grads(1)
    scatter.step(4, 0)
    scatter.step(0, 1)
    tail.step(1)
    scatter.step(1, 3)
    row_terms(3, range(6), lambda t, rows: side_by_side(qkv, 2 * t, rows))
    scatter.step(0, 2)
    tail.step(2)
    scatter.step(4, 1)

    def last_rows(here, there):
        cot[here] = (d_two[here] + part[here] + come[here].astype(F32)).astype(BF16)

    by_chunks(last_rows)
    grad_move = (8, cot, input_grad, input_grad)
    reduced(1)
    reduced(0)
    tail.step(3)
    scatter.step(4, 2)
    swap_start(*grad_move)
    tail.step(4)
    reduced(4)
    vec_out[0:16] = kept_tail[4]
    vec_out[16:] = kept_front[4]

    for move in [out_move, grad_move] + share_moves:
        swap_wait(*move)
    for copy in sent + terms_sent[-1:] + list(shared.values()):
        copy.wait_send()
    for phase in range(PHASES):
        for step in range(STEPS):
            gather.wait_send(phase, step)
    for phase in range(PHASES + 1):
        for step in range(scatter_steps(phase)):
            scatter.wait_send(phase, step)
    for stage in range(4):
        vectors.wait_send(stage)
        front.wait_send(stage)
        tail.wait_send(stage)


def layer_call(*arrays):
    full = (TILES, 4, 4, 4, 16, COLS)
    rows = (GROUP, WIDTH)
    half = (HALF, WIDTH)
    front = VEC_ROWS - 16
    scratch = [
        (full, BF16), (full, BF16),
        (rows, BF16), (rows, BF16), (rows, BF16), ((WIDTH, GROUP), BF16), ((WIDTH, GROUP), BF16),
        ((12, GROUP, PAIR), BF16), ((8, GROUP, GROUP), BF16), ((GROUP, GROUP), BF16),
        ((4, GROUP, PAIR), BF16), ((4, GROUP, PAIR), BF16), ((2, GROUP, GROUP), BF16),
        (half, F32), (half, BF16), (half, BF16),
        (half, F32), ((HALF, 128), F32), (half, F32), (half, BF16),
        ((8, GROUP, COLS), BF16), ((8, GROUP, COLS), BF16),
        ((1, GROUP), jnp.int32), ((8, GROUP), F32), ((8, GROUP), F32), ((GROUP, 128), F32),
        ((6, 1, WIDTH), F32), ((14, 1, COLS), F32), ((26, 1, COLS), F32), ((6, 1, WIDTH), F32),
        (half, BF16),
    ] + [((length,), BF16) for length in VECTORS] + [
        ((VEC_ROWS, 128), F32),
        ((5, VEC_ROWS, 128), BF16), ((10, VEC_ROWS, 128), BF16),
        ((5, front, 128), F32), ((10, front, 128), F32),
        ((5, 16, 128), F32), ((10, 16, 128), F32),
    ]
    sems = [PHASES * STEPS] * 2 + [(PHASES + 1) * STEPS] * 2 + [12] * 2 + [14] * 2 + [8] * 2 + [11]
    return pl.pallas_call(
        layer_kernel,
        out_shape=(
            jax.ShapeDtypeStruct(half, BF16),
            jax.ShapeDtypeStruct(half, BF16),
            jax.ShapeDtypeStruct((TILES, 16, COLS), BF16),
            jax.ShapeDtypeStruct((VEC_ROWS, 128), F32),
        ),
        in_specs=[pl.BlockSpec(memory_space=pl.ANY)] * len(arrays),
        out_specs=(pl.BlockSpec(memory_space=pl.ANY),) * 3 + (pl.BlockSpec(memory_space=pltpu.VMEM),),
        scratch_shapes=[pltpu.VMEM(*s) for s in scratch]
        + [pltpu.SemaphoreType.DMA((n,)) for n in sems]
        + [pltpu.VMEM(s, BF16) for s in landing_shapes()],
        compiler_params=pltpu.CompilerParams(
            collective_id=0, has_side_effects=True, vmem_limit_bytes=64 * 2**20
        ),
    )(*arrays)


def finish_kernel(
    layer_in, grad_in, shares_in, totals_in,
    layer_out, input_grad, g_q, g_k, g_v, g_o, g_u, g_d, o_0, o_1, o_2, o_3, o_4, o_5, o_6, o_7, o_8,
    layer, grad_low, shares, totals, grad, f_q, f_k, f_v, f_o, f_u, f_d, s_0, s_1, s_2, s_3, s_4, s_5, s_6, s_7, s_8,
    in_sem, out_sem,
):
    pairs = ((totals_in, totals), (shares_in, shares), (grad_in, grad_low), (layer_in, layer))
    loads = [pltpu.make_async_copy(src, dst, in_sem.at[n]) for n, (src, dst) in enumerate(pairs)]
    for load in loads:
        load.start()
    dp, tensor = lax.axis_index("dp"), lax.axis_index("tensor")
    stores = []

    def store(src, dst):
        stores.append(pltpu.make_async_copy(src, dst, out_sem.at[len(stores)]))
        stores[-1].start()

    loads[0].wait()
    rows = (s_0, s_1, s_2, s_3, s_4, s_5, s_6, s_7, s_8)
    outs = (o_0, o_1, o_2, o_3, o_4, o_5, o_6, o_7, o_8)
    for n, (kept, out, length, row) in enumerate(zip(rows, outs, VECTORS, VECTOR_ROWS)):
        at = (tensor * 64 + dp if n < 3 else dp) * length
        value = jnp.broadcast_to(totals[pl.ds(row + at // 128, 1), :], (8, 128))
        value = pltpu.roll(value, lax.rem(128 - lax.rem(at, 128), 128), 1)
        kept[...] = value[0:1, :length].reshape(length)
        store(kept, out)
    loads[1].wait()
    tile = 0
    for kept, out, count in zip((f_q, f_k, f_v, f_o, f_u, f_d), (g_q, g_k, g_v, g_o, g_u, g_d), WEIGHT_TILES):
        for k in range(count):
            kept[:, k * COLS : k * COLS + COLS] = shares[tile].astype(F32)
            tile += 1
        store(kept, out)
    loads[2].wait()
    for k in range(4):
        part = slice(k * 64, k * 64 + 64)
        grad[part] = grad_low[part].astype(F32)
        store(grad.at[part], input_grad.at[part])
    loads[3].wait()
    store(layer, layer_out)
    for copy in stores:
        copy.wait()


def finish_call(*arrays):
    half = (HALF, WIDTH)
    shares = [(16, count * COLS) for count in WEIGHT_TILES]
    vectors = [(length,) for length in VECTORS]
    outs = [(half, BF16)] + [(shape, F32) for shape in [half] + shares + vectors]
    scratch = [(half, BF16), (half, BF16), ((TILES, 16, COLS), BF16), ((VEC_ROWS, 128), F32)] + outs[1:]
    return pl.pallas_call(
        finish_kernel,
        out_shape=tuple(jax.ShapeDtypeStruct(*o) for o in outs),
        in_specs=[pl.BlockSpec(memory_space=pl.ANY)] * len(arrays),
        out_specs=(pl.BlockSpec(memory_space=pl.ANY),) * len(outs),
        scratch_shapes=[pltpu.VMEM(*o) for o in scratch]
        + [pltpu.SemaphoreType.DMA((4,)), pltpu.SemaphoreType.DMA((20,))],
    )(*arrays)


def on_device(
    tokens, segment, w_query, w_key, w_value, w_out, w_up, w_down, b_query, b_value, b_up,
    b_out, b_down, gain_one, shift_one, gain_two, shift_two, out_grad,
):
    made = layer_call(
        w_query, w_key, w_value, w_out, w_up, w_down, b_query, b_value, b_up,
        b_out, b_down, gain_one, shift_one, gain_two, shift_two, segment, tokens, out_grad,
    )
    return tuple(finish_call(*made))


def solution(mesh):
    placed = (
        P(("dp", "tensor"), None),
        P("dp"),
        P("dp", "tensor"),
        P("dp", "tensor"),
        P("dp", "tensor"),
        P("dp", "tensor"),
        P("dp", "tensor"),
        P("dp", "tensor"),
        P(("tensor", "dp")),
        P(("tensor", "dp")),
        P(("tensor", "dp")),
        P("dp"),
        P("dp"),
        P("dp"),
        P("dp"),
        P("dp"),
        P("dp"),
        P(("dp", "tensor"), None),
    )
    return jax.shard_map(
        on_device,
        mesh=mesh,
        in_specs=placed,
        out_specs=(
            P(("dp", "tensor"), None),
            P(("dp", "tensor"), None),
            P("dp", "tensor"),
            P("dp", "tensor"),
            P("dp", "tensor"),
            P("dp", "tensor"),
            P("dp", "tensor"),
            P("dp", "tensor"),
            P(("tensor", "dp")),
            P(("tensor", "dp")),
            P(("tensor", "dp")),
            P("dp"),
            P("dp"),
            P("dp"),
            P("dp"),
            P("dp"),
            P("dp"),
        ),
        check_vma=False,
    )
```
